32 devices in a mesh: leaf: 4 (over x, core), fsdp: 8 (over z, y).
Axes of the slice: x: 2, y: 2, z: 4, core: 2. Of those that a mesh axis runs over, the one named last changes fastest.
Arguments:
- layer_entry_matrix: bfloat16 [2, 8, 2048, 768], P(None, 'fsdp', 'leaf'), may hold values from -6 to 6
- loss_sensitivity: bfloat16 [2, 8, 2048, 768], P(None, 'fsdp', 'leaf'), may hold values from -6 to 6
- ancestor_block_table: int32 [2, 8, 16], P(None, 'fsdp'), may hold values from 0 to 15, as said below
- gate_trained_scores: float32 [12, 512, 512], P(None, 'fsdp'), may hold values from -6 to 6
- gate_random_jitter: float32 [12, 512, 512], P(None, 'fsdp'), may hold values from -6 to 6
- softening_scale: float32 [12], replicated, may hold values from 0.5 to 2
- triple_projection_matrix: bfloat16 [768, 2304], P('fsdp'), may hold values from -0.21875 to 0.21875
- asker_constant_vector: bfloat16 [768], P('fsdp'), may hold values from -3 to 3
- content_constant_vector: bfloat16 [768], P('fsdp'), may hold values from -3 to 3
- mixer_exit_matrix: bfloat16 [768, 768], P('fsdp'), may hold values from -9.75 to 9.75
- mixer_exit_constant: bfloat16 [768], P('fsdp'), may hold values from -3 to 3
- mixer_scaling_factor: bfloat16 [768], P('fsdp'), may hold values from 0.5 to 1.5
- mixer_recentering_term: bfloat16 [768], P('fsdp'), may hold values from -3 to 3
- dense_expand_matrix: bfloat16 [768, 3072], P('fsdp'), may hold values from -0.21875 to 0.21875
- dense_expand_constant: bfloat16 [3072], P('fsdp'), may hold values from -3 to 3
- dense_contract_matrix: bfloat16 [3072, 768], P('fsdp'), may hold values from -0.109375 to 0.109375
- dense_contract_constant: bfloat16 [768], P('fsdp'), may hold values from -3 to 3
- dense_scaling_factor: bfloat16 [768], P('fsdp'), may hold values from 0.5 to 1.5
- dense_recentering_term: bfloat16 [768], P('fsdp'), may hold values from -3 to 3
Outputs:
- layer_out: bfloat16 [2, 8, 2048, 768], P(None, 'fsdp', 'leaf')
- tokens_grad: bfloat16 [2, 8, 2048, 768], P(None, 'fsdp', 'leaf')
- qkv_weight_grad: float32 [768, 2304], P('fsdp')
- query_bias_grad: float32 [768], P('fsdp')
- value_bias_grad: float32 [768], P('fsdp')
- out_weight_grad: float32 [768, 768], P('fsdp')
- out_bias_grad: float32 [768], P('fsdp')
- first_gain_grad: float32 [768], P('fsdp')
- first_shift_grad: float32 [768], P('fsdp')
- up_weight_grad: float32 [768, 3072], P('fsdp')
- up_bias_grad: float32 [3072], P('fsdp')
- down_weight_grad: float32 [3072, 768], P('fsdp')
- down_bias_grad: float32 [768], P('fsdp')
- second_gain_grad: float32 [768], P('fsdp')
- second_shift_grad: float32 [768], P('fsdp')
- mask_logits_grad: float32 [12, 512, 512], P(None, 'fsdp')
The draws below stay inside these ranges and needn't reach their ends.
Inputs may be any that keep to these rules, and one draw needn't show every extreme that they name: `ancestor_block_table`: in every tree, 4 trunk blocks form a chain whose first block is its own parent, 4 branch blocks have the last trunk block as parent, and 2 leaf blocks have each branch block as parent; the blocks stand in any order.
All inputs are finite; a program needn't handle non-finite values.
Results may differ from the reference program's by a relative error of at most 0.018.
Values may be sent and summed in bfloat16 or wider, within the bound.
A program may use at most 256 MiB of HBM per device.

```python
import math
import jax
import jax.numpy as jnp
from jax import lax

D = 768
FOCUS_COUNT = 12
FF = 3072
MASK_LEN = 512
BLK = 128
TRUNK_BLK = 4
BRANCHES = 4
LEAVES = 2
MB = 2
NB = 16
TT = 2048
TREES = 8


def single_tree(key):
    logical = jnp.arange(NB, dtype=jnp.int32)
    parent_logical = jnp.where(logical < TRUNK_BLK, jnp.maximum(logical - 1, 0), jnp.where(logical < TRUNK_BLK + BRANCHES, TRUNK_BLK - 1, TRUNK_BLK + (logical - TRUNK_BLK - BRANCHES) // LEAVES)).astype(jnp.int32)
    order = jax.random.permutation(key, NB).astype(jnp.int32)
    return jnp.zeros((NB,), jnp.int32).at[order].set(order[parent_logical])


def draw_ancestor_block_table(key, part):
    keys = jax.random.split(jax.random.fold_in(key, 17), MB * TREES)
    return jax.vmap(single_tree)(keys).reshape(MB, TREES, NB)


def steps_of(stream_key, shape, cuts, smallest, top_value):
    loudness = 1.0
    for dim, shards_of in cuts:
        steps = jax.random.uniform(jax.random.fold_in(jax.random.fold_in(stream_key, 6), dim), (shards_of,), jnp.float32, smallest / len(cuts), top_value / len(cuts))
        loudness = loudness * jnp.repeat(jnp.exp(steps), shape[dim] // shards_of).reshape((-1,) + (1,) * (len(shape) - 1 - dim))
    return loudness


def normal_values(stream_key, extent, deviation, most, shards=(), kind=jnp.bfloat16):
    values = deviation * jax.random.normal(stream_key, extent, jnp.float32)
    if shards:
        values = values * steps_of(stream_key, extent, shards, -0.22, 0.18)
    return jnp.clip(values, -most, most).astype(kind)


def setup_inputs(seed: int = 0) -> dict:
    streams_of = jax.random.split(jax.random.key(seed), 20)
    layer_entry_matrix = normal_values(streams_of[0], (MB, TREES, TT, D), 1.0, 6.0, ((1, 8), (2, 4)))
    loss_sensitivity = normal_values(streams_of[1], (MB, TREES, TT, D), 1.0, 6.0, ((1, 8), (2, 4)))
    ancestor_block_table = draw_ancestor_block_table(jax.random.fold_in(streams_of[19], 71), 0)
    gate_trained_scores = normal_values(streams_of[3], (FOCUS_COUNT, MASK_LEN, MASK_LEN), 1.0, 6.0, ((1, 8),), jnp.float32)
    gate_random_jitter = normal_values(streams_of[4], (FOCUS_COUNT, MASK_LEN, MASK_LEN), 1.0, 6.0, ((1, 8),), jnp.float32)
    softening_scale = jnp.clip(jnp.exp(jax.random.uniform(streams_of[5], (FOCUS_COUNT,), jnp.float32, math.log(0.5), math.log(2.0))), 0.5, 2.0)
    triple_projection_matrix = normal_values(streams_of[6], (D, 3 * D), D ** -0.5, 0.21875, ((0, 8),))
    asker_constant_vector = normal_values(streams_of[7], (D,), 0.5, 3.0, ((0, 8),))
    content_constant_vector = normal_values(streams_of[8], (D,), 0.5, 3.0, ((0, 8),))
    mixer_exit_matrix = normal_values(streams_of[9], (D, D), ((NB * BLK) ** 0.5 / D ** 0.5), 9.75, ((0, 8),))
    mixer_exit_constant = normal_values(streams_of[10], (D,), 0.5, 3.0, ((0, 8),))
    mixer_scaling_factor = jnp.clip(1.0 + 0.1 * jax.random.normal(streams_of[11], (D,), jnp.float32), 0.5, 1.5).astype(jnp.bfloat16)
    mixer_recentering_term = normal_values(streams_of[12], (D,), 0.5, 3.0, ((0, 8),))
    dense_expand_matrix = normal_values(streams_of[13], (D, FF), D ** -0.5, 0.21875, ((0, 8),))
    dense_expand_constant = normal_values(streams_of[14], (FF,), 0.5, 3.0, ((0, 8),))
    dense_contract_matrix = normal_values(streams_of[15], (FF, D), FF ** -0.5, 0.109375, ((0, 8),))
    dense_contract_constant = normal_values(streams_of[16], (D,), 0.5, 3.0, ((0, 8),))
    dense_scaling_factor = jnp.clip(1.0 + 0.1 * jax.random.normal(streams_of[17], (D,), jnp.float32), 0.5, 1.5).astype(jnp.bfloat16)
    dense_recentering_term = normal_values(streams_of[18], (D,), 0.5, 3.0, ((0, 8),))
    return dict(layer_entry_matrix=layer_entry_matrix, loss_sensitivity=loss_sensitivity, ancestor_block_table=ancestor_block_table, gate_trained_scores=gate_trained_scores, gate_random_jitter=gate_random_jitter, softening_scale=softening_scale, triple_projection_matrix=triple_projection_matrix, asker_constant_vector=asker_constant_vector, content_constant_vector=content_constant_vector, mixer_exit_matrix=mixer_exit_matrix, mixer_exit_constant=mixer_exit_constant, mixer_scaling_factor=mixer_scaling_factor, mixer_recentering_term=mixer_recentering_term, dense_expand_matrix=dense_expand_matrix, dense_expand_constant=dense_expand_constant, dense_contract_matrix=dense_contract_matrix, dense_contract_constant=dense_contract_constant, dense_scaling_factor=dense_scaling_factor, dense_recentering_term=dense_recentering_term)


EPSILON = 1e-05
MASKED = -1e+30
HIGHEST = lax.Precision.HIGHEST

@jax.custom_vjp
def reduced_accuracy(v):
    return lax.optimization_barrier(v.astype(jnp.bfloat16)).astype(jnp.float32)

@jax.custom_vjp
def low_back(v):
    return v

def low_keep(v):
    return (reduced_accuracy(v), None)

def low_pass(kept, grad):
    return (grad,)

def back_keep(v):
    return (v, None)

def back_low(kept, grad):
    return (reduced_accuracy(grad),)
reduced_accuracy.defvjp(low_keep, low_pass)
low_back.defvjp(back_keep, back_low)

def product(left, right):
    return jnp.dot(left, right, precision=HIGHEST, preferred_element_type=jnp.float32)

def tree_tables(block_parent):
    blocks = block_parent.shape[0]
    indices = jnp.arange(blocks, dtype=jnp.int32)
    itself = (indices[:, None] == indices[None, :]).astype(jnp.int32)
    upward = (block_parent[:, None] == indices[None, :]).astype(jnp.int32)
    reachable = jnp.maximum(itself, upward)
    for rounds in range(blocks.bit_length()):
        reachable = jnp.minimum(jnp.dot(reachable, reachable), 1)
    depth_of = lax.optimization_barrier(jnp.sum(reachable, axis=1, dtype=jnp.int32)) - 1
    allowed = jnp.maximum(reachable, reachable.T) > 0
    return (depth_of, allowed)

def layer_norm(values, gain_vec, shift_vec):
    average = lax.optimization_barrier(jnp.mean(values, axis=-1, keepdims=True))
    centred = values - average
    inv_scale = lax.rsqrt(lax.optimization_barrier(jnp.mean(centred * centred, axis=-1, keepdims=True)) + EPSILON)
    return centred * inv_scale * gain_vec + shift_vec

def tree_layer(inputs, block_parent, params, softened_entries):
    triple_projection_matrix, asker_constant_vector, content_constant_vector, mixer_exit_matrix, mixer_exit_constant, mixer_scaling_factor, mixer_recentering_term, dense_expand_matrix, dense_expand_constant, dense_contract_matrix, dense_contract_constant, dense_scaling_factor, dense_recentering_term = params
    token_count, model_width = inputs.shape
    head_count = softened_entries.shape[0]
    mask_span = softened_entries.shape[1]
    head_size = model_width // head_count
    blocks = block_parent.shape[0]
    block_rows = token_count // blocks
    depth_of, allowed = tree_tables(block_parent)
    offsets = jnp.arange(block_rows, dtype=jnp.int32)
    position = ((depth_of[:, None] * block_rows + offsets[None, :]) % mask_span).reshape(token_count).astype(jnp.int32)
    visible = jnp.repeat(jnp.repeat(allowed, block_rows, axis=0), block_rows, axis=1)
    joined_proj = product(inputs, triple_projection_matrix)
    query_low = low_back(reduced_accuracy(joined_proj[:, :model_width] + asker_constant_vector))
    key_low = low_back(reduced_accuracy(joined_proj[:, model_width:2 * model_width]))
    value_low = low_back(reduced_accuracy(joined_proj[:, 2 * model_width:] + content_constant_vector))
    score_scale = 1.0 / math.sqrt(head_size)

    def one_head(pieces):
        query_head, key_head, value_head, mask_head = pieces
        scores = low_back(product(query_head, key_head.T) * score_scale)
        scores = jnp.where(visible, scores, MASKED)
        shifted = scores - lax.optimization_barrier(jnp.max(scores, axis=1, keepdims=True))
        exponent = jnp.exp(shifted)
        normalized = exponent / lax.optimization_barrier(jnp.sum(exponent, axis=1, keepdims=True))
        pair_mask = mask_head[position][:, position]
        weights = reduced_accuracy(normalized * pair_mask)
        return product(weights, value_head)

    def split_heads(matrix):
        return matrix.reshape(token_count, head_count, head_size).transpose(1, 0, 2)
    head_outs = lax.map(jax.checkpoint(one_head), (split_heads(query_low), split_heads(key_low), split_heads(value_low), softened_entries))
    attended = low_back(reduced_accuracy(head_outs.transpose(1, 0, 2).reshape(token_count, model_width)))
    first_sum = inputs + low_back(product(attended, mixer_exit_matrix) + mixer_exit_constant)
    hidden = layer_norm(first_sum, mixer_scaling_factor, mixer_recentering_term)
    up_proj = low_back(product(reduced_accuracy(hidden), dense_expand_matrix) + dense_expand_constant)
    active = reduced_accuracy(jax.nn.gelu(up_proj, approximate=False))
    second_sum = hidden + low_back(product(active, dense_contract_matrix) + dense_contract_constant)
    return layer_norm(second_sum, dense_scaling_factor, dense_recentering_term)

def reference(layer_entry_matrix, loss_sensitivity, ancestor_block_table, gate_trained_scores, gate_random_jitter, softening_scale, triple_projection_matrix, asker_constant_vector, content_constant_vector, mixer_exit_matrix, mixer_exit_constant, mixer_scaling_factor, mixer_recentering_term, dense_expand_matrix, dense_expand_constant, dense_contract_matrix, dense_contract_constant, dense_scaling_factor, dense_recentering_term):
    params = tuple((entry.astype(jnp.float32) for entry in (triple_projection_matrix, asker_constant_vector, content_constant_vector, mixer_exit_matrix, mixer_exit_constant, mixer_scaling_factor, mixer_recentering_term, dense_expand_matrix, dense_expand_constant, dense_contract_matrix, dense_contract_constant, dense_scaling_factor, dense_recentering_term)))
    tree_count = layer_entry_matrix.shape[0] * layer_entry_matrix.shape[1]
    inputs = layer_entry_matrix.astype(jnp.float32).reshape(tree_count, layer_entry_matrix.shape[2], layer_entry_matrix.shape[3])
    shapes = ancestor_block_table.reshape(tree_count, ancestor_block_table.shape[2])

    def forward(inputs, params, score_entries):
        softened_entries = reduced_accuracy(jax.nn.sigmoid((score_entries + gate_random_jitter) / softening_scale[:, None, None]))

        def tree_step(carried, pieces):
            return (carried, jax.checkpoint(tree_layer)(pieces[0], pieces[1], params, softened_entries))
        carried, outputs = lax.scan(tree_step, jnp.zeros((), jnp.float32), (inputs, shapes))
        return outputs
    outputs, pullback = jax.vjp(forward, inputs, params, gate_trained_scores)
    delta_inputs, delta_params, delta_logits = pullback(loss_sensitivity.astype(jnp.float32).reshape(outputs.shape))
    return (outputs.astype(jnp.bfloat16).reshape(layer_entry_matrix.shape), delta_inputs.astype(jnp.bfloat16).reshape(layer_entry_matrix.shape), delta_params[0], delta_params[1], delta_params[2], delta_params[3], delta_params[4], delta_params[5], delta_params[6], delta_params[7], delta_params[8], delta_params[9], delta_params[10], delta_params[11], delta_params[12], delta_logits)
```

```python
import functools
import math

import jax
import jax.numpy as jnp
from jax import lax
from jax.experimental import pallas as pl
from jax.experimental.pallas import tpu as pltpu
from jax.sharding import PartitionSpec as P

EPSILON = 1e-05
F32 = jnp.float32
BF = jnp.bfloat16
TRUNK = 4
GROUPS = 4
CORES = 2
LOW_HALF = 64


def layer_norm(values, gain_vec, shift_vec):
    average = jnp.mean(values, axis=-1, keepdims=True)
    centred = values - average
    inv_scale = lax.rsqrt(jnp.mean(centred * centred, axis=-1, keepdims=True) + EPSILON)
    normed = centred * inv_scale
    return (normed * gain_vec + shift_vec, normed, inv_scale)


def norm_backward(upstream, normed, inv_scale, gain_vec):
    scaled = upstream * gain_vec
    inner_term = (
        scaled
        - jnp.mean(scaled, axis=-1, keepdims=True)
        - normed * jnp.mean(scaled * normed, axis=-1, keepdims=True)
    )
    return (inv_scale * inner_term, jnp.sum(upstream * normed, axis=0), jnp.sum(upstream, axis=0))


def gelu_parts(values):
    cdf = 0.5 * (1.0 + lax.erf(values / math.sqrt(2.0)))
    density = jnp.exp(-0.5 * values * values) / math.sqrt(2.0 * math.pi)
    return (values * cdf, cdf + values * density)


def dot_nn(left, right):
    return jnp.dot(left, right, preferred_element_type=F32)


def dot_nt(left, right):
    return lax.dot_general(left, right, (((1,), (1,)), ((), ())), preferred_element_type=F32)


def dot_tn(left, right):
    return lax.dot_general(left, right, (((0,), (0,)), ((), ())), preferred_element_type=F32)


def tree_order(parent):
    count = parent.shape[0]
    ids = jnp.arange(count, dtype=jnp.int32)
    up = (parent[:, None] == ids[None, :]) & (ids[:, None] != ids[None, :])
    up = up.astype(F32)
    reach = up
    power = up
    for _ in range(TRUNK + 1):
        power = jnp.sum(power[:, :, None] * up[None, :, :], axis=1)
        reach = reach + power
    depth = jnp.sum(reach, axis=1)
    before = (ids[None, :] < ids[:, None]).astype(F32)
    branch = (depth == TRUNK).astype(F32)
    rank = jnp.sum(before * branch[None, :], axis=1)
    own_rank = jnp.where(depth == TRUNK, rank, jnp.sum(up * rank[None, :], axis=1))
    siblings = jnp.sum(up[:, None, :] * up[None, :, :], axis=2) * before
    second = jnp.sum(siblings, axis=1)
    within = jnp.where(depth == TRUNK, 1.0, 2.0 * second)
    place = jnp.where(depth < TRUNK, depth, TRUNK + 3.0 * own_rank + within).astype(jnp.int32)
    order = jnp.sum((place[:, None] == ids[None, :]) * ids[:, None], axis=0).astype(jnp.int32)
    return (order, place)


def low_lanes():
    return lax.broadcasted_iota(jnp.int32, (1, 2 * LOW_HALF), 1) < LOW_HALF


def one_head(pair, which):
    keep = low_lanes() if which == 0 else jnp.logical_not(low_lanes())
    return jnp.where(keep, pair, jnp.zeros_like(pair))


def group_columns(row, block):
    return ((0, 2 * block, (1, 0)), (0, 3 * block, (1, 0, 1)), (block, 2 * block, (0, 1)))[row]


def mask_columns(mask_rows, tiles, block):
    return jnp.concatenate([mask_rows[:, t * block : (t + 1) * block] for t in tiles], axis=1)


def attend_kernel(block, query_ref, key_ref, value_ref, mask_ref, out_ref, log_ref):
    trunk = TRUNK * block
    wide = 3 * block
    low = low_lanes()

    def soften(parts, masks, values):
        top = parts[0].max(axis=1, keepdims=True)
        for part in parts[1:]:
            top = jnp.maximum(top, part.max(axis=1, keepdims=True))
        total = 0.0
        out = 0.0
        for part, mask, value in zip(parts, masks, values):
            weight = jnp.exp(part - top)
            total = total + weight.sum(axis=1, keepdims=True)
            out = out + dot_nn((weight * mask.astype(F32)).astype(BF), value)
        return (out * (1.0 / total), top + jnp.log(total))

    def emit(rows, results):
        count = results[0][1].shape[0]
        out_ref[rows, :] = jnp.where(low, results[0][0], results[1][0]).astype(BF)
        logs = [jnp.broadcast_to(result[1], (count, 2 * LOW_HALF)) for result in results]
        log_ref[rows, :] = jnp.where(low, logs[0], logs[1])

    def trunk_rows(index, carry):
        rows = pl.ds(pl.multiple_of(index * block, block), block)
        query = query_ref[rows, :]
        results = []
        for which in range(2):
            mask_rows = mask_ref[which, rows, :]
            columns = [(0, trunk, mask_rows)]
            side = mask_columns(mask_rows, (1, 0, 1), block)
            columns += [(trunk + wide * g, wide, side) for g in range(GROUPS)]
            head = one_head(query, which)
            parts = [dot_nt(head, key_ref[c : c + w, :]) for c, w, _ in columns]
            values = [value_ref[c : c + w, :] for c, w, _ in columns]
            results.append(soften(parts, [column[2] for column in columns], values))
        emit(rows, results)
        return carry

    lax.fori_loop(0, TRUNK, trunk_rows, 0)

    def group_rows(group, carry):
        base = pl.multiple_of(trunk + wide * group, block)
        for row in range(3):
            rows = pl.ds(pl.multiple_of(base + block * row, block), block)
            query = query_ref[rows, :]
            tile = 0 if row == 1 else 1
            start, width, tiles = group_columns(row, block)
            columns = pl.ds(pl.multiple_of(base + start, block), width)
            results = []
            for which in range(2):
                mask_rows = mask_ref[which, tile * block : (tile + 1) * block, :]
                head = one_head(query, which)
                parts = [dot_nt(head, key_ref[0:trunk, :]), dot_nt(head, key_ref[columns, :])]
                masks = [mask_rows, mask_columns(mask_rows, tiles, block)]
                values = [value_ref[0:trunk, :], value_ref[columns, :]]
                results.append(soften(parts, masks, values))
            emit(rows, results)
        return carry

    lax.fori_loop(0, GROUPS, group_rows, 0)


def attend(query, key, value, mask, block):
    rows, width = query.shape
    pairs = width // (2 * LOW_HALF)
    span = mask.shape[1]
    spec = pl.BlockSpec((rows, 2 * LOW_HALF), lambda p: (0, p))
    return pl.pallas_call(
        functools.partial(attend_kernel, block),
        grid=(pairs,),
        name="attend",
        in_specs=[spec, spec, spec, pl.BlockSpec((2, span, span), lambda p: (p, 0, 0))],
        out_specs=[spec, spec],
        out_shape=[
            jax.ShapeDtypeStruct((rows, width), BF),
            jax.ShapeDtypeStruct((rows, width), F32),
        ],
        compiler_params=pltpu.CompilerParams(vmem_limit_bytes=48 << 20),
    )(query, key, value, mask)


def attend_back_kernel(
    block,
    scale,
    query_ref,
    key_ref,
    value_ref,
    mask_ref,
    out_ref,
    log_ref,
    delta_ref,
    dquery_ref,
    dkey_ref,
    dvalue_ref,
    dmask_ref,
    key_sum,
    value_sum,
    query_turned,
    delta_turned,
):
    trunk = TRUNK * block
    wide = 3 * block
    low = low_lanes()
    key_sum[...] = jnp.zeros_like(key_sum)
    value_sum[...] = jnp.zeros_like(value_sum)
    dmask_ref[...] = jnp.zeros_like(dmask_ref)
    query_turned[...] = query_ref[...].astype(F32).T.astype(BF)
    delta_turned[...] = delta_ref[...].astype(F32).T.astype(BF)

    def work(rows, mask_place, columns):
        query = query_ref[rows, :]
        delta = delta_ref[rows, :]
        product = delta.astype(F32) * out_ref[rows, :].astype(F32)
        logs = log_ref[rows, :]
        dqueries = []
        for which in range(2):
            first = LOW_HALF * which
            lanes = slice(first, first + LOW_HALF)
            query_head = one_head(query, which)
            delta_head = one_head(delta, which)
            log = logs[:, first : first + 1]
            row_term = jnp.sum(product[:, lanes], axis=1, keepdims=True)
            mask_rows = mask_ref[which, mask_place, :]
            dquery = 0.0
            for place, tiles in columns:
                key = key_ref[place, :]
                value = value_ref[place, :]
                probs = jnp.exp(dot_nt(query_head, key) - log)
                pair = dot_nt(delta_head, value) * probs
                mask = mask_rows if tiles is None else mask_columns(mask_rows, tiles, block)
                mask = mask.astype(F32)
                if tiles is None:
                    dmask_ref[which, mask_place, :] += pair
                else:
                    for tile in sorted(set(tiles)):
                        dmask_ref[which, mask_place, tile * block : (tile + 1) * block] += sum(
                            pair[:, a * block : (a + 1) * block]
                            for a, t in enumerate(tiles)
                            if t == tile
                        )
                dscores = (pair * mask - probs * row_term).astype(BF)
                weights = (probs * mask).astype(BF)
                dquery = dquery + dot_nn(dscores, key)
                key_sum[lanes, place] += dot_nn(query_turned[lanes, rows], dscores)
                value_sum[lanes, place] += dot_nn(delta_turned[lanes, rows], weights)
            dqueries.append(dquery)
        dquery_ref[rows, :] = (jnp.where(low, dqueries[0], dqueries[1]) * scale).astype(BF)

    def trunk_rows(index, carry):
        rows = pl.ds(pl.multiple_of(index * block, block), block)
        columns = [(pl.ds(0, trunk), None)]
        columns += [(pl.ds(trunk + wide * g, wide), (1, 0, 1)) for g in range(GROUPS)]
        work(rows, rows, columns)
        return carry

    lax.fori_loop(0, TRUNK, trunk_rows, 0)

    def group_rows(group, carry):
        base = pl.multiple_of(trunk + wide * group, block)
        for row in range(3):
            rows = pl.ds(pl.multiple_of(base + block * row, block), block)
            tile = 0 if row == 1 else 1
            start, width, tiles = group_columns(row, block)
            near = pl.ds(pl.multiple_of(base + start, block), width)
            work(rows, pl.ds(tile * block, block), [(pl.ds(0, trunk), None), (near, tiles)])
        return carry

    lax.fori_loop(0, GROUPS, group_rows, 0)
    dkey_ref[...] = key_sum[...].T.astype(BF)
    dvalue_ref[...] = value_sum[...].T.astype(BF)


def attend_back(query, key, value, mask, out, logs, delta, block, scale):
    rows, width = query.shape
    pair_width = 2 * LOW_HALF
    pairs = width // pair_width
    span = mask.shape[1]
    spec = pl.BlockSpec((rows, pair_width), lambda p: (0, p))
    mask_spec = pl.BlockSpec((2, span, span), lambda p: (p, 0, 0))
    return pl.pallas_call(
        functools.partial(attend_back_kernel, block, scale),
        grid=(pairs,),
        name="attend_back",
        in_specs=[spec, spec, spec, mask_spec, spec, spec, spec],
        out_specs=[spec, spec, spec, mask_spec],
        out_shape=[jax.ShapeDtypeStruct((rows, width), BF)] * 3
        + [jax.ShapeDtypeStruct(mask.shape, F32)],
        scratch_shapes=[
            pltpu.VMEM((pair_width, rows), F32),
            pltpu.VMEM((pair_width, rows), F32),
            pltpu.VMEM((pair_width, rows), BF),
            pltpu.VMEM((pair_width, rows), BF),
        ],
        compiler_params=pltpu.CompilerParams(vmem_limit_bytes=48 << 20),
    )(query, key, value, mask, out, logs, delta)


def reorder_kernel(order_ref, source_ref, target_ref):
    target_ref[...] = source_ref[...]


def reorder(tokens, order):
    count, block, width = tokens.shape
    return pl.pallas_call(
        reorder_kernel,
        name="reorder",
        grid_spec=pltpu.PrefetchScalarGridSpec(
            num_scalar_prefetch=1,
            grid=(count,),
            in_specs=[pl.BlockSpec((1, block, width), lambda i, order_ref: (order_ref[i], 0, 0))],
            out_specs=pl.BlockSpec((1, block, width), lambda i, order_ref: (i, 0, 0)),
        ),
        out_shape=jax.ShapeDtypeStruct(tokens.shape, tokens.dtype),
    )(order, tokens)


def gather_rows(array, axis=0):
    return lax.all_gather(array, "fsdp", axis=axis, tiled=True)


def per_device(
    layer_entry_matrix,
    loss_sensitivity,
    ancestor_block_table,
    gate_trained_scores,
    gate_random_jitter,
    softening_scale,
    triple_projection_matrix,
    asker_constant_vector,
    content_constant_vector,
    mixer_exit_matrix,
    mixer_exit_constant,
    mixer_scaling_factor,
    mixer_recentering_term,
    dense_expand_matrix,
    dense_expand_constant,
    dense_contract_matrix,
    dense_contract_constant,
    dense_scaling_factor,
    dense_recentering_term,
):
    micro, _, own_rows, width = layer_entry_matrix.shape
    leaf_count = lax.axis_size("leaf")
    blocks = ancestor_block_table.shape[2]
    rows = own_rows * leaf_count
    block = rows // blocks
    heads, _, span = gate_trained_scores.shape
    leaf = lax.axis_index("leaf")
    tree = leaf // CORES
    core = leaf % CORES
    my_heads = heads // CORES
    my_width = width // CORES
    half = rows // CORES
    pairs = [[CORES * i + c for c in range(CORES)] for i in range(leaf_count // CORES)]
    score_scale = 1.0 / math.sqrt(width // heads)

    orders = [tree_order(ancestor_block_table[m, 0]) for m in range(micro)]
    order = jnp.where(tree == 0, orders[0][0], orders[1][0])

    def own_tree(tokens):
        whole = lax.all_gather(tokens[:, 0], "leaf", axis=1, tiled=True)
        mine = lax.dynamic_index_in_dim(whole, tree, 0, keepdims=False)
        return reorder(mine.reshape(blocks, block, width), order).reshape(rows, width)

    def own_tokens(halves):
        whole = lax.all_gather(halves, "leaf", axis=0, tiled=True)
        whole = whole.reshape(micro, blocks, block, width)
        mine = [reorder(whole[m], orders[m][1]) for m in range(micro)]
        mine = jnp.stack(mine).reshape(micro, 1, rows, width)
        return lax.dynamic_slice_in_dim(mine, leaf * own_rows, own_rows, 2)

    def own_half(array):
        return lax.dynamic_slice_in_dim(array, core * half, half, 0)

    softened = jax.nn.sigmoid(
        (gate_trained_scores + gate_random_jitter) / softening_scale[:, None, None]
    )
    relaxed = lax.dynamic_slice_in_dim(softened.astype(BF), core * my_heads, my_heads, 0)
    mask = gather_rows(relaxed, 1)
    joined_weight = gather_rows(triple_projection_matrix)
    out_weight = gather_rows(mixer_exit_matrix)
    up_weight = gather_rows(dense_expand_matrix)
    down_weight = gather_rows(dense_contract_matrix)
    vectors = [
        asker_constant_vector,
        content_constant_vector,
        mixer_exit_constant,
        mixer_scaling_factor,
        mixer_recentering_term,
        dense_contract_constant,
        dense_scaling_factor,
        dense_recentering_term,
        dense_expand_constant,
    ]
    packed = gather_rows(jnp.concatenate(vectors)[None])
    places = []
    first = 0
    for vector in vectors:
        places.append((first, first + vector.shape[0]))
        first += vector.shape[0]
    (
        query_bias,
        value_bias,
        out_bias,
        first_gain,
        first_shift,
        down_bias,
        second_gain,
        second_shift,
        up_bias,
    ) = [packed[:, a:b].reshape(-1).astype(F32) for a, b in places]

    tokens = own_tree(layer_entry_matrix)
    upstream = own_half(own_tree(loss_sensitivity)).astype(F32)

    def my_columns(matrix, which):
        return lax.dynamic_slice_in_dim(matrix, which * width + core * my_width, my_width, 1)

    def my_part(vector):
        return lax.dynamic_slice_in_dim(vector, core * my_width, my_width, 0)

    weight3 = jnp.concatenate([my_columns(joined_weight, i) for i in range(3)], axis=1)
    joined = dot_nn(tokens, weight3)
    query = (joined[:, :my_width] + my_part(query_bias)).astype(BF) * jnp.asarray(score_scale, BF)
    key = joined[:, my_width : 2 * my_width].astype(BF)
    value = (joined[:, 2 * my_width :] + my_part(value_bias)).astype(BF)

    attended_mine, logs = attend(query, key, value, mask, block)
    attended = own_half(
        lax.all_gather(attended_mine, "leaf", axis=1, tiled=True, axis_index_groups=pairs)
    )

    rows_mine = own_half(tokens).astype(F32)
    hidden, normed_first, inv_first = layer_norm(
        rows_mine + dot_nn(attended, out_weight) + out_bias, first_gain, first_shift
    )
    hidden_low = hidden.astype(BF)
    active, slope = gelu_parts(dot_nn(hidden_low, up_weight) + up_bias)
    active = active.astype(BF)
    output, normed_second, inv_second = layer_norm(
        hidden + dot_nn(active, down_weight) + down_bias, second_gain, second_shift
    )
    layer_out = own_tokens(output.astype(BF))

    delta_second, second_gain_grad, second_shift_grad = norm_backward(
        upstream, normed_second, inv_second, second_gain
    )
    delta_branch = delta_second.astype(BF)
    down_weight_grad = dot_tn(active, delta_branch)
    down_bias_grad = jnp.sum(delta_branch.astype(F32), axis=0)
    delta_up = (dot_nt(delta_branch, down_weight) * slope).astype(BF)
    up_weight_grad = dot_tn(hidden_low, delta_up)
    up_bias_grad = jnp.sum(delta_up.astype(F32), axis=0)
    delta_first, first_gain_grad, first_shift_grad = norm_backward(
        delta_second + dot_nt(delta_up, up_weight), normed_first, inv_first, first_gain
    )
    delta_proj = delta_first.astype(BF)
    out_weight_grad = dot_tn(attended, delta_proj)
    out_bias_grad = jnp.sum(delta_proj.astype(F32), axis=0)
    delta_attended = lax.all_gather(
        dot_nt(delta_proj, out_weight).astype(BF),
        "leaf",
        axis=0,
        tiled=True,
        axis_index_groups=pairs,
    )
    delta_attended = lax.dynamic_slice_in_dim(delta_attended, core * my_width, my_width, 1)

    dquery, dkey, dvalue, dmask = attend_back(
        query, key, value, mask, attended_mine, logs, delta_attended, block, score_scale
    )
    djoined = jnp.concatenate([dquery, dkey, dvalue], axis=1)
    joined_grad = dot_tn(tokens, djoined)
    query_bias_grad = jnp.sum(dquery.astype(F32), axis=0)
    value_bias_grad = jnp.sum(dvalue.astype(F32), axis=0)
    dtokens = lax.psum_scatter(
        dot_nt(djoined, weight3).astype(BF),
        "leaf",
        scatter_dimension=0,
        tiled=True,
        axis_index_groups=pairs,
    )
    tokens_grad = own_tokens((delta_first + dtokens.astype(F32)).astype(BF))

    def placed(part, whole_size, start, axis):
        shape = list(part.shape)
        shape[axis] = whole_size
        return lax.dynamic_update_slice_in_dim(jnp.zeros(shape, part.dtype), part, start, axis)

    def owned(grad, axis=0):
        return lax.psum_scatter(
            grad.astype(BF), "fsdp", scatter_dimension=axis, tiled=True
        )

    joined_part = owned(joined_grad)
    joined_full = jnp.zeros((joined_part.shape[0], 3 * width), BF)
    for i in range(3):
        joined_full = lax.dynamic_update_slice_in_dim(
            joined_full,
            joined_part[:, i * my_width : (i + 1) * my_width],
            i * width + core * my_width,
            1,
        )
    matrices = (
        joined_full,
        owned(out_weight_grad),
        owned(up_weight_grad),
        owned(down_weight_grad),
        placed(owned(dmask, 1), heads, core * my_heads, 0),
    )
    joined_total, out_total, up_total, down_total, mask_total = [
        lax.psum(matrix, "leaf").astype(F32) for matrix in matrices
    ]
    small = (
        placed(query_bias_grad, width, core * my_width, 0),
        placed(value_bias_grad, width, core * my_width, 0),
        out_bias_grad,
        first_gain_grad,
        first_shift_grad,
        up_bias_grad,
        down_bias_grad,
        second_gain_grad,
        second_shift_grad,
    )
    fsdp_count = lax.axis_size("fsdp")
    packed_grads = jnp.concatenate([s.reshape(fsdp_count, -1) for s in small], axis=1)
    packed_grads = lax.psum(
        lax.psum_scatter(packed_grads, "fsdp", scatter_dimension=0, tiled=True), "leaf"
    )[0]
    vector_grads = []
    first = 0
    for s in small:
        size = s.shape[0] // fsdp_count
        vector_grads.append(packed_grads[first : first + size])
        first += size
    mask_gradient = mask_total * softened * (1.0 - softened) / softening_scale[:, None, None]
    return (
        layer_out,
        tokens_grad,
        joined_total,
        vector_grads[0],
        vector_grads[1],
        out_total,
        vector_grads[2],
        vector_grads[3],
        vector_grads[4],
        up_total,
        vector_grads[5],
        down_total,
        vector_grads[6],
        vector_grads[7],
        vector_grads[8],
        mask_gradient,
    )


def solution(mesh):
    placed = (
        P(None, "fsdp", "leaf", None),
        P(None, "fsdp", "leaf", None),
        P(None, "fsdp", None),
        P(None, "fsdp", None),
        P(None, "fsdp", None),
        P(),
        P("fsdp", None),
        P("fsdp"),
        P("fsdp"),
        P("fsdp", None),
        P("fsdp"),
        P("fsdp"),
        P("fsdp"),
        P("fsdp", None),
        P("fsdp"),
        P("fsdp", None),
        P("fsdp"),
        P("fsdp"),
        P("fsdp"),
    )
    return jax.shard_map(
        per_device,
        mesh=mesh,
        in_specs=placed,
        out_specs=(
            P(None, "fsdp", "leaf", None),
            P(None, "fsdp", "leaf", None),
            P("fsdp", None),
            P("fsdp"),
            P("fsdp"),
            P("fsdp", None),
            P("fsdp"),
            P("fsdp"),
            P("fsdp"),
            P("fsdp", None),
            P("fsdp"),
            P("fsdp", None),
            P("fsdp"),
            P("fsdp"),
            P("fsdp"),
            P(None, "fsdp", None),
        ),
        check_vma=False,
    )
```

```python
import functools
import math

import jax
import jax.numpy as jnp
from jax import lax
from jax.experimental import pallas as pl
from jax.experimental.pallas import tpu as pltpu
from jax.sharding import PartitionSpec as P

EPSILON = 1e-05
F32 = jnp.float32
BF = jnp.bfloat16
TRUNK = 4
GROUPS = 4
CORES = 2
LOW_HALF = 64


def layer_norm(values, gain_vec, shift_vec):
    average = jnp.mean(values, axis=-1, keepdims=True)
    centred = values - average
    inv_scale = lax.rsqrt(jnp.mean(centred * centred, axis=-1, keepdims=True) + EPSILON)
    normed = centred * inv_scale
    return (normed * gain_vec + shift_vec, normed, inv_scale)


def norm_backward(upstream, normed, inv_scale, gain_vec):
    scaled = upstream * gain_vec
    inner_term = (
        scaled
        - jnp.mean(scaled, axis=-1, keepdims=True)
        - normed * jnp.mean(scaled * normed, axis=-1, keepdims=True)
    )
    return (inv_scale * inner_term, jnp.sum(upstream * normed, axis=0), jnp.sum(upstream, axis=0))


def gelu_parts(values):
    cdf = 0.5 * (1.0 + lax.erf(values / math.sqrt(2.0)))
    density = jnp.exp(-0.5 * values * values) / math.sqrt(2.0 * math.pi)
    return (values * cdf, cdf + values * density)


def dot_nn(left, right):
    return jnp.dot(left, right, preferred_element_type=F32)


def dot_nt(left, right):
    return lax.dot_general(left, right, (((1,), (1,)), ((), ())), preferred_element_type=F32)


def dot_tn(left, right):
    return lax.dot_general(left, right, (((0,), (0,)), ((), ())), preferred_element_type=F32)


def tree_order(parent):
    count = parent.shape[0]
    ids = jnp.arange(count, dtype=jnp.int32)
    up = (parent[:, None] == ids[None, :]) & (ids[:, None] != ids[None, :])
    up = up.astype(F32)
    reach = up
    power = up
    for _ in range(TRUNK + 1):
        power = jnp.sum(power[:, :, None] * up[None, :, :], axis=1)
        reach = reach + power
    depth = jnp.sum(reach, axis=1)
    before = (ids[None, :] < ids[:, None]).astype(F32)
    branch = (depth == TRUNK).astype(F32)
    rank = jnp.sum(before * branch[None, :], axis=1)
    own_rank = jnp.where(depth == TRUNK, rank, jnp.sum(up * rank[None, :], axis=1))
    siblings = jnp.sum(up[:, None, :] * up[None, :, :], axis=2) * before
    second = jnp.sum(siblings, axis=1)
    within = jnp.where(depth == TRUNK, 1.0, 2.0 * second)
    place = jnp.where(depth < TRUNK, depth, TRUNK + 3.0 * own_rank + within).astype(jnp.int32)
    order = jnp.sum((place[:, None] == ids[None, :]) * ids[:, None], axis=0).astype(jnp.int32)
    return (order, place)


def low_lanes():
    return lax.broadcasted_iota(jnp.int32, (1, 2 * LOW_HALF), 1) < LOW_HALF


def one_head(pair, which):
    keep = low_lanes() if which == 0 else jnp.logical_not(low_lanes())
    return jnp.where(keep, pair, jnp.zeros_like(pair))


def group_columns(row, block):
    return ((0, 2 * block, (1, 0)), (0, 3 * block, (1, 0, 1)), (block, 2 * block, (0, 1)))[row]


def mask_columns(mask_rows, tiles, block):
    return jnp.concatenate([mask_rows[:, t * block : (t + 1) * block] for t in tiles], axis=1)


def attend_kernel(block, query_ref, key_ref, value_ref, mask_ref, out_ref, log_ref):
    trunk = TRUNK * block
    wide = 3 * block
    low = low_lanes()

    def soften(parts, masks, values):
        top = parts[0].max(axis=1, keepdims=True)
        for part in parts[1:]:
            top = jnp.maximum(top, part.max(axis=1, keepdims=True))
        total = 0.0
        out = 0.0
        for part, mask, value in zip(parts, masks, values):
            weight = jnp.exp(part - top)
            total = total + weight.sum(axis=1, keepdims=True)
            out = out + dot_nn((weight * mask.astype(F32)).astype(BF), value)
        return (out * (1.0 / total), top + jnp.log(total))

    def emit(rows, results):
        count = results[0][1].shape[0]
        out_ref[rows, :] = jnp.where(low, results[0][0], results[1][0]).astype(BF)
        logs = [jnp.broadcast_to(result[1], (count, 2 * LOW_HALF)) for result in results]
        log_ref[rows, :] = jnp.where(low, logs[0], logs[1])

    def trunk_rows(index, carry):
        rows = pl.ds(pl.multiple_of(index * block, block), block)
        query = query_ref[rows, :]
        results = []
        for which in range(2):
            mask_rows = mask_ref[which, rows, :]
            columns = [(0, trunk, mask_rows)]
            side = mask_columns(mask_rows, (1, 0, 1), block)
            columns += [(trunk + wide * g, wide, side) for g in range(GROUPS)]
            head = one_head(query, which)
            parts = [dot_nt(head, key_ref[c : c + w, :]) for c, w, _ in columns]
            values = [value_ref[c : c + w, :] for c, w, _ in columns]
            results.append(soften(parts, [column[2] for column in columns], values))
        emit(rows, results)
        return carry

    lax.fori_loop(0, TRUNK, trunk_rows, 0)

    def group_rows(group, carry):
        base = pl.multiple_of(trunk + wide * group, block)
        for row in range(3):
            rows = pl.ds(pl.multiple_of(base + block * row, block), block)
            query = query_ref[rows, :]
            tile = 0 if row == 1 else 1
            start, width, tiles = group_columns(row, block)
            columns = pl.ds(pl.multiple_of(base + start, block), width)
            results = []
            for which in range(2):
                mask_rows = mask_ref[which, tile * block : (tile + 1) * block, :]
                head = one_head(query, which)
                parts = [dot_nt(head, key_ref[0:trunk, :]), dot_nt(head, key_ref[columns, :])]
                masks = [mask_rows, mask_columns(mask_rows, tiles, block)]
                values = [value_ref[0:trunk, :], value_ref[columns, :]]
                results.append(soften(parts, masks, values))
            emit(rows, results)
        return carry

    lax.fori_loop(0, GROUPS, group_rows, 0)


def attend(query, key, value, mask, block):
    rows, width = query.shape
    pairs = width // (2 * LOW_HALF)
    span = mask.shape[1]
    spec = pl.BlockSpec((rows, 2 * LOW_HALF), lambda p: (0, p))
    return pl.pallas_call(
        functools.partial(attend_kernel, block),
        grid=(pairs,),
        name="attend",
        in_specs=[spec, spec, spec, pl.BlockSpec((2, span, span), lambda p: (p, 0, 0))],
        out_specs=[spec, spec],
        out_shape=[
            jax.ShapeDtypeStruct((rows, width), BF),
            jax.ShapeDtypeStruct((rows, width), F32),
        ],
        compiler_params=pltpu.CompilerParams(vmem_limit_bytes=48 << 20),
    )(query, key, value, mask)


def attend_back_kernel(
    block,
    scale,
    query_ref,
    key_ref,
    value_ref,
    mask_ref,
    out_ref,
    log_ref,
    delta_ref,
    dquery_ref,
    dkey_ref,
    dvalue_ref,
    dmask_ref,
    key_sum,
    value_sum,
    query_turned,
    delta_turned,
):
    trunk = TRUNK * block
    wide = 3 * block
    low = low_lanes()
    key_sum[...] = jnp.zeros_like(key_sum)
    value_sum[...] = jnp.zeros_like(value_sum)
    dmask_ref[...] = jnp.zeros_like(dmask_ref)
    query_turned[...] = query_ref[...].astype(F32).T.astype(BF)
    delta_turned[...] = delta_ref[...].astype(F32).T.astype(BF)

    def work(rows, mask_place, columns):
        query = query_ref[rows, :]
        delta = delta_ref[rows, :]
        product = delta.astype(F32) * out_ref[rows, :].astype(F32)
        logs = log_ref[rows, :]
        dqueries = []
        for which in range(2):
            first = LOW_HALF * which
            lanes = slice(first, first + LOW_HALF)
            query_head = one_head(query, which)
            delta_head = one_head(delta, which)
            log = logs[:, first : first + 1]
            row_term = jnp.sum(product[:, lanes], axis=1, keepdims=True)
            mask_rows = mask_ref[which, mask_place, :]
            dquery = 0.0
            for place, tiles in columns:
                key = key_ref[place, :]
                value = value_ref[place, :]
                probs = jnp.exp(dot_nt(query_head, key) - log)
                pair = dot_nt(delta_head, value) * probs
                mask = mask_rows if tiles is None else mask_columns(mask_rows, tiles, block)
                mask = mask.astype(F32)
                if tiles is None:
                    dmask_ref[which, mask_place, :] += pair
                else:
                    for tile in sorted(set(tiles)):
                        dmask_ref[which, mask_place, tile * block : (tile + 1) * block] += sum(
                            pair[:, a * block : (a + 1) * block]
                            for a, t in enumerate(tiles)
                            if t == tile
                        )
                dscores = (pair * mask - probs * row_term).astype(BF)
                weights = (probs * mask).astype(BF)
                dquery = dquery + dot_nn(dscores, key)
                key_sum[lanes, place] += dot_nn(query_turned[lanes, rows], dscores)
                value_sum[lanes, place] += dot_nn(delta_turned[lanes, rows], weights)
            dqueries.append(dquery)
        dquery_ref[rows, :] = (jnp.where(low, dqueries[0], dqueries[1]) * scale).astype(BF)

    def trunk_rows(index, carry):
        rows = pl.ds(pl.multiple_of(index * block, block), block)
        columns = [(pl.ds(0, trunk), None)]
        columns += [(pl.ds(trunk + wide * g, wide), (1, 0, 1)) for g in range(GROUPS)]
        work(rows, rows, columns)
        return carry

    lax.fori_loop(0, TRUNK, trunk_rows, 0)

    def group_rows(group, carry):
        base = pl.multiple_of(trunk + wide * group, block)
        for row in range(3):
            rows = pl.ds(pl.multiple_of(base + block * row, block), block)
            tile = 0 if row == 1 else 1
            start, width, tiles = group_columns(row, block)
            near = pl.ds(pl.multiple_of(base + start, block), width)
            work(rows, pl.ds(tile * block, block), [(pl.ds(0, trunk), None), (near, tiles)])
        return carry

    lax.fori_loop(0, GROUPS, group_rows, 0)
    dkey_ref[...] = key_sum[...].T.astype(BF)
    dvalue_ref[...] = value_sum[...].T.astype(BF)


def attend_back(query, key, value, mask, out, logs, delta, block, scale):
    rows, width = query.shape
    pair_width = 2 * LOW_HALF
    pairs = width // pair_width
    span = mask.shape[1]
    spec = pl.BlockSpec((rows, pair_width), lambda p: (0, p))
    mask_spec = pl.BlockSpec((2, span, span), lambda p: (p, 0, 0))
    return pl.pallas_call(
        functools.partial(attend_back_kernel, block, scale),
        grid=(pairs,),
        name="attend_back",
        in_specs=[spec, spec, spec, mask_spec, spec, spec, spec],
        out_specs=[spec, spec, spec, mask_spec],
        out_shape=[jax.ShapeDtypeStruct((rows, width), BF)] * 3
        + [jax.ShapeDtypeStruct(mask.shape, F32)],
        scratch_shapes=[
            pltpu.VMEM((pair_width, rows), F32),
            pltpu.VMEM((pair_width, rows), F32),
            pltpu.VMEM((pair_width, rows), BF),
            pltpu.VMEM((pair_width, rows), BF),
        ],
        compiler_params=pltpu.CompilerParams(vmem_limit_bytes=48 << 20),
    )(query, key, value, mask, out, logs, delta)


def reorder_kernel(order_ref, source_ref, target_ref):
    target_ref[...] = source_ref[...]


def reorder(tokens, order):
    count, block, width = tokens.shape
    return pl.pallas_call(
        reorder_kernel,
        name="reorder",
        grid_spec=pltpu.PrefetchScalarGridSpec(
            num_scalar_prefetch=1,
            grid=(count,),
            in_specs=[pl.BlockSpec((1, block, width), lambda i, order_ref: (order_ref[i], 0, 0))],
            out_specs=pl.BlockSpec((1, block, width), lambda i, order_ref: (i, 0, 0)),
        ),
        out_shape=jax.ShapeDtypeStruct(tokens.shape, tokens.dtype),
    )(order, tokens)


MESH = pl.DeviceIdType.MESH
ANY = pl.BlockSpec(memory_space=pl.ANY)
VMEM = pl.BlockSpec(memory_space=pltpu.VMEM)
SMEM = pl.BlockSpec(memory_space=pltpu.SMEM)
VMEM_LIMIT = 60 << 20
LINE = 4
ALL = slice(None)


class Net:
    def __init__(self, send, recv, local):
        leaf, shard = lax.axis_index("leaf"), lax.axis_index("fsdp")
        self.leaf, self.shard = leaf, shard
        self.x, self.c = leaf // 2, leaf % 2
        self.z, self.y = shard // 2, shard % 2
        self.send, self.recv, self.local = send, recv, local

    def near(self, which):
        x, c, y, z = self.x, self.c, self.y, self.z
        if which == "x":
            x = 1 - x
        elif which == "c":
            c = 1 - c
        elif which == "xc":
            x, c = 1 - x, 1 - c
        elif which == "y":
            y = 1 - y
        else:
            z = (z + which) % LINE
        return (x * 2 + c, z * 2 + y)

    def greet(self, peers):
        barrier = pltpu.get_barrier_semaphore()
        for peer in peers:
            pl.semaphore_signal(barrier, inc=1, device_id=self.near(peer), device_id_type=MESH)
        pl.semaphore_wait(barrier, len(peers))

    def remote(self, row, slot, source, target, peer):
        return pltpu.make_async_remote_copy(
            src_ref=source,
            dst_ref=target,
            send_sem=self.send.at[row, slot],
            recv_sem=self.recv.at[row, slot],
            device_id=self.near(peer),
            device_id_type=MESH,
        )

    def stay(self, row, source, target):
        return pltpu.make_async_copy(source, target, self.local.at[row])


class Gather:
    def __init__(self, net, row, own, whole, share):
        self.net, self.row, self.own, self.whole, self.share = net, row, own, whole, share

    def copy(self, slot):
        net, whole = self.net, self.whole
        x, y, z = net.x, net.y, net.z
        if slot < 3:
            return net.remote(self.row, slot, self.own(x), whole(z, y, x), slot + 1)
        if slot < 6:
            piece = whole((z + LINE - (slot - 2)) % LINE, y, x)
            return net.remote(self.row, slot, piece, piece, "x")
        if slot == 6:
            piece, peer = whole(ALL, y, x), "y"
        elif slot == 7:
            piece, peer = whole(slice(0, 2), 1 - y, x), "x"
        elif slot == 8:
            piece, peer = whole(slice(2, 4), y, 1 - x), "y"
        else:
            piece, peer = whole(ALL, ALL, ALL), "c"
        return net.remote(self.row, slot, piece, piece, peer)

    def home(self):
        return self.net.stay(self.row, self.own(ALL), self.whole(self.net.z, self.net.y, ALL))

    def step(self, number):
        if number == 0:
            self.home().start()
            for slot in range(3):
                self.copy(slot).start()
        elif number == 1:
            self.home().wait()
            for slot in range(3):
                self.copy(slot).wait_recv()
            for slot in range(3, 7):
                self.copy(slot).start()
        elif number == 2:
            for slot in range(3, 7):
                self.copy(slot).wait_recv()
            for slot in (7, 8):
                self.copy(slot).start()
        elif number == 3:
            for slot in (7, 8):
                self.copy(slot).wait_recv()
            if self.share:
                self.copy(9).start()
        elif number == 4:
            if self.share:
                self.copy(9).wait_recv()

    def finish(self):
        for slot in range(10 if self.share else 9):
            self.copy(slot).wait_send()


class Scatter:
    def __init__(self, net, row, load, part, twin, twin_load, first, second, third, final):
        self.net, self.row, self.load, self.part = net, row, load, part
        self.twin, self.twin_load = twin, twin_load
        self.first, self.second, self.third, self.final = first, second, third, final

    def copy(self, slot):
        net, part = self.net, self.part
        x, y, z, c = net.x, net.y, net.z, net.c
        if slot == 0:
            return net.remote(self.row, slot, self.twin_load, self.twin, "c")
        if slot == 1:
            return net.remote(self.row, slot, part.at[0:1, 1 - y, 1 - x], self.first.at[0:1], "x")
        if slot == 2:
            return net.remote(self.row, slot, part.at[1:4, 1 - y, 1 - x], self.first.at[1:4], "y")
        if slot == 3:
            return net.remote(self.row, slot, part.at[:, y, 1 - x], self.second.at[0], "x")
        if slot == 4:
            return net.remote(self.row, slot, part.at[:, 1 - y, x], self.second.at[1], "y")
        if slot < 8:
            step = slot - 4
            piece = part.at[(z + step) % LINE, y, x]
            return net.remote(self.row, slot, piece, self.third.at[step - 1], step)
        peer = ("x", "c", "xc")[slot - 8]
        return net.remote(self.row, slot, part.at[z, y, x], self.final(x, c), peer)

    def home(self):
        return self.net.stay(self.row, self.load, self.part)

    def keep(self):
        net = self.net
        piece = self.part.at[net.z, net.y, net.x]
        return net.stay(self.row, piece, self.final(net.x, net.c))

    def step(self, number):
        net, part = self.net, self.part
        x, y, z = net.x, net.y, net.z
        if number == 0:
            if self.load is not None:
                self.home().start()
            if self.twin is not None:
                self.copy(0).start()
        elif number == 1:
            if self.load is not None:
                self.home().wait()
            if self.twin is not None:
                self.copy(0).wait_recv()
                for a in range(LINE):
                    part[a] = (part[a].astype(F32) + self.twin[a].astype(F32)).astype(BF)
            self.copy(1).start()
            self.copy(2).start()
        elif number == 2:
            self.copy(1).wait_recv()
            other = part[0, 1 - y, x].astype(F32) + self.first[0].astype(F32)
            part[0, 1 - y, x] = other.astype(BF)
            self.copy(2).wait_recv()
            other = part[1:4, y, 1 - x].astype(F32) + self.first[1:4].astype(F32)
            part[1:4, y, 1 - x] = other.astype(BF)
            self.copy(3).start()
            self.copy(4).start()
        elif number == 3:
            self.copy(3).wait_recv()
            self.copy(4).wait_recv()
            mine = part[:, y, x].astype(F32) + self.second[0].astype(F32)
            part[:, y, x] = (mine + self.second[1].astype(F32)).astype(BF)
            for slot in (5, 6, 7):
                self.copy(slot).start()
        elif number == 4:
            total = part[z, y, x].astype(F32)
            for slot in (5, 6, 7):
                self.copy(slot).wait_recv()
                total = total + self.third[slot - 5].astype(F32)
            part[z, y, x] = total.astype(BF)
            for slot in (8, 9, 10):
                self.copy(slot).start()
            self.keep().start()
        elif number == 5:
            self.keep().wait()
            for slot in (8, 9, 10):
                self.copy(slot).wait_recv()

    def finish(self):
        for slot in range(0 if self.twin is not None else 1, 11):
            self.copy(slot).wait_send()


def copy_semaphores(rows, slots):
    return [
        pltpu.SemaphoreType.DMA((rows, slots)),
        pltpu.SemaphoreType.DMA((rows, slots)),
        pltpu.SemaphoreType.DMA((rows,)),
    ]


def run_plan(plan, slot, total):
    for number in range(total):
        steps = [entry for entry in plan if int(entry[0]) == number]
        if steps:

            @pl.when(slot == number)
            def _(steps=steps):
                for _, chunk, step in steps:
                    chunk.step(step)


def run_rest(plan, total):
    for time, chunk, step in plan:
        if time >= total:
            chunk.step(step)


def enter_kernel(
    tokens_ref, joined_ref, mask_ref, vectors_ref, tree_ref, weight_ref, heads_ref, packed_ref, *sems
):
    net = Net(*sems)
    x, c, y, z, leaf = net.x, net.c, net.y, net.z, net.leaf
    piece = joined_ref.shape[2] // 6
    chunks = []
    for i in range(3):
        source = pl.ds(pl.multiple_of((2 * i + c) * piece, piece), piece)
        target = pl.ds(i * piece, piece)
        chunks.append(
            Gather(
                net,
                i,
                lambda half, source=source: joined_ref.at[half, :, source],
                lambda a, b, half, target=target: weight_ref.at[a, b, half, :, target],
                False,
            )
        )
    for i in range(2):
        head = c * (mask_ref.shape[0] // 2) + i
        chunks.append(
            Gather(
                net,
                3 + i,
                lambda half, head=head: mask_ref.at[head, half],
                lambda a, b, half, i=i: heads_ref.at[i, a, b, half],
                False,
            )
        )
    net.greet(("x", "c", "y", 1, 2, 3))
    row = len(chunks)
    half_rows = tokens_ref.shape[1] // 2
    other = (leaf + 2) % 4

    def token_copy(slot):
        part = pl.ds((slot % 2) * half_rows, half_rows)
        if slot < 2:
            return net.remote(row, slot, tokens_ref.at[1 - x, part], tree_ref.at[leaf, part], "x")
        if slot < 4:
            return net.remote(row, slot, tokens_ref.at[x, part], tree_ref.at[leaf, part], "c")
        place = tree_ref.at[other, part]
        return net.remote(row, slot, place, place, "c")

    def vector_copy(slot):
        if slot < 3:
            return net.remote(row + 1, slot, vectors_ref, packed_ref.at[z, y], slot + 1)
        return net.remote(row + 1, slot, packed_ref.at[:, y], packed_ref.at[:, y], "y")

    keep_tokens = net.stay(row, tokens_ref.at[x], tree_ref.at[leaf])
    keep_vectors = net.stay(row + 1, vectors_ref, packed_ref.at[z, y])
    for slot in range(2):
        token_copy(slot).start()
    for slot in range(3):
        vector_copy(slot).start()
    keep_vectors.start()
    keep_tokens.start()
    chunks[0].step(0)
    chunks[1].step(0)
    for slot in (2, 3):
        token_copy(slot).start()
    for time in range(len(chunks) + 2):
        if time < len(chunks):
            chunks[time].step(1)
        if 0 <= time - 2 < len(chunks):
            chunks[time - 2].step(2)
        if time + 2 < len(chunks):
            chunks[time + 2].step(0)
        if time == 1:
            keep_vectors.wait()
            for slot in range(3):
                vector_copy(slot).wait_recv()
            vector_copy(3).start()
        if time == 3:
            token_copy(0).wait_recv()
            token_copy(4).start()
    for chunk in chunks:
        chunk.step(3)
    token_copy(1).wait_recv()
    token_copy(5).start()
    for slot in (2, 3, 4, 5):
        token_copy(slot).wait_recv()
    vector_copy(3).wait_recv()
    keep_tokens.wait()
    for chunk in chunks:
        chunk.finish()
    for slot in range(6):
        token_copy(slot).wait_send()
    for slot in range(4):
        vector_copy(slot).wait_send()


def enter(tokens, joined, mask, vectors):
    micro, rows, width = tokens.shape
    heads, _, strip, span = mask.shape
    _, half, columns = joined.shape
    return pl.pallas_call(
        enter_kernel,
        name="enter",
        in_specs=[ANY] * 4,
        out_specs=[VMEM] * 4,
        out_shape=[
            jax.ShapeDtypeStruct((4, rows, width), BF),
            jax.ShapeDtypeStruct((LINE, 2, 2, half, columns // 2), BF),
            jax.ShapeDtypeStruct((2, LINE, 2, 2, strip, span), BF),
            jax.ShapeDtypeStruct((LINE, 2) + vectors.shape, vectors.dtype),
        ],
        scratch_shapes=copy_semaphores(7, 9),
        compiler_params=pltpu.CompilerParams(
            collective_id=0, has_side_effects=True, vmem_limit_bytes=VMEM_LIMIT
        ),
    )(tokens, joined, mask, vectors)


def joined_kernel(
    order_ref, tree_ref, weight_ref, query_bias_ref, value_bias_ref, tokens_ref, query_ref, key_ref, value_ref, sems
):
    blocks, block, width = tokens_ref.shape
    mine = query_ref.shape[1]
    per = tree_ref.shape[1] // block

    def copy(i):
        place = order_ref[i]
        rows = pl.ds(pl.multiple_of((place % per) * block, block), block)
        return pltpu.make_async_copy(tree_ref.at[place // per, rows], tokens_ref.at[i], sems.at[i])

    for i in range(blocks):
        copy(i).start()

    def project(i, carry):
        copy(2 * i).wait()
        copy(2 * i + 1).wait()
        pair = tokens_ref[pl.ds(2 * i, 2)].reshape(2 * block, width)
        rows = pl.ds(pl.multiple_of(2 * block * i, 2 * block), 2 * block)
        joined = dot_nn(pair, weight_ref[...])
        query = (joined[:, :mine] + query_bias_ref[...]).astype(BF).astype(F32)
        query_ref[rows, :] = (query * (1.0 / math.sqrt(LOW_HALF))).astype(BF)
        key_ref[rows, :] = joined[:, mine : 2 * mine].astype(BF)
        value_ref[rows, :] = (joined[:, 2 * mine :] + value_bias_ref[...]).astype(BF)
        return carry

    lax.fori_loop(0, blocks // 2, project, 0)


def join(order, tree, weight, query_bias, value_bias):
    parts, rows, width = tree.shape
    blocks = order.shape[0]
    block = parts * rows // blocks
    mine = weight.shape[1] // 3
    return pl.pallas_call(
        joined_kernel,
        name="join",
        in_specs=[SMEM, ANY, VMEM, VMEM, VMEM],
        out_specs=[VMEM] * 4,
        out_shape=[jax.ShapeDtypeStruct((blocks, block, width), BF)]
        + [jax.ShapeDtypeStruct((parts * rows, mine), BF)] * 3,
        scratch_shapes=[pltpu.SemaphoreType.DMA((blocks,))],
        compiler_params=pltpu.CompilerParams(vmem_limit_bytes=VMEM_LIMIT),
    )(order, tree, weight, query_bias, value_bias)


def pick_kernel(order_ref, tree_ref, out_ref, sems):
    count, block, _ = out_ref.shape
    per = tree_ref.shape[1] // block
    copies = []
    for i in range(count):
        place = order_ref[i]
        rows = pl.ds(pl.multiple_of((place % per) * block, block), block)
        copies.append(
            pltpu.make_async_copy(tree_ref.at[place // per, rows], out_ref.at[i], sems.at[i])
        )
    for copy in copies:
        copy.start()
    for copy in copies:
        copy.wait()


def pick(order, tree, block):
    count = order.shape[0]
    return pl.pallas_call(
        pick_kernel,
        name="pick",
        in_specs=[SMEM, ANY],
        out_specs=VMEM,
        out_shape=jax.ShapeDtypeStruct((count, block, tree.shape[2]), tree.dtype),
        scratch_shapes=[pltpu.SemaphoreType.DMA((count,))],
        compiler_params=pltpu.CompilerParams(vmem_limit_bytes=VMEM_LIMIT),
    )(order, tree)


class Sharing:
    def __init__(self, net, row, own, tree):
        self.net, self.row, self.own, self.tree = net, row, own, tree

    def copy(self, slot):
        net, own, tree = self.net, self.own, self.tree
        half = own.shape[1] // 2
        part = pl.ds((slot % 2) * half, half)
        if slot < 2:
            return net.remote(self.row, slot, own.at[1 - net.x, part], tree.at[net.leaf, part], "x")
        if slot < 4:
            return net.remote(self.row, slot, own.at[net.x, part], tree.at[net.leaf, part], "c")
        place = tree.at[(net.leaf + 2) % 4, part]
        return net.remote(self.row, slot, place, place, "c")

    def home(self):
        return self.net.stay(self.row, self.own.at[self.net.x], self.tree.at[self.net.leaf])

    def step(self, number):
        if number == 0:
            for slot in range(4):
                self.copy(slot).start()
            self.home().start()
        elif number < 3:
            self.copy(number - 1).wait_recv()
            self.copy(number + 3).start()
        elif number == 3:
            for slot in (2, 3, 4, 5):
                self.copy(slot).wait_recv()
            self.home().wait()

    def finish(self):
        for slot in range(6):
            self.copy(slot).wait_send()


ATTEND_PLAN = (1.9, 1.5, 3.0, 3.0, 3.0)


def attend_wide_kernel(
    block,
    query_ref,
    key_ref,
    value_ref,
    first_ref,
    relaxed_ref,
    out_shard,
    up_shard,
    down_shard,
    upstream_ref,
    attended_ref,
    log_ref,
    whole_ref,
    mask_ref,
    out_weight,
    up_weight,
    down_weight,
    tree_ref,
    *sems,
):
    net = Net(*sems)
    c = net.c
    trunk = TRUNK * block
    wide = 3 * block
    low = low_lanes()
    rows_all, width_all = query_ref.shape
    pairs = width_all // (2 * LOW_HALF)
    heads = relaxed_ref.shape[0] // 2
    half = rows_all // 2
    piece = out_shard.shape[2] // 2
    chunks = []
    for h in range(2, heads):
        head = c * heads + h
        chunks.append(
            Gather(
                net,
                len(chunks),
                lambda part, head=head: relaxed_ref.at[head, part],
                lambda a, b, part, h=h: mask_ref.at[h, a, b, part],
                False,
            )
        )
    columns = pl.ds(pl.multiple_of(c * piece, piece), piece)
    chunks.append(
        Gather(
            net,
            len(chunks),
            lambda part: out_shard.at[part, :, columns],
            lambda a, b, part: out_weight.at[a, b, part, :, columns],
            True,
        )
    )
    for j in range(4):
        place = pl.ds(pl.multiple_of((4 * c + j) * piece, piece), piece)
        chunks.append(
            Gather(
                net,
                len(chunks),
                lambda part, place=place: up_shard.at[part, :, place],
                lambda a, b, part, place=place: up_weight.at[a, b, part, :, place],
                True,
            )
        )
    for j in range(4):
        chunks.append(
            Gather(
                net,
                len(chunks),
                lambda part, j=j: down_shard.at[j, part, :, columns],
                lambda a, b, part, j=j: down_weight.at[a, b, j, part, :, columns],
                True,
            )
        )
    share = Sharing(net, len(chunks), upstream_ref, tree_ref)
    net.greet(("x", "c", "y", 1, 2, 3))
    first_copy = net.stay(len(chunks) + 1, first_ref, mask_ref.at[0:2])
    first_copy.start()
    total = 8 * pairs
    plan = []
    pace, lead, lag1, lag2, lag3 = ATTEND_PLAN
    for i, chunk in enumerate(chunks):
        start = i * pace
        plan.append((max(0.0, start - lead), chunk, 0))
        start = start + lag1
        for step in (1, 2, 3, 4):
            plan.append((start, chunk, step))
            start = start + (lag2, lag3, lag3, lag3)[step - 1]
    for i in range(4):
        plan.append(((4 + 3 * i) * pace, share, i))
    fixed = []
    for time, chunk, step in plan:
        for h in range(2, heads):
            if chunk is chunks[h - 2]:
                time = min(time, 8 * (h // 2) - 0.01 * (4 - step))
        fixed.append((time, chunk, step))
    plan = sorted(fixed, key=lambda entry: entry[0])
    first_copy.wait()

    def soften(parts, masks, values):
        top = parts[0].max(axis=1, keepdims=True)
        for part in parts[1:]:
            top = jnp.maximum(top, part.max(axis=1, keepdims=True))
        scale = 0.0
        out = 0.0
        for part, mask, value in zip(parts, masks, values):
            weight = jnp.exp(part - top)
            scale = scale + weight.sum(axis=1, keepdims=True)
            out = out + dot_nn((weight * mask.astype(F32)).astype(BF), value)
        return (out * (1.0 / scale), top + jnp.log(scale))

    def emit(rows, lanes, results):
        count = results[0][1].shape[0]
        attended_ref[rows, lanes] = jnp.where(low, results[0][0], results[1][0]).astype(BF)
        logs = [jnp.broadcast_to(result[1], (count, 2 * LOW_HALF)) for result in results]
        log_ref[rows, lanes] = jnp.where(low, logs[0], logs[1])

    def one_pair(p, carry):
        lanes = pl.ds(pl.multiple_of(p * 2 * LOW_HALF, 2 * LOW_HALF), 2 * LOW_HALF)

        def mask_strip(which, tile):
            return mask_ref[2 * p + which, tile].reshape(block, mask_ref.shape[-1])

        def trunk_rows(index, carry):
            run_plan(plan, 8 * p + index, total)
            rows = pl.ds(pl.multiple_of(index * block, block), block)
            query = query_ref[rows, lanes]
            results = []
            for which in range(2):
                mask_rows = mask_strip(which, index)
                columns = [(0, trunk, mask_rows)]
                side = mask_columns(mask_rows, (1, 0, 1), block)
                columns += [(trunk + wide * g, wide, side) for g in range(GROUPS)]
                head = one_head(query, which)
                parts = [dot_nt(head, key_ref[a : a + w, lanes]) for a, w, _ in columns]
                values = [value_ref[a : a + w, lanes] for a, w, _ in columns]
                results.append(soften(parts, [column[2] for column in columns], values))
            emit(rows, lanes, results)
            return carry

        lax.fori_loop(0, TRUNK, trunk_rows, 0)

        def group_rows(group, carry):
            run_plan(plan, 8 * p + 4 + group, total)
            base = pl.multiple_of(trunk + wide * group, block)
            for row in range(3):
                rows = pl.ds(pl.multiple_of(base + block * row, block), block)
                query = query_ref[rows, lanes]
                tile = 0 if row == 1 else 1
                start, width, tiles = group_columns(row, block)
                columns = pl.ds(pl.multiple_of(base + start, block), width)
                results = []
                for which in range(2):
                    mask_rows = mask_strip(which, tile)
                    head = one_head(query, which)
                    parts = [
                        dot_nt(head, key_ref[0:trunk, lanes]),
                        dot_nt(head, key_ref[columns, lanes]),
                    ]
                    masks = [mask_rows, mask_columns(mask_rows, tiles, block)]
                    values = [value_ref[0:trunk, lanes], value_ref[columns, lanes]]
                    results.append(soften(parts, masks, values))
                emit(rows, lanes, results)
            return carry

        lax.fori_loop(0, GROUPS, group_rows, 0)
        return carry

    lax.fori_loop(0, pairs, one_pair, 0)
    mine = pl.ds(pl.multiple_of(c * half, half), half)
    theirs = pl.ds(pl.multiple_of((1 - c) * half, half), half)
    place = pl.ds(pl.multiple_of(c * width_all, width_all), width_all)
    cross = net.remote(
        len(chunks) + 1, 0, attended_ref.at[theirs], whole_ref.at[:, place], "c"
    )
    cross.start()
    whole_ref[:, place] = attended_ref[mine, :]
    run_rest(plan, total)
    cross.wait_recv()
    for chunk in chunks + [share]:
        chunk.finish()
    cross.wait_send()


def attend_wide(query, key, value, first, relaxed, out_shard, up_shard, down_shard, upstream, block):
    rows, width = query.shape
    heads = relaxed.shape[0] // 2
    grown = lambda shard: jax.ShapeDtypeStruct((LINE, 2) + shard.shape, BF)
    return pl.pallas_call(
        functools.partial(attend_wide_kernel, block),
        name="attend_wide",
        in_specs=[VMEM] * 3 + [ANY] * 6,
        out_specs=[VMEM] * 8,
        out_shape=[
            jax.ShapeDtypeStruct((rows, width), BF),
            jax.ShapeDtypeStruct((rows, width), F32),
            jax.ShapeDtypeStruct((rows // 2, 2 * width), BF),
            jax.ShapeDtypeStruct((heads,) + first.shape[1:], BF),
            grown(out_shard),
            grown(up_shard),
            grown(down_shard),
            jax.ShapeDtypeStruct((4,) + upstream.shape[1:], BF),
        ],
        scratch_shapes=copy_semaphores(15, 10),
        compiler_params=pltpu.CompilerParams(
            collective_id=1, has_side_effects=True, vmem_limit_bytes=VMEM_LIMIT
        ),
    )(query, key, value, first, relaxed, out_shard, up_shard, down_shard, upstream)


BACK_PLAN = (1.6, 1.0, 1.6, 1.6, 1.6, 1.6)


def attend_back_wide_kernel(
    block,
    scale,
    query_ref,
    key_ref,
    value_ref,
    mask_ref,
    out_ref,
    log_ref,
    delta_half,
    layer_half,
    place_ref,
    out_grad,
    up_grad,
    down_grad,
    dquery_ref,
    dkey_ref,
    dvalue_ref,
    last_ref,
    out_final,
    up_final,
    down_final,
    mask_final,
    layer_ref,
    delta_ref,
    key_sum,
    value_sum,
    query_turned,
    delta_turned,
    dmask_sum,
    part,
    twin,
    first,
    second,
    third,
    mask_part,
    mask_first,
    mask_second,
    mask_third,
    layer_tree,
    layer_own,
    *sems,
):
    net = Net(*sems)
    x, c, leaf = net.x, net.c, net.leaf
    trunk = TRUNK * block
    wide = 3 * block
    low = low_lanes()
    rows_all, width_all = query_ref.shape
    pairs = width_all // (2 * LOW_HALF)
    half = rows_all // 2
    piece = width_all
    total = 8 * pairs
    ready = 2 * (pairs - 1)
    chunks = []

    def dense(load, twin_load, final):
        k = len(chunks)
        chunks.append(
            Scatter(
                net,
                k,
                load,
                part.at[k],
                twin.at[k],
                twin_load,
                first.at[k],
                second.at[k],
                third.at[k],
                final,
            )
        )

    def own(core):
        return pl.ds(pl.multiple_of(core * piece, piece), piece)

    dense(
        out_grad.at[:, :, :, :, own(c)],
        out_grad.at[:, :, :, :, own(1 - c)],
        lambda a, b: out_final.at[a, :, own(b)],
    )
    for j in range(4):
        dense(
            down_grad.at[:, :, j, :, :, own(c)],
            down_grad.at[:, :, j, :, :, own(1 - c)],
            lambda a, b, j=j: down_final.at[j, a, :, own(b)],
        )
    for j in range(4):
        dense(
            up_grad.at[:, :, :, :, own(4 * c + j)],
            up_grad.at[:, :, :, :, own(4 * (1 - c) + j)],
            lambda a, b, j=j: up_final.at[a, :, own(4 * b + j)],
        )
    dense_count = len(chunks)
    for h in range(ready):
        chunks.append(
            Scatter(
                net,
                len(chunks),
                None,
                mask_part.at[h],
                None,
                None,
                mask_first.at[h],
                mask_second.at[h],
                mask_third.at[h],
                lambda a, b, h=h: mask_final.at[b, h, a],
            )
        )
    spare = len(chunks)
    net.greet(("x", "c", "xc", "y", 1, 2, 3))

    mine = pl.ds(pl.multiple_of(c * half, half), half)
    delta_cross = net.remote(spare, 0, delta_half.at[:, own(1 - c)], delta_ref.at[mine], "c")
    delta_cross.start()
    delta_home = net.stay(spare, delta_half.at[:, own(c)], delta_ref.at[mine])
    delta_home.start()

    layer_rows = layer_ref.shape[1]
    per = layer_rows // block
    blocks_mine = pl.ds(c * 2 * per, 2 * per)

    class Output:
        def copies(self):
            return (
                net.remote(spare, 1, layer_half, layer_tree.at[blocks_mine], "c"),
                net.remote(spare, 2, layer_own.at[1 - x], layer_ref.at[x], "x"),
            )

        def home(self):
            return net.stay(spare + 1, layer_half, layer_tree.at[blocks_mine])

        def step(self, number):
            to_core, to_chip = self.copies()
            if number == 0:
                to_core.start()
                self.home().start()
            elif number == 1:
                to_core.wait_recv()
                self.home().wait()
                for a in range(2):
                    for b in range(per):
                        place = place_ref[(2 * a + c) * per + b]
                        layer_own[a, b * block : (b + 1) * block] = layer_tree[place]
                to_chip.start()
                layer_ref[x] = layer_own[x]
            elif number == 2:
                to_chip.wait_recv()

        def finish(self):
            for copy in self.copies():
                copy.wait_send()

    output = Output()
    plan = []
    pace, lag0, lag1, lag2, lag3, lag4 = BACK_PLAN
    for i, chunk in enumerate(chunks):
        start = i * pace
        if i >= dense_count:
            start = max(start, 8.0 * ((i - dense_count) // 2 + 1) + 0.1 * (i % 2))
        for step in range(6):
            plan.append((start, chunk, step))
            start = start + (lag0, lag1, lag2, lag3, lag4, 0)[step]
    plan += [(0.0, output, 0), (1.0, output, 1), (12.0, output, 2)]
    plan = sorted(plan, key=lambda entry: entry[0])
    delta_home.wait()
    delta_cross.wait_recv()

    def one_pair(p, carry):
        pair_lanes = pl.ds(pl.multiple_of(p * 2 * LOW_HALF, 2 * LOW_HALF), 2 * LOW_HALF)
        key_sum[...] = jnp.zeros_like(key_sum)
        value_sum[...] = jnp.zeros_like(value_sum)
        dmask_sum[...] = jnp.zeros_like(dmask_sum)
        query_turned[...] = query_ref[:, pair_lanes].astype(F32).T.astype(BF)
        delta_turned[...] = delta_ref[:, pair_lanes].astype(F32).T.astype(BF)

        def work(rows, mask_place, columns):
            query = query_ref[rows, pair_lanes]
            delta = delta_ref[rows, pair_lanes]
            product = delta.astype(F32) * out_ref[rows, pair_lanes].astype(F32)
            logs = log_ref[rows, pair_lanes]
            dqueries = []
            for which in range(2):
                start = LOW_HALF * which
                lanes = slice(start, start + LOW_HALF)
                query_head = one_head(query, which)
                delta_head = one_head(delta, which)
                log = logs[:, start : start + 1]
                row_term = jnp.sum(product[:, lanes], axis=1, keepdims=True)
                mask_rows = mask_ref[2 * p + which, mask_place, :]
                dquery = 0.0
                for place, tiles in columns:
                    key = key_ref[place, pair_lanes]
                    value = value_ref[place, pair_lanes]
                    probs = jnp.exp(dot_nt(query_head, key) - log)
                    pair = dot_nt(delta_head, value) * probs
                    mask = mask_rows if tiles is None else mask_columns(mask_rows, tiles, block)
                    mask = mask.astype(F32)
                    if tiles is None:
                        dmask_sum[which, mask_place, :] += pair
                    else:
                        for tile in sorted(set(tiles)):
                            dmask_sum[which, mask_place, tile * block : (tile + 1) * block] += sum(
                                pair[:, a * block : (a + 1) * block]
                                for a, t in enumerate(tiles)
                                if t == tile
                            )
                    dscores = (pair * mask - probs * row_term).astype(BF)
                    weights = (probs * mask).astype(BF)
                    dquery = dquery + dot_nn(dscores, key)
                    key_sum[lanes, place] += dot_nn(query_turned[lanes, rows], dscores)
                    value_sum[lanes, place] += dot_nn(delta_turned[lanes, rows], weights)
                dqueries.append(dquery)
            both = jnp.where(low, dqueries[0], dqueries[1]) * scale
            dquery_ref[rows, pair_lanes] = both.astype(BF)

        def trunk_rows(index, carry):
            run_plan(plan, 8 * p + index, total)
            rows = pl.ds(pl.multiple_of(index * block, block), block)
            columns = [(pl.ds(0, trunk), None)]
            columns += [(pl.ds(trunk + wide * g, wide), (1, 0, 1)) for g in range(GROUPS)]
            work(rows, rows, columns)
            return carry

        lax.fori_loop(0, TRUNK, trunk_rows, 0)

        def group_rows(group, carry):
            run_plan(plan, 8 * p + 4 + group, total)
            base = pl.multiple_of(trunk + wide * group, block)
            for row in range(3):
                rows = pl.ds(pl.multiple_of(base + block * row, block), block)
                tile = 0 if row == 1 else 1
                start, width, tiles = group_columns(row, block)
                near = pl.ds(pl.multiple_of(base + start, block), width)
                work(rows, pl.ds(tile * block, block), [(pl.ds(0, trunk), None), (near, tiles)])
            return carry

        lax.fori_loop(0, GROUPS, group_rows, 0)
        dkey_ref[:, pair_lanes] = key_sum[...].T.astype(BF)
        dvalue_ref[:, pair_lanes] = value_sum[...].T.astype(BF)
        shape = mask_part.shape[2:]

        def put(target, at):
            for which in range(2):
                for tile in range(LINE):
                    strip = dmask_sum[which, tile * block : (tile + 1) * block, :].astype(BF)
                    target[at + which, tile] = strip.reshape(shape)

        @pl.when(p < pairs - 1)
        def _():
            put(mask_part, 2 * p)

        @pl.when(p == pairs - 1)
        def _():
            put(last_ref, 0)

        return carry

    lax.fori_loop(0, pairs, one_pair, 0)
    run_rest(plan, total)
    for chunk in chunks + [output]:
        chunk.finish()
    delta_cross.wait_send()


def scatter_buffers(count, shape, with_twin):
    half, columns = shape
    whole = pltpu.VMEM((count, LINE, 2, 2, half, columns), BF)
    line = pltpu.VMEM((count, LINE, half, columns), BF)
    return (
        [whole]
        + ([whole] if with_twin else [])
        + [
            line,
            pltpu.VMEM((count, 2, LINE, half, columns), BF),
            pltpu.VMEM((count, LINE - 1, half, columns), BF),
        ]
    )


def attend_back_wide(
    query, key, value, mask, out, logs, delta, layer, place, out_grad, up_grad, down_grad, block, scale
):
    rows, width = query.shape
    heads, span, _ = mask.shape
    half = rows // 2
    strip = span // 16
    own_rows = rows // 4
    piece_rows = out_grad.shape[3]
    like = jax.ShapeDtypeStruct
    return pl.pallas_call(
        functools.partial(attend_back_wide_kernel, block, scale),
        name="attend_back_wide",
        in_specs=[VMEM] * 6 + [ANY] * 2 + [SMEM] + [ANY] * 3,
        out_specs=[VMEM] * 9,
        out_shape=[like((rows, width), BF)] * 3
        + [
            like((2, LINE, 2, 2, strip, span), BF),
            like((2,) + out_grad.shape[3:], BF),
            like((2,) + up_grad.shape[3:], BF),
            like((4, 2) + down_grad.shape[4:], BF),
            like((2, heads - 2, 2, strip, span), BF),
            like((2, own_rows, 2 * width), BF),
        ],
        scratch_shapes=[
            pltpu.VMEM((rows, width), BF),
            pltpu.VMEM((2 * LOW_HALF, rows), F32),
            pltpu.VMEM((2 * LOW_HALF, rows), F32),
            pltpu.VMEM((2 * LOW_HALF, rows), BF),
            pltpu.VMEM((2 * LOW_HALF, rows), BF),
            pltpu.VMEM((2, span, span), F32),
        ]
        + scatter_buffers(9, (piece_rows, width), True)
        + scatter_buffers(heads - 2, (strip, span), False)
        + [
            pltpu.VMEM((2 * layer.shape[0],) + layer.shape[1:], BF),
            pltpu.VMEM((2, own_rows, 2 * width), BF),
        ]
        + copy_semaphores(15, 11),
        compiler_params=pltpu.CompilerParams(
            collective_id=2, has_side_effects=True, vmem_limit_bytes=VMEM_LIMIT
        ),
    )(query, key, value, mask, out, logs, delta, layer, place, out_grad, up_grad, down_grad)


def leave_kernel(
    block,
    tokens_ref,
    place_ref,
    last_ref,
    joined_ref,
    vectors_ref,
    mask_final,
    joined_final,
    tokens_out,
    vectors_out,
    part,
    first,
    second,
    third,
    mask_part,
    mask_first,
    mask_second,
    mask_third,
    give,
    keep,
    got,
    sums,
    from_core,
    from_chip,
    from_y,
    from_z,
    *sems,
):
    net = Net(*sems)
    x, c, y, z = net.x, net.c, net.y, net.z
    width = joined_ref.shape[4] // 3
    chunks = []
    for h in range(2):
        chunks.append(
            Scatter(
                net,
                len(chunks),
                last_ref.at[h],
                mask_part.at[h],
                None,
                None,
                mask_first.at[h],
                mask_second.at[h],
                mask_third.at[h],
                lambda a, b, h=h: mask_final.at[b, h, a],
            )
        )

    def joined_place(a, b, i):
        return joined_final.at[a, :, pl.ds(pl.multiple_of((2 * i + b) * width, width), width)]

    for i in range(3):
        chunks.append(
            Scatter(
                net,
                len(chunks),
                joined_ref.at[:, :, :, :, pl.ds(i * width, width)],
                part.at[i],
                None,
                None,
                first.at[i],
                second.at[i],
                third.at[i],
                lambda a, b, i=i: joined_place(a, b, i),
            )
        )
    row = len(chunks)
    net.greet(("x", "c", "xc", "y", 1, 2, 3))
    for chunk in chunks:
        chunk.step(0)
    own_rows = give.shape[1]
    per = own_rows // block

    def collect(target, core):
        for a in range(2):
            for b in range(per):
                place = place_ref[(2 * a + core) * per + b]
                target[a, b * block : (b + 1) * block] = tokens_ref[place]

    collect(give, 1 - c)
    core_copy = net.remote(row, 0, give, got, "c")
    core_copy.start()
    vector_copies = (
        net.remote(row, 1, vectors_ref, from_core, "c"),
        net.remote(row, 2, sums.at[0], from_chip, "x"),
        net.remote(row, 3, sums.at[1, :, 1 - y], from_y, "y"),
    )
    vector_copies[0].start()
    for chunk in chunks:
        chunk.step(1)
    collect(keep, c)
    core_copy.wait_recv()
    keep[...] = (keep[...].astype(F32) + got[...].astype(F32)).astype(BF)
    chip_copy = net.remote(row, 4, keep.at[1 - x], tokens_out.at[x], "x")
    chip_copy.start()
    tokens_out[x] = keep[x]
    vector_copies[0].wait_recv()
    sums[0] = vectors_ref[...] + from_core[...]
    vector_copies[1].start()
    for chunk in chunks:
        chunk.step(2)
    vector_copies[1].wait_recv()
    sums[1] = sums[0] + from_chip[...]
    vector_copies[2].start()
    for chunk in chunks:
        chunk.step(3)
    vector_copies[2].wait_recv()
    sums[2, :, 0] = sums[1, :, y] + from_y[...]
    line_copies = [
        net.remote(row, 4 + step, sums.at[2, (z + step) % LINE, 0], from_z.at[step - 1], step)
        for step in (1, 2, 3)
    ]
    for copy in line_copies:
        copy.start()
    for chunk in chunks:
        chunk.step(4)
    total = sums[2, z, 0]
    for i, copy in enumerate(line_copies):
        copy.wait_recv()
        total = total + from_z[i]
    vectors_out[...] = total
    for chunk in chunks:
        chunk.step(5)
    chip_copy.wait_recv()
    for chunk in chunks:
        chunk.finish()
    core_copy.wait_send()
    chip_copy.wait_send()
    for copy in vector_copies + tuple(line_copies):
        copy.wait_send()


def leave(tokens, place, last, joined, vectors, block):
    blocks, _, width = tokens.shape
    like = jax.ShapeDtypeStruct
    own_rows = blocks * block // 4
    strip, span = last.shape[4:]
    half, columns = joined.shape[3:]
    return pl.pallas_call(
        functools.partial(leave_kernel, block),
        name="leave",
        in_specs=[VMEM, SMEM, ANY, ANY, VMEM],
        out_specs=[VMEM] * 4,
        out_shape=[
            like((2, 2, 2, strip, span), BF),
            like((2, half, 2 * columns), BF),
            like((2, own_rows, width), BF),
            like(vectors.shape[2:], F32),
        ],
        scratch_shapes=scatter_buffers(3, (half, columns // 3), False)
        + scatter_buffers(2, (strip, span), False)
        + [pltpu.VMEM((2, own_rows, width), BF)] * 3
        + [
            pltpu.VMEM((3,) + vectors.shape, F32),
            pltpu.VMEM(vectors.shape, F32),
            pltpu.VMEM(vectors.shape, F32),
            pltpu.VMEM(vectors.shape[:1] + vectors.shape[2:], F32),
            pltpu.VMEM((LINE - 1,) + vectors.shape[2:], F32),
        ]
        + copy_semaphores(6, 11),
        compiler_params=pltpu.CompilerParams(
            collective_id=3, has_side_effects=True, vmem_limit_bytes=VMEM_LIMIT
        ),
    )(tokens, place, last, joined, vectors)


def gather_rows(array, axis=0):
    return lax.all_gather(array, "fsdp", axis=axis, tiled=True)


def per_device(
    layer_entry_matrix,
    loss_sensitivity,
    ancestor_block_table,
    gate_trained_scores,
    gate_random_jitter,
    softening_scale,
    triple_projection_matrix,
    asker_constant_vector,
    content_constant_vector,
    mixer_exit_matrix,
    mixer_exit_constant,
    mixer_scaling_factor,
    mixer_recentering_term,
    dense_expand_matrix,
    dense_expand_constant,
    dense_contract_matrix,
    dense_contract_constant,
    dense_scaling_factor,
    dense_recentering_term,
):
    micro, _, own_rows, width = layer_entry_matrix.shape
    leaf_count = lax.axis_size("leaf")
    blocks = ancestor_block_table.shape[2]
    rows = own_rows * leaf_count
    block = rows // blocks
    heads, _, span = gate_trained_scores.shape
    leaf = lax.axis_index("leaf")
    tree = leaf // CORES
    core = leaf % CORES
    my_heads = heads // CORES
    my_width = width // CORES
    half = rows // CORES
    pairs = [[CORES * i + c for c in range(CORES)] for i in range(leaf_count // CORES)]
    score_scale = 1.0 / math.sqrt(width // heads)

    orders = [tree_order(ancestor_block_table[m, 0]) for m in range(micro)]
    order = jnp.where(tree == 0, orders[0][0], orders[1][0])

    def own_tree(tokens):
        whole = lax.all_gather(tokens[:, 0], "leaf", axis=1, tiled=True)
        mine = lax.dynamic_index_in_dim(whole, tree, 0, keepdims=False)
        return reorder(mine.reshape(blocks, block, width), order).reshape(rows, width)

    def own_tokens(halves):
        whole = lax.all_gather(halves, "leaf", axis=0, tiled=True)
        whole = whole.reshape(micro, blocks, block, width)
        mine = [reorder(whole[m], orders[m][1]) for m in range(micro)]
        mine = jnp.stack(mine).reshape(micro, 1, rows, width)
        return lax.dynamic_slice_in_dim(mine, leaf * own_rows, own_rows, 2)

    def own_half(array):
        return lax.dynamic_slice_in_dim(array, core * half, half, 0)

    softened = jax.nn.sigmoid(
        (gate_trained_scores + gate_random_jitter) / softening_scale[:, None, None]
    )
    relaxed = lax.dynamic_slice_in_dim(softened.astype(BF), core * my_heads, my_heads, 0)
    mask = gather_rows(relaxed, 1)
    joined_weight = gather_rows(triple_projection_matrix)
    out_weight = gather_rows(mixer_exit_matrix)
    up_weight = gather_rows(dense_expand_matrix)
    down_weight = gather_rows(dense_contract_matrix)
    vectors = [
        asker_constant_vector,
        content_constant_vector,
        mixer_exit_constant,
        mixer_scaling_factor,
        mixer_recentering_term,
        dense_contract_constant,
        dense_scaling_factor,
        dense_recentering_term,
        dense_expand_constant,
    ]
    packed = gather_rows(jnp.concatenate(vectors)[None])
    places = []
    first = 0
    for vector in vectors:
        places.append((first, first + vector.shape[0]))
        first += vector.shape[0]
    (
        query_bias,
        value_bias,
        out_bias,
        first_gain,
        first_shift,
        down_bias,
        second_gain,
        second_shift,
        up_bias,
    ) = [packed[:, a:b].reshape(-1).astype(F32) for a, b in places]

    tokens = own_tree(layer_entry_matrix)
    upstream = own_half(own_tree(loss_sensitivity)).astype(F32)

    def my_columns(matrix, which):
        return lax.dynamic_slice_in_dim(matrix, which * width + core * my_width, my_width, 1)

    def my_part(vector):
        return lax.dynamic_slice_in_dim(vector, core * my_width, my_width, 0)

    weight3 = jnp.concatenate([my_columns(joined_weight, i) for i in range(3)], axis=1)
    joined = dot_nn(tokens, weight3)
    query = (joined[:, :my_width] + my_part(query_bias)).astype(BF) * jnp.asarray(score_scale, BF)
    key = joined[:, my_width : 2 * my_width].astype(BF)
    value = (joined[:, 2 * my_width :] + my_part(value_bias)).astype(BF)

    attended_mine, logs = attend(query, key, value, mask, block)
    attended = own_half(
        lax.all_gather(attended_mine, "leaf", axis=1, tiled=True, axis_index_groups=pairs)
    )

    rows_mine = own_half(tokens).astype(F32)
    hidden, normed_first, inv_first = layer_norm(
        rows_mine + dot_nn(attended, out_weight) + out_bias, first_gain, first_shift
    )
    hidden_low = hidden.astype(BF)
    active, slope = gelu_parts(dot_nn(hidden_low, up_weight) + up_bias)
    active = active.astype(BF)
    output, normed_second, inv_second = layer_norm(
        hidden + dot_nn(active, down_weight) + down_bias, second_gain, second_shift
    )
    layer_out = own_tokens(output.astype(BF))

    delta_second, second_gain_grad, second_shift_grad = norm_backward(
        upstream, normed_second, inv_second, second_gain
    )
    delta_branch = delta_second.astype(BF)
    down_weight_grad = dot_tn(active, delta_branch)
    down_bias_grad = jnp.sum(delta_branch.astype(F32), axis=0)
    delta_up = (dot_nt(delta_branch, down_weight) * slope).astype(BF)
    up_weight_grad = dot_tn(hidden_low, delta_up)
    up_bias_grad = jnp.sum(delta_up.astype(F32), axis=0)
    delta_first, first_gain_grad, first_shift_grad = norm_backward(
        delta_second + dot_nt(delta_up, up_weight), normed_first, inv_first, first_gain
    )
    delta_proj = delta_first.astype(BF)
    out_weight_grad = dot_tn(attended, delta_proj)
    out_bias_grad = jnp.sum(delta_proj.astype(F32), axis=0)
    delta_attended = lax.all_gather(
        dot_nt(delta_proj, out_weight).astype(BF),
        "leaf",
        axis=0,
        tiled=True,
        axis_index_groups=pairs,
    )
    delta_attended = lax.dynamic_slice_in_dim(delta_attended, core * my_width, my_width, 1)

    dquery, dkey, dvalue, dmask = attend_back(
        query, key, value, mask, attended_mine, logs, delta_attended, block, score_scale
    )
    djoined = jnp.concatenate([dquery, dkey, dvalue], axis=1)
    joined_grad = dot_tn(tokens, djoined)
    query_bias_grad = jnp.sum(dquery.astype(F32), axis=0)
    value_bias_grad = jnp.sum(dvalue.astype(F32), axis=0)
    dtokens = lax.psum_scatter(
        dot_nt(djoined, weight3).astype(BF),
        "leaf",
        scatter_dimension=0,
        tiled=True,
        axis_index_groups=pairs,
    )
    tokens_grad = own_tokens((delta_first + dtokens.astype(F32)).astype(BF))

    def placed(part, whole_size, start, axis):
        shape = list(part.shape)
        shape[axis] = whole_size
        return lax.dynamic_update_slice_in_dim(jnp.zeros(shape, part.dtype), part, start, axis)

    def owned(grad, axis=0):
        return lax.psum_scatter(
            grad.astype(BF), "fsdp", scatter_dimension=axis, tiled=True
        )

    joined_part = owned(joined_grad)
    joined_full = jnp.zeros((joined_part.shape[0], 3 * width), BF)
    for i in range(3):
        joined_full = lax.dynamic_update_slice_in_dim(
            joined_full,
            joined_part[:, i * my_width : (i + 1) * my_width],
            i * width + core * my_width,
            1,
        )
    matrices = (
        joined_full,
        owned(out_weight_grad),
        owned(up_weight_grad),
        owned(down_weight_grad),
        placed(owned(dmask, 1), heads, core * my_heads, 0),
    )
    joined_total, out_total, up_total, down_total, mask_total = [
        lax.psum(matrix, "leaf").astype(F32) for matrix in matrices
    ]
    small = (
        placed(query_bias_grad, width, core * my_width, 0),
        placed(value_bias_grad, width, core * my_width, 0),
        out_bias_grad,
        first_gain_grad,
        first_shift_grad,
        up_bias_grad,
        down_bias_grad,
        second_gain_grad,
        second_shift_grad,
    )
    fsdp_count = lax.axis_size("fsdp")
    packed_grads = jnp.concatenate([s.reshape(fsdp_count, -1) for s in small], axis=1)
    packed_grads = lax.psum(
        lax.psum_scatter(packed_grads, "fsdp", scatter_dimension=0, tiled=True), "leaf"
    )[0]
    vector_grads = []
    first = 0
    for s in small:
        size = s.shape[0] // fsdp_count
        vector_grads.append(packed_grads[first : first + size])
        first += size
    mask_gradient = mask_total * softened * (1.0 - softened) / softening_scale[:, None, None]
    return (
        layer_out,
        tokens_grad,
        joined_total,
        vector_grads[0],
        vector_grads[1],
        out_total,
        vector_grads[2],
        vector_grads[3],
        vector_grads[4],
        up_total,
        vector_grads[5],
        down_total,
        vector_grads[6],
        vector_grads[7],
        vector_grads[8],
        mask_gradient,
    )


def fast_device(
    layer_entry_matrix,
    loss_sensitivity,
    ancestor_block_table,
    gate_trained_scores,
    gate_random_jitter,
    softening_scale,
    triple_projection_matrix,
    asker_constant_vector,
    content_constant_vector,
    mixer_exit_matrix,
    mixer_exit_constant,
    mixer_scaling_factor,
    mixer_recentering_term,
    dense_expand_matrix,
    dense_expand_constant,
    dense_contract_matrix,
    dense_contract_constant,
    dense_scaling_factor,
    dense_recentering_term,
):
    micro, _, own_rows, width = layer_entry_matrix.shape
    blocks = ancestor_block_table.shape[2]
    rows = own_rows * 4
    block = rows // blocks
    heads, strip, span = gate_trained_scores.shape
    leaf = lax.axis_index("leaf")
    tree, core = leaf // CORES, leaf % CORES
    mine = width // CORES
    half = rows // CORES
    shard = width // 8
    hidden_shard = dense_contract_matrix.shape[0]
    score_scale = 1.0 / math.sqrt(width // heads)

    table = lax.dynamic_index_in_dim(ancestor_block_table[:, 0], tree, 0, keepdims=False)
    order, place = tree_order(table)
    softened = jax.nn.sigmoid(
        (gate_trained_scores + gate_random_jitter) / softening_scale[:, None, None]
    )
    relaxed = softened.astype(BF).reshape(heads, 2, strip // 2, span)
    vectors = [
        asker_constant_vector,
        content_constant_vector,
        mixer_exit_constant,
        mixer_scaling_factor,
        mixer_recentering_term,
        dense_contract_constant,
        dense_scaling_factor,
        dense_recentering_term,
        dense_expand_constant,
    ]
    sizes = [vector.shape[0] for vector in vectors]
    used = sum(sizes)
    flat = jnp.pad(jnp.concatenate(vectors), (0, 2048 - used)).reshape(16, 128)

    tree_tokens, joined_weight, first_masks, packed = enter(
        layer_entry_matrix[:, 0], triple_projection_matrix.reshape(2, shard // 2, 3 * width), relaxed, flat
    )
    packed = packed.reshape(8, 2048).astype(F32)
    places = [sum(sizes[:i]) for i in range(len(sizes))]
    (
        query_bias,
        value_bias,
        out_bias,
        first_gain,
        first_shift,
        down_bias,
        second_gain,
        second_shift,
        up_bias,
    ) = [packed[:, a : a + n].reshape(1, -1) for a, n in zip(places, sizes)]

    def my_part(vector):
        return lax.dynamic_slice_in_dim(vector, core * mine, mine, 1)

    joined_weight = joined_weight.reshape(width, 3 * mine)
    tokens, query, key, value = join(
        order, tree_tokens, joined_weight, my_part(query_bias), my_part(value_bias)
    )
    attended_mine, logs, attended, mask, out_weight, up_weight, down_weight, tree_upstream = (
        attend_wide(
            query,
            key,
            value,
            first_masks,
            relaxed,
            mixer_exit_matrix.reshape(2, shard // 2, width),
            dense_expand_matrix.reshape(2, shard // 2, -1),
            dense_contract_matrix.reshape(4, 2, hidden_shard // 8, width),
            loss_sensitivity[:, 0],
            block,
        )
    )
    mask = mask.reshape(heads // CORES, span, span)
    out_weight = out_weight.reshape(width, width)
    up_weight = up_weight.reshape(width, -1)
    down_weight = down_weight.reshape(-1, width)
    half_order = lax.dynamic_slice_in_dim(order, core * (blocks // 2), blocks // 2, 0)
    upstream = pick(half_order, tree_upstream, block).reshape(half, width).astype(F32)
    tokens = tokens.reshape(rows, width)
    rows_mine = lax.dynamic_slice_in_dim(tokens, core * half, half, 0).astype(F32)

    hidden, normed_first, inv_first = layer_norm(
        rows_mine + dot_nn(attended, out_weight) + out_bias, first_gain, first_shift
    )
    hidden_low = hidden.astype(BF)
    active, slope = gelu_parts(dot_nn(hidden_low, up_weight) + up_bias)
    active = active.astype(BF)
    output, normed_second, inv_second = layer_norm(
        hidden + dot_nn(active, down_weight) + down_bias, second_gain, second_shift
    )
    delta_second, second_gain_grad, second_shift_grad = norm_backward(
        upstream, normed_second, inv_second, second_gain
    )
    delta_branch = delta_second.astype(BF)
    down_weight_grad = dot_tn(active, delta_branch).astype(BF)
    down_bias_grad = jnp.sum(delta_branch.astype(F32), axis=0)
    delta_up = (dot_nt(delta_branch, down_weight) * slope).astype(BF)
    up_weight_grad = dot_tn(hidden_low, delta_up).astype(BF)
    up_bias_grad = jnp.sum(delta_up.astype(F32), axis=0)
    delta_first, first_gain_grad, first_shift_grad = norm_backward(
        delta_second + dot_nt(delta_up, up_weight), normed_first, inv_first, first_gain
    )
    delta_proj = delta_first.astype(BF)
    out_weight_grad = dot_tn(attended, delta_proj).astype(BF)
    out_bias_grad = jnp.sum(delta_proj.astype(F32), axis=0)
    delta_attended = dot_nt(delta_proj, out_weight).astype(BF)

    (
        dquery,
        dkey,
        dvalue,
        last_masks,
        out_total,
        up_total,
        down_total,
        mask_total,
        layer_out,
    ) = attend_back_wide(
        query,
        key,
        value,
        mask,
        attended_mine,
        logs,
        delta_attended,
        output.astype(BF).reshape(blocks // 2, block, width),
        place,
        out_weight_grad.reshape(LINE, 2, 2, shard // 2, width),
        up_weight_grad.reshape(LINE, 2, 2, shard // 2, -1),
        down_weight_grad.reshape(LINE, 2, 4, 2, hidden_shard // 8, width),
        block,
        score_scale,
    )
    djoined = jnp.concatenate([dquery, dkey, dvalue], axis=1)
    joined_grad = dot_tn(tokens, djoined).astype(BF)
    query_bias_grad = jnp.sum(dquery.astype(F32), axis=0)
    value_bias_grad = jnp.sum(dvalue.astype(F32), axis=0)
    rest = lax.dynamic_update_slice_in_dim(
        jnp.zeros((rows, width), F32), delta_first, core * half, 0
    )
    dtokens = (dot_nt(djoined, joined_weight) + rest).astype(BF)

    def placed(part):
        return lax.dynamic_update_slice_in_dim(jnp.zeros((width,), F32), part, core * mine, 0)

    small = (
        placed(query_bias_grad),
        placed(value_bias_grad),
        out_bias_grad,
        first_gain_grad,
        first_shift_grad,
        down_bias_grad,
        second_gain_grad,
        second_shift_grad,
        up_bias_grad,
    )
    small = jnp.concatenate([s.reshape(8, -1) for s in small], axis=1)
    small = jnp.pad(small, ((0, 0), (0, 2048 - used))).reshape(LINE, 2, 16, 128)
    mask_last, joined_total, tokens_grad, small = leave(
        dtokens.reshape(blocks, block, width),
        place,
        last_masks,
        joined_grad.reshape(LINE, 2, 2, shard // 2, 3 * mine),
        small,
        block,
    )
    small = small.reshape(2048)
    vector_grads = [small[a : a + n] for a, n in zip(places, sizes)]
    mask_total = jnp.concatenate([mask_total, mask_last], axis=1).reshape(heads, strip, span)
    mask_gradient = (
        mask_total.astype(F32) * softened * (1.0 - softened) / softening_scale[:, None, None]
    )
    return (
        layer_out[:, None],
        tokens_grad[:, None],
        joined_total.reshape(shard, 3 * width).astype(F32),
        vector_grads[0],
        vector_grads[1],
        out_total.reshape(shard, width).astype(F32),
        vector_grads[2],
        vector_grads[3],
        vector_grads[4],
        up_total.reshape(shard, -1).astype(F32),
        vector_grads[8],
        down_total.reshape(hidden_shard, width).astype(F32),
        vector_grads[5],
        vector_grads[6],
        vector_grads[7],
        mask_gradient,
    )


def solution(mesh):
    placed = (
        P(None, "fsdp", "leaf", None),
        P(None, "fsdp", "leaf", None),
        P(None, "fsdp", None),
        P(None, "fsdp", None),
        P(None, "fsdp", None),
        P(),
        P("fsdp", None),
        P("fsdp"),
        P("fsdp"),
        P("fsdp", None),
        P("fsdp"),
        P("fsdp"),
        P("fsdp"),
        P("fsdp", None),
        P("fsdp"),
        P("fsdp", None),
        P("fsdp"),
        P("fsdp"),
        P("fsdp"),
    )
    return jax.shard_map(
        fast_device if mesh.shape["fsdp"] == 8 and mesh.shape["leaf"] == 4 else per_device,
        mesh=mesh,
        in_specs=placed,
        out_specs=(
            P(None, "fsdp", "leaf", None),
            P(None, "fsdp", "leaf", None),
            P("fsdp", None),
            P("fsdp"),
            P("fsdp"),
            P("fsdp", None),
            P("fsdp"),
            P("fsdp"),
            P("fsdp"),
            P("fsdp", None),
            P("fsdp"),
            P("fsdp", None),
            P("fsdp"),
            P("fsdp"),
            P("fsdp"),
            P(None, "fsdp", None),
        ),
        check_vma=False,
    )
```

```python
import functools
import math

import jax
import jax.numpy as jnp
from jax import lax
from jax.experimental import pallas as pl
from jax.experimental.pallas import tpu as pltpu
from jax.sharding import PartitionSpec as P

EPSILON = 1e-05
F32 = jnp.float32
BF = jnp.bfloat16
TRUNK = 4
GROUPS = 4
CORES = 2
LOW_HALF = 64


def layer_norm(values, gain_vec, shift_vec):
    average = jnp.mean(values, axis=-1, keepdims=True)
    centred = values - average
    inv_scale = lax.rsqrt(jnp.mean(centred * centred, axis=-1, keepdims=True) + EPSILON)
    normed = centred * inv_scale
    return (normed * gain_vec + shift_vec, normed, inv_scale)


def norm_backward(upstream, normed, inv_scale, gain_vec):
    scaled = upstream * gain_vec
    inner_term = (
        scaled
        - jnp.mean(scaled, axis=-1, keepdims=True)
        - normed * jnp.mean(scaled * normed, axis=-1, keepdims=True)
    )
    return (inv_scale * inner_term, jnp.sum(upstream * normed, axis=0), jnp.sum(upstream, axis=0))


def gelu_parts(values):
    cdf = 0.5 * (1.0 + lax.erf(values / math.sqrt(2.0)))
    density = jnp.exp(-0.5 * values * values) / math.sqrt(2.0 * math.pi)
    return (values * cdf, cdf + values * density)


def dot_nn(left, right):
    return jnp.dot(left, right, preferred_element_type=F32)


def dot_nt(left, right):
    return lax.dot_general(left, right, (((1,), (1,)), ((), ())), preferred_element_type=F32)


def dot_tn(left, right):
    return lax.dot_general(left, right, (((0,), (0,)), ((), ())), preferred_element_type=F32)


def tree_order(parent):
    count = parent.shape[0]
    ids = jnp.arange(count, dtype=jnp.int32)
    up = (parent[:, None] == ids[None, :]) & (ids[:, None] != ids[None, :])
    up = up.astype(F32)
    reach = up
    power = up
    for _ in range(TRUNK + 1):
        power = jnp.sum(power[:, :, None] * up[None, :, :], axis=1)
        reach = reach + power
    depth = jnp.sum(reach, axis=1)
    before = (ids[None, :] < ids[:, None]).astype(F32)
    branch = (depth == TRUNK).astype(F32)
    rank = jnp.sum(before * branch[None, :], axis=1)
    own_rank = jnp.where(depth == TRUNK, rank, jnp.sum(up * rank[None, :], axis=1))
    siblings = jnp.sum(up[:, None, :] * up[None, :, :], axis=2) * before
    second = jnp.sum(siblings, axis=1)
    within = jnp.where(depth == TRUNK, 1.0, 2.0 * second)
    place = jnp.where(depth < TRUNK, depth, TRUNK + 3.0 * own_rank + within).astype(jnp.int32)
    order = jnp.sum((place[:, None] == ids[None, :]) * ids[:, None], axis=0).astype(jnp.int32)
    return (order, place)


def low_lanes():
    return lax.broadcasted_iota(jnp.int32, (1, 2 * LOW_HALF), 1) < LOW_HALF


def one_head(pair, which):
    keep = low_lanes() if which == 0 else jnp.logical_not(low_lanes())
    return jnp.where(keep, pair, jnp.zeros_like(pair))


def group_columns(row, block):
    return ((0, 2 * block, (1, 0)), (0, 3 * block, (1, 0, 1)), (block, 2 * block, (0, 1)))[row]


def mask_columns(mask_rows, tiles, block):
    return jnp.concatenate([mask_rows[:, t * block : (t + 1) * block] for t in tiles], axis=1)


def attend_kernel(block, query_ref, key_ref, value_ref, mask_ref, out_ref, log_ref):
    trunk = TRUNK * block
    wide = 3 * block
    low = low_lanes()

    def soften(parts, masks, values):
        top = parts[0].max(axis=1, keepdims=True)
        for part in parts[1:]:
            top = jnp.maximum(top, part.max(axis=1, keepdims=True))
        total = 0.0
        out = 0.0
        for part, mask, value in zip(parts, masks, values):
            weight = jnp.exp(part - top)
            total = total + weight.sum(axis=1, keepdims=True)
            out = out + dot_nn((weight * mask.astype(F32)).astype(BF), value)
        return (out * (1.0 / total), top + jnp.log(total))

    def emit(rows, results):
        count = results[0][1].shape[0]
        out_ref[rows, :] = jnp.where(low, results[0][0], results[1][0]).astype(BF)
        logs = [jnp.broadcast_to(result[1], (count, 2 * LOW_HALF)) for result in results]
        log_ref[rows, :] = jnp.where(low, logs[0], logs[1])

    def trunk_rows(index, carry):
        rows = pl.ds(pl.multiple_of(index * block, block), block)
        query = query_ref[rows, :]
        results = []
        for which in range(2):
            mask_rows = mask_ref[which, rows, :]
            columns = [(0, trunk, mask_rows)]
            side = mask_columns(mask_rows, (1, 0, 1), block)
            columns += [(trunk + wide * g, wide, side) for g in range(GROUPS)]
            head = one_head(query, which)
            parts = [dot_nt(head, key_ref[c : c + w, :]) for c, w, _ in columns]
            values = [value_ref[c : c + w, :] for c, w, _ in columns]
            results.append(soften(parts, [column[2] for column in columns], values))
        emit(rows, results)
        return carry

    lax.fori_loop(0, TRUNK, trunk_rows, 0)

    def group_rows(group, carry):
        base = pl.multiple_of(trunk + wide * group, block)
        for row in range(3):
            rows = pl.ds(pl.multiple_of(base + block * row, block), block)
            query = query_ref[rows, :]
            tile = 0 if row == 1 else 1
            start, width, tiles = group_columns(row, block)
            columns = pl.ds(pl.multiple_of(base + start, block), width)
            results = []
            for which in range(2):
                mask_rows = mask_ref[which, tile * block : (tile + 1) * block, :]
                head = one_head(query, which)
                parts = [dot_nt(head, key_ref[0:trunk, :]), dot_nt(head, key_ref[columns, :])]
                masks = [mask_rows, mask_columns(mask_rows, tiles, block)]
                values = [value_ref[0:trunk, :], value_ref[columns, :]]
                results.append(soften(parts, masks, values))
            emit(rows, results)
        return carry

    lax.fori_loop(0, GROUPS, group_rows, 0)


def attend(query, key, value, mask, block):
    rows, width = query.shape
    pairs = width // (2 * LOW_HALF)
    span = mask.shape[1]
    spec = pl.BlockSpec((rows, 2 * LOW_HALF), lambda p: (0, p))
    return pl.pallas_call(
        functools.partial(attend_kernel, block),
        grid=(pairs,),
        name="attend",
        in_specs=[spec, spec, spec, pl.BlockSpec((2, span, span), lambda p: (p, 0, 0))],
        out_specs=[spec, spec],
        out_shape=[
            jax.ShapeDtypeStruct((rows, width), BF),
            jax.ShapeDtypeStruct((rows, width), F32),
        ],
        compiler_params=pltpu.CompilerParams(vmem_limit_bytes=48 << 20),
    )(query, key, value, mask)


def attend_back_kernel(
    block,
    scale,
    query_ref,
    key_ref,
    value_ref,
    mask_ref,
    out_ref,
    log_ref,
    delta_ref,
    dquery_ref,
    dkey_ref,
    dvalue_ref,
    dmask_ref,
    key_sum,
    value_sum,
    query_turned,
    delta_turned,
):
    trunk = TRUNK * block
    wide = 3 * block
    low = low_lanes()
    key_sum[...] = jnp.zeros_like(key_sum)
    value_sum[...] = jnp.zeros_like(value_sum)
    dmask_ref[...] = jnp.zeros_like(dmask_ref)
    query_turned[...] = query_ref[...].astype(F32).T.astype(BF)
    delta_turned[...] = delta_ref[...].astype(F32).T.astype(BF)

    def work(rows, mask_place, columns):
        query = query_ref[rows, :]
        delta = delta_ref[rows, :]
        product = delta.astype(F32) * out_ref[rows, :].astype(F32)
        logs = log_ref[rows, :]
        dqueries = []
        for which in range(2):
            first = LOW_HALF * which
            lanes = slice(first, first + LOW_HALF)
            query_head = one_head(query, which)
            delta_head = one_head(delta, which)
            log = logs[:, first : first + 1]
            row_term = jnp.sum(product[:, lanes], axis=1, keepdims=True)
            mask_rows = mask_ref[which, mask_place, :]
            dquery = 0.0
            for place, tiles in columns:
                key = key_ref[place, :]
                value = value_ref[place, :]
                probs = jnp.exp(dot_nt(query_head, key) - log)
                pair = dot_nt(delta_head, value) * probs
                mask = mask_rows if tiles is None else mask_columns(mask_rows, tiles, block)
                mask = mask.astype(F32)
                if tiles is None:
                    dmask_ref[which, mask_place, :] += pair
                else:
                    for tile in sorted(set(tiles)):
                        dmask_ref[which, mask_place, tile * block : (tile + 1) * block] += sum(
                            pair[:, a * block : (a + 1) * block]
                            for a, t in enumerate(tiles)
                            if t == tile
                        )
                dscores = (pair * mask - probs * row_term).astype(BF)
                weights = (probs * mask).astype(BF)
                dquery = dquery + dot_nn(dscores, key)
                key_sum[lanes, place] += dot_nn(query_turned[lanes, rows], dscores)
                value_sum[lanes, place] += dot_nn(delta_turned[lanes, rows], weights)
            dqueries.append(dquery)
        dquery_ref[rows, :] = (jnp.where(low, dqueries[0], dqueries[1]) * scale).astype(BF)

    def trunk_rows(index, carry):
        rows = pl.ds(pl.multiple_of(index * block, block), block)
        columns = [(pl.ds(0, trunk), None)]
        columns += [(pl.ds(trunk + wide * g, wide), (1, 0, 1)) for g in range(GROUPS)]
        work(rows, rows, columns)
        return carry

    lax.fori_loop(0, TRUNK, trunk_rows, 0)

    def group_rows(group, carry):
        base = pl.multiple_of(trunk + wide * group, block)
        for row in range(3):
            rows = pl.ds(pl.multiple_of(base + block * row, block), block)
            tile = 0 if row == 1 else 1
            start, width, tiles = group_columns(row, block)
            near = pl.ds(pl.multiple_of(base + start, block), width)
            work(rows, pl.ds(tile * block, block), [(pl.ds(0, trunk), None), (near, tiles)])
        return carry

    lax.fori_loop(0, GROUPS, group_rows, 0)
    dkey_ref[...] = key_sum[...].T.astype(BF)
    dvalue_ref[...] = value_sum[...].T.astype(BF)


def attend_back(query, key, value, mask, out, logs, delta, block, scale):
    rows, width = query.shape
    pair_width = 2 * LOW_HALF
    pairs = width // pair_width
    span = mask.shape[1]
    spec = pl.BlockSpec((rows, pair_width), lambda p: (0, p))
    mask_spec = pl.BlockSpec((2, span, span), lambda p: (p, 0, 0))
    return pl.pallas_call(
        functools.partial(attend_back_kernel, block, scale),
        grid=(pairs,),
        name="attend_back",
        in_specs=[spec, spec, spec, mask_spec, spec, spec, spec],
        out_specs=[spec, spec, spec, mask_spec],
        out_shape=[jax.ShapeDtypeStruct((rows, width), BF)] * 3
        + [jax.ShapeDtypeStruct(mask.shape, F32)],
        scratch_shapes=[
            pltpu.VMEM((pair_width, rows), F32),
            pltpu.VMEM((pair_width, rows), F32),
            pltpu.VMEM((pair_width, rows), BF),
            pltpu.VMEM((pair_width, rows), BF),
        ],
        compiler_params=pltpu.CompilerParams(vmem_limit_bytes=48 << 20),
    )(query, key, value, mask, out, logs, delta)


def reorder_kernel(order_ref, source_ref, target_ref):
    target_ref[...] = source_ref[...]


def reorder(tokens, order):
    count, block, width = tokens.shape
    return pl.pallas_call(
        reorder_kernel,
        name="reorder",
        grid_spec=pltpu.PrefetchScalarGridSpec(
            num_scalar_prefetch=1,
            grid=(count,),
            in_specs=[pl.BlockSpec((1, block, width), lambda i, order_ref: (order_ref[i], 0, 0))],
            out_specs=pl.BlockSpec((1, block, width), lambda i, order_ref: (i, 0, 0)),
        ),
        out_shape=jax.ShapeDtypeStruct(tokens.shape, tokens.dtype),
    )(order, tokens)


MESH = pl.DeviceIdType.MESH
ANY = pl.BlockSpec(memory_space=pl.ANY)
VMEM = pl.BlockSpec(memory_space=pltpu.VMEM)
SMEM = pl.BlockSpec(memory_space=pltpu.SMEM)
VMEM_LIMIT = 62 << 20
LINE = 4
ALL = slice(None)


class Net:
    def __init__(self, send, recv, local):
        leaf, shard = lax.axis_index("leaf"), lax.axis_index("fsdp")
        self.leaf, self.shard = leaf, shard
        self.x, self.c = leaf // 2, leaf % 2
        self.z, self.y = shard // 2, shard % 2
        self.send, self.recv, self.local = send, recv, local

    def near(self, which):
        x, c, y, z = self.x, self.c, self.y, self.z
        if which == "x":
            x = 1 - x
        elif which == "c":
            c = 1 - c
        elif which == "xc":
            x, c = 1 - x, 1 - c
        elif which == "y":
            y = 1 - y
        else:
            z = (z + which) % LINE
        return (x * 2 + c, z * 2 + y)

    def greet(self, peers):
        barrier = pltpu.get_barrier_semaphore()
        for peer in peers:
            pl.semaphore_signal(barrier, inc=1, device_id=self.near(peer), device_id_type=MESH)
        pl.semaphore_wait(barrier, len(peers))

    def remote(self, row, slot, source, target, peer):
        return pltpu.make_async_remote_copy(
            src_ref=source,
            dst_ref=target,
            send_sem=self.send.at[row, slot],
            recv_sem=self.recv.at[row, slot],
            device_id=self.near(peer),
            device_id_type=MESH,
        )

    def stay(self, row, source, target):
        return pltpu.make_async_copy(source, target, self.local.at[row])


class Gather:
    def __init__(self, net, row, own, whole, share, split=2):
        self.net, self.row, self.own, self.whole, self.share = net, row, own, whole, share
        self.split = split

    def copy(self, slot):
        net, whole = self.net, self.whole
        x, y, z = net.x, net.y, net.z
        if slot < 3:
            return net.remote(self.row, slot, self.own(x), whole(z, y, x), slot + 1)
        if slot < 6:
            piece = whole((z + LINE - (slot - 2)) % LINE, y, x)
            return net.remote(self.row, slot, piece, piece, "x")
        if slot == 6:
            piece, peer = whole(ALL, y, x), "y"
        elif slot == 7:
            piece, peer = whole(slice(0, self.split), 1 - y, x), "x"
        elif slot == 8:
            piece, peer = whole(slice(self.split, 4), y, 1 - x), "y"
        else:
            piece, peer = whole(ALL, ALL, ALL), "c"
        return net.remote(self.row, slot, piece, piece, peer)

    def home(self):
        return self.net.stay(self.row, self.own(ALL), self.whole(self.net.z, self.net.y, ALL))

    def step(self, number):
        if number == 0:
            self.home().start()
            for slot in range(3):
                self.copy(slot).start()
        elif number == 1:
            self.home().wait()
            for slot in range(3):
                self.copy(slot).wait_recv()
            for slot in range(3, 7):
                self.copy(slot).start()
        elif number == 2:
            for slot in range(3, 7):
                self.copy(slot).wait_recv()
            for slot in (7, 8):
                self.copy(slot).start()
        elif number == 3:
            for slot in (7, 8):
                self.copy(slot).wait_recv()
            if self.share:
                self.copy(9).start()
        elif number == 4:
            if self.share:
                self.copy(9).wait_recv()

    def finish(self):
        for slot in range(10 if self.share else 9):
            self.copy(slot).wait_send()


class Scatter:
    def __init__(self, net, row, load, part, twin, twin_load, first, second, third, final):
        self.net, self.row, self.load, self.part = net, row, load, part
        self.twin, self.twin_load = twin, twin_load
        self.first, self.second, self.third, self.final = first, second, third, final

    def copy(self, slot):
        net, part = self.net, self.part
        x, y, z, c = net.x, net.y, net.z, net.c
        if slot == 0:
            return net.remote(self.row, slot, self.twin_load, self.twin, "c")
        if slot == 1:
            return net.remote(self.row, slot, part.at[0:1, 1 - y, 1 - x], self.first.at[0:1], "x")
        if slot == 2:
            return net.remote(self.row, slot, part.at[1:4, 1 - y, 1 - x], self.first.at[1:4], "y")
        if slot == 3:
            return net.remote(self.row, slot, part.at[:, y, 1 - x], self.second.at[0], "x")
        if slot == 4:
            return net.remote(self.row, slot, part.at[:, 1 - y, x], self.second.at[1], "y")
        if slot < 8:
            step = slot - 4
            piece = part.at[(z + step) % LINE, y, x]
            return net.remote(self.row, slot, piece, self.third.at[step - 1], step)
        if slot < 10:
            return net.remote(self.row, slot, part.at[z, y, x], self.final(x, c), "xc"[slot - 8])
        piece = self.final(1 - x, c)
        return net.remote(self.row, slot, piece, piece, "c")

    def home(self):
        return self.net.stay(self.row, self.load, self.part)

    def keep(self):
        net = self.net
        piece = self.part.at[net.z, net.y, net.x]
        return net.stay(self.row, piece, self.final(net.x, net.c))

    def step(self, number):
        net, part = self.net, self.part
        x, y, z = net.x, net.y, net.z
        if number == 0:
            if self.load is not None:
                self.home().start()
            if self.twin is not None:
                self.copy(0).start()
        elif number == 1:
            if self.load is not None:
                self.home().wait()
            if self.twin is not None:
                self.copy(0).wait_recv()
                for a in range(LINE):
                    part[a] = part[a] + self.twin[a]
            self.copy(1).start()
            self.copy(2).start()
        elif number == 2:
            self.copy(1).wait_recv()
            part[0, 1 - y, x] = part[0, 1 - y, x] + self.first[0]
            self.copy(2).wait_recv()
            part[1:4, y, 1 - x] = part[1:4, y, 1 - x] + self.first[1:4]
            self.copy(3).start()
            self.copy(4).start()
        elif number == 3:
            self.copy(3).wait_recv()
            self.copy(4).wait_recv()
            mine = part[:, y, x].astype(F32) + self.second[0].astype(F32)
            part[:, y, x] = (mine + self.second[1].astype(F32)).astype(BF)
            for slot in (5, 6, 7):
                self.copy(slot).start()
        elif number == 4:
            total = part[z, y, x].astype(F32)
            for slot in (5, 6, 7):
                self.copy(slot).wait_recv()
                total = total + self.third[slot - 5].astype(F32)
            part[z, y, x] = total.astype(BF)
            for slot in (8, 9):
                self.copy(slot).start()
            self.keep().start()
        elif number == 5:
            self.keep().wait()
            self.copy(8).wait_recv()
            self.copy(10).start()
        elif number == 6:
            for slot in (9, 10):
                self.copy(slot).wait_recv()

    def finish(self):
        for slot in range(0 if self.twin is not None else 1, 11):
            self.copy(slot).wait_send()


def copy_semaphores(rows, slots):
    return [
        pltpu.SemaphoreType.DMA((rows, slots)),
        pltpu.SemaphoreType.DMA((rows, slots)),
        pltpu.SemaphoreType.DMA((rows,)),
    ]


def run_plan(plan, slot, total):
    for number in range(total):
        steps = [entry for entry in plan if int(entry[0]) == number]
        if steps:

            @pl.when(slot == number)
            def _(steps=steps):
                for _, chunk, step in steps:
                    chunk.step(step)


def run_rest(plan, total):
    for time, chunk, step in plan:
        if time >= total:
            chunk.step(step)


def pick_kernel(order_ref, low_ref, high_ref, out_ref, sems):
    count = low_ref.shape[0]
    for i in range(out_ref.shape[0]):
        at = order_ref[i]

        @pl.when(at < count)
        def _(i=i, at=at):
            pltpu.make_async_copy(low_ref.at[at], out_ref.at[i], sems.at[i]).start()

        @pl.when(at >= count)
        def _(i=i, at=at):
            pltpu.make_async_copy(high_ref.at[at - count], out_ref.at[i], sems.at[i]).start()

    for i in range(out_ref.shape[0]):
        pltpu.make_async_copy(low_ref.at[0], out_ref.at[i], sems.at[i]).wait()


def pick(order, low, high):
    count = order.shape[0]
    return pl.pallas_call(
        pick_kernel,
        name="pick",
        in_specs=[SMEM, ANY, ANY],
        out_specs=VMEM,
        out_shape=jax.ShapeDtypeStruct((count,) + low.shape[1:], low.dtype),
        scratch_shapes=[pltpu.SemaphoreType.DMA((count,))],
        compiler_params=pltpu.CompilerParams(vmem_limit_bytes=VMEM_LIMIT),
    )(order, low, high)


class Sharing:
    def __init__(self, net, row, own, tree, stage=None):
        self.net, self.row, self.own, self.tree, self.stage = net, row, own, tree, stage

    def copy(self, slot):
        net, own, tree = self.net, self.own, self.tree
        count = own.shape[1]
        half = count // 2
        part = pl.ds((slot % 2) * half, half)
        place = tree.at[pl.ds(net.leaf * count + (slot % 2) * half, half)]
        if slot < 2:
            return net.remote(self.row, slot, own.at[1 - net.x, part], place, "x")
        if slot < 4:
            return net.remote(self.row, slot, own.at[net.x, part], place, "c")
        place = tree.at[pl.ds((net.leaf + 2) % 4 * count + (slot % 2) * half, half)]
        return net.remote(self.row, slot, place, place, "c")

    def home(self):
        count = self.own.shape[1]
        source = self.own.at[self.net.x] if self.stage is None else self.stage
        return self.net.stay(self.row, source, self.tree.at[pl.ds(self.net.leaf * count, count)])

    def load(self):
        return self.net.stay(self.row + 1, self.own.at[self.net.x], self.stage)

    def step(self, number):
        if number == 0:
            for slot in range(4):
                self.copy(slot).start()
            if self.stage is not None:
                self.load().wait()
            self.home().start()
        elif number < 3:
            self.copy(number - 1).wait_recv()
            self.copy(number + 3).start()
        elif number == 3:
            for slot in (2, 3, 4, 5):
                self.copy(slot).wait_recv()
            self.home().wait()

    def finish(self):
        for slot in range(6):
            self.copy(slot).wait_send()


class Flush:
    def __init__(self, net, row, source, target):
        self.move = lambda: net.stay(row, source, target)

    def step(self, number):
        self.move().start()

    def finish(self):
        self.move().wait()


class WideGather(Gather):
    def copy(self, slot):
        net, whole = self.net, self.whole
        if slot < 3:
            piece = whole(net.z, net.y, ALL)
            return net.remote(self.row, slot, self.own(ALL), piece, slot + 1)
        if slot == 3:
            piece, peer = whole(ALL, net.y, ALL), "y"
        else:
            piece, peer = whole(ALL, ALL, ALL), "c"
        return net.remote(self.row, slot, piece, piece, peer)

    def step(self, number):
        if number == 0:
            self.home().start()
            for slot in range(3):
                self.copy(slot).start()
        elif number == 1:
            self.home().wait()
            for slot in range(3):
                self.copy(slot).wait_recv()
            self.copy(3).start()
        elif number == 2:
            self.copy(3).wait_recv()
            if self.share:
                self.copy(4).start()
        elif number == 4:
            if self.share:
                self.copy(4).wait_recv()

    def finish(self):
        for slot in range(5 if self.share else 4):
            self.copy(slot).wait_send()


class FarGather(Gather):
    def __init__(self, net, row, own, whole, share, split, stage, spare):
        super().__init__(net, row, own, whole, share, split)
        self.stage, self.spare = stage, spare

    def load(self):
        return self.net.stay(self.spare, self.own(ALL), self.stage)

    def home(self):
        return self.net.stay(self.row, self.stage, self.whole(self.net.z, self.net.y, ALL))

    def step(self, number):
        if number == 0:
            self.load().wait()
        super().step(number)


FRONT = dict(
    pace=4.9,
    lead=5.0,
    lag1=7.0,
    lag2=8.0,
    lag3=8.0,
    lag4=6.0,
    origin=34.0,
    join=1.0,
    attend=1.85,
    norm=0.7,
    rise=1.0,
    splits=(1, 2),
    wide=(),
    upstream=(60.0, 72.0, 80.0, 90.0),
)


def front_kernel(
    block,
    order_ref,
    entry_ref,
    upstream_ref,
    joined_shard,
    relaxed_ref,
    out_shard,
    up_shard,
    down_shard,
    vectors_ref,
    tokens_out,
    joined_out,
    query_out,
    key_out,
    value_out,
    mask_out,
    attended_out,
    log_out,
    whole_out,
    out_out,
    up_out,
    down_out,
    tree_out,
    normed_out,
    inv_out,
    active_out,
    slope_out,
    small_out,
    rise_bias_out,
    entry_tree,
    tokens_ref,
    joined_weight,
    query_ref,
    key_ref,
    value_ref,
    mask_ref,
    attended_ref,
    log_ref,
    whole_ref,
    out_weight,
    up_weight,
    normed_ref,
    low_ref,
    active_ref,
    slope_ref,
    packed_ref,
    down_stage,
    upstream_stage,
    *sems,
):
    net = Net(*sems)
    c, y, z = net.c, net.y, net.z
    trunk = TRUNK * block
    wide = 3 * block
    low = low_lanes()
    rows_all, mine = query_ref.shape
    width = tokens_ref.shape[2]
    blocks = tokens_ref.shape[0]
    pairs = mine // (2 * LOW_HALF)
    heads = relaxed_ref.shape[0] // 2
    half = rows_all // 2
    expand = up_weight.shape[4]
    splits = FRONT["splits"]
    chunks = []

    def add(own, whole, share):
        split = splits[len(chunks) % len(splits)]
        kind = WideGather if len(chunks) in FRONT["wide"] else Gather
        chunks.append(kind(net, len(chunks), own, whole, share, split))

    def columns(index):
        return pl.ds(pl.multiple_of(index * mine, mine), mine)

    for i in range(3):
        add(
            lambda part, i=i: joined_shard.at[part, :, columns(2 * i + c)],
            lambda a, b, part, i=i: joined_weight.at[a, b, part, :, columns(i)],
            False,
        )
    for h in range(heads):
        add(
            lambda part, h=h: relaxed_ref.at[c * heads + h, part],
            lambda a, b, part, h=h: mask_ref.at[h, a, b, part],
            False,
        )
    add(
        lambda part: out_shard.at[part, :, columns(c)],
        lambda a, b, part: out_weight.at[a, b, part, :, columns(c)],
        True,
    )
    for j in range(4):
        add(
            lambda part, j=j: up_shard.at[part, :, columns(4 * c + j)],
            lambda a, b, part, j=j: up_weight.at[a, b, part, :, columns(4 * c + j)],
            True,
        )
    spare = len(chunks) + 4
    for j in range(4):
        chunks.append(
            FarGather(
                net,
                len(chunks),
                lambda part, j=j: down_shard.at[j, part, :, columns(c)],
                lambda a, b, part, j=j: down_out.at[a, b, j, part, :, columns(c)],
                True,
                splits[len(chunks) % len(splits)],
                down_stage.at[j],
                spare + j,
            )
        )
    spare += 4
    entry = Sharing(net, spare, entry_ref, entry_tree)
    upstream = Sharing(net, spare + 1, upstream_ref, tree_out, upstream_stage)
    vector_row = spare + 3
    flushes = []
    first_flush = spare + 4

    def flush(source, target):
        flushes.append(Flush(net, first_flush + len(flushes), source, target))
        return flushes[-1]

    def vector_copy(slot):
        if slot < 3:
            return net.remote(vector_row, slot, vectors_ref, packed_ref.at[z, y], slot + 1)
        return net.remote(vector_row, slot, packed_ref.at[:, y], packed_ref.at[:, y], "y")

    class Vectors:
        def home(self):
            return net.stay(vector_row, vectors_ref, packed_ref.at[z, y])

        def step(self, number):
            if number == 0:
                self.home().start()
                for slot in range(3):
                    vector_copy(slot).start()
            elif number == 1:
                self.home().wait()
                for slot in range(3):
                    vector_copy(slot).wait_recv()
                vector_copy(3).start()
            elif number == 2:
                vector_copy(3).wait_recv()

        def finish(self):
            for slot in range(4):
                vector_copy(slot).wait_send()

    vectors = Vectors()
    net.greet(("x", "c", "y", 1, 2, 3))
    for chunk in chunks[-4:]:
        chunk.load().start()
    upstream.load().start()

    starts = []
    time = FRONT["origin"]
    for count, length in (
        (blocks // 2, FRONT["join"]),
        (8 * pairs, FRONT["attend"]),
        (half // block, FRONT["norm"]),
        (2 * (expand // mine), FRONT["rise"]),
    ):
        for _ in range(count):
            starts.append(time)
            time += length
    total = len(starts)
    first_attend = blocks // 2
    first_norm = first_attend + 8 * pairs
    first_rise = first_norm + half // block

    plan = []
    for i, chunk in enumerate(chunks):
        start = i * FRONT["pace"]
        limit = 1e9
        if i < 3:
            limit = starts[0]
        elif i < 3 + heads:
            limit = starts[first_attend + 8 * ((i - 3) // 2)]
        elif i == 3 + heads:
            limit = starts[first_norm]
        elif i < 8 + heads:
            limit = starts[first_rise + 4 * (i - 4 - heads)]
        moments = [max(0.0, start - FRONT["lead"]), start + FRONT["lag1"]]
        for lag in ("lag2", "lag3", "lag4"):
            moments.append(moments[-1] + FRONT[lag])
        for step, moment in enumerate(moments):
            plan.append((min(moment, limit - 0.001 * (6 - step)), chunk, step))
    for step, moment in enumerate((0.0, 14.0, 24.0, 30.0)):
        plan.append((min(moment, starts[0] - 0.001), entry, step))
    for step, moment in enumerate((0.1, 9.0, 20.0)):
        plan.append((min(moment, starts[0] - 0.001), vectors, step))
    for step, moment in enumerate(FRONT["upstream"]):
        plan.append((moment, upstream, step))
    after = starts[first_attend] + 0.5
    plan.append((after, flush(joined_weight, joined_out), 0))
    plan.append((after + 2, flush(tokens_ref, tokens_out), 0))
    plan.append((after + 6, flush(query_ref, query_out), 0))
    plan.append((after + 8, flush(key_ref, key_out), 0))
    plan.append((after + 10, flush(value_ref, value_out), 0))
    plan.append((starts[first_attend + 16] + 0.1, flush(mask_ref, mask_out), 0))
    plan.append((starts[first_norm], flush(attended_ref, attended_out), 0))
    plan.append((starts[first_norm], flush(log_ref, log_out), 0))
    plan.append((starts[first_norm], flush(whole_ref, whole_out), 0))
    plan.append((starts[first_norm] + 0.1, flush(out_weight, out_out), 0))
    plan.append((starts[-4] + 0.01, flush(up_weight, up_out), 0))
    plan.append((starts[first_rise] + 1, flush(normed_ref, normed_out), 0))
    plan.sort(key=lambda item: item[0])
    placed = []
    for moment, item, step in plan:
        slot = next((s for s in range(total) if starts[s] > moment), total)
        slot = -1 if moment < starts[0] else max(slot - 1, 0)
        if moment >= starts[-1] + FRONT["rise"]:
            slot = total
        placed.append((slot, item, step))

    def events(slot, first, last, kinds=None):
        for number in range(first, last):
            if kinds is not None and (number - first) % 8 not in kinds:
                continue
            steps = [entry for entry in placed if entry[0] == number]
            if steps:

                @pl.when(slot == number)
                def _(steps=steps):
                    for _, item, step in steps:
                        item.step(step)

    for slot, item, step in placed:
        if slot < 0:
            item.step(step)

    shard = width // 8
    lane = lax.broadcasted_iota(jnp.int32, (128, width), 1)
    line = lax.broadcasted_iota(jnp.int32, (128, width), 0)
    assembled = jnp.zeros((16, width), F32)
    for f in range(8):
        place = jnp.where((lane == line + shard * f) & (line < shard), 1.0, 0.0).astype(BF)
        assembled = assembled + dot_nn(packed_ref[f // 2, f % 2], place)
        for m in range(3):
            at = (f * 3 + m) * 128
            rise_bias_out[0:1, at : at + 128] = packed_ref[f // 2, f % 2, 8 + m : 9 + m, :].astype(F32)
    small_out[...] = assembled

    def project(i, carry):
        events(i, 0, first_attend)
        tokens_ref[2 * i] = entry_tree[order_ref[2 * i]]
        tokens_ref[2 * i + 1] = entry_tree[order_ref[2 * i + 1]]
        rows = pl.ds(pl.multiple_of(2 * block * i, 2 * block), 2 * block)
        pair = tokens_ref[pl.ds(2 * i, 2)].reshape(2 * block, width)
        joined = dot_nn(pair, joined_weight[...].reshape(width, 3 * mine))
        query = (joined[:, :mine] + small_out[0:1, columns(c)]).astype(BF).astype(F32)
        query_ref[rows, :] = (query * (1.0 / math.sqrt(LOW_HALF))).astype(BF)
        key_ref[rows, :] = joined[:, mine : 2 * mine].astype(BF)
        value_ref[rows, :] = (joined[:, 2 * mine :] + small_out[1:2, columns(c)]).astype(BF)
        return carry

    lax.fori_loop(0, blocks // 2, project, 0)

    def soften(parts, masks, values):
        top = parts[0].max(axis=1, keepdims=True)
        for part in parts[1:]:
            top = jnp.maximum(top, part.max(axis=1, keepdims=True))
        scale = 0.0
        out = 0.0
        for part, mask, value in zip(parts, masks, values):
            weight = jnp.exp(part - top)
            scale = scale + weight.sum(axis=1, keepdims=True)
            out = out + dot_nn((weight * mask.astype(F32)).astype(BF), value)
        return (out * (1.0 / scale), top + jnp.log(scale))

    def emit(rows, p, lanes, results):
        attended_ref[rows, lanes] = jnp.where(low, results[0][0], results[1][0]).astype(BF)
        logs = log_ref[rows, :]
        for which in range(2):
            logs = jnp.where(lane_row == 2 * p + which, results[which][1], logs)
        log_ref[rows, :] = logs

    lane_row = lax.broadcasted_iota(jnp.int32, (1, 128), 1)
    log_ref[...] = jnp.zeros_like(log_ref)

    def one_pair(p, carry):
        lanes = pl.ds(pl.multiple_of(p * 2 * LOW_HALF, 2 * LOW_HALF), 2 * LOW_HALF)

        def mask_strip(which, tile):
            return mask_ref[2 * p + which, tile].reshape(block, mask_ref.shape[-1])

        def trunk_rows(index, carry):
            for part_slot in range(2):
                slot = first_attend + 8 * p + 2 * index + part_slot
                events(slot, first_attend, first_norm, range(part_slot, 4, 2))
            rows = pl.ds(pl.multiple_of(index * 2 * block, 2 * block), 2 * block)
            query = query_ref[rows, lanes]
            results = []
            for which in range(2):
                strips = [mask_strip(which, 2 * index + s) for s in range(2)]
                mask_rows = jnp.concatenate(strips, axis=0)
                places = [(0, trunk, mask_rows)]
                side = mask_columns(mask_rows, (1, 0, 1), block)
                places += [(trunk + wide * g, wide, side) for g in range(GROUPS)]
                head = one_head(query, which)
                parts = [dot_nt(head, key_ref[a : a + w, lanes]) for a, w, _ in places]
                values = [value_ref[a : a + w, lanes] for a, w, _ in places]
                results.append(soften(parts, [place[2] for place in places], values))
            emit(rows, p, lanes, results)
            return carry

        lax.fori_loop(0, TRUNK // 2, trunk_rows, 0)

        def group_rows(group, carry):
            events(first_attend + 8 * p + 4 + group, first_attend, first_norm, range(4, 8))
            base = pl.multiple_of(trunk + wide * group, block)
            rows = pl.ds(base, wide)
            query = query_ref[rows, lanes]
            results = []
            for which in range(2):
                strips = [mask_strip(which, t) for t in (1, 0, 1)]
                head = one_head(query, which)
                far = dot_nt(head, key_ref[0:trunk, lanes])
                top = far.max(axis=1, keepdims=True)
                near = []
                tops = []
                for row in range(3):
                    start, size, tiles = group_columns(row, block)
                    place = pl.ds(pl.multiple_of(base + start, block), size)
                    at = slice(row * block, (row + 1) * block)
                    part = dot_nt(head[at], key_ref[place, lanes])
                    near.append((part, place, mask_columns(strips[row], tiles, block)))
                    tops.append(jnp.maximum(top[at], part.max(axis=1, keepdims=True)))
                top = jnp.concatenate(tops, axis=0)
                weight = jnp.exp(far - top)
                mask_rows = jnp.concatenate(strips, axis=0).astype(F32)
                scale = weight.sum(axis=1, keepdims=True)
                out = dot_nn((weight * mask_rows).astype(BF), value_ref[0:trunk, lanes])
                scales = []
                outs = []
                for row, (part, place, mask) in enumerate(near):
                    weight = jnp.exp(part - tops[row])
                    scales.append(weight.sum(axis=1, keepdims=True))
                    weight = (weight * mask.astype(F32)).astype(BF)
                    outs.append(dot_nn(weight, value_ref[place, lanes]))
                scale = scale + jnp.concatenate(scales, axis=0)
                out = (out + jnp.concatenate(outs, axis=0)) * (1.0 / scale)
                results.append((out, top + jnp.log(scale)))
            emit(rows, p, lanes, results)
            return carry

        lax.fori_loop(0, GROUPS, group_rows, 0)
        return carry

    lax.fori_loop(0, pairs, one_pair, 0)
    mine_rows = pl.ds(pl.multiple_of(c * half, half), half)
    their_rows = pl.ds(pl.multiple_of((1 - c) * half, half), half)
    cross = net.remote(vector_row, 4, attended_ref.at[their_rows], whole_ref.at[:, columns(c)], "c")
    cross.start()
    whole_ref[:, columns(c)] = attended_ref[mine_rows, :]
    cross.wait_recv()

    def normalize(i, carry):
        events(first_norm + i, first_norm, first_rise)
        rows = pl.ds(pl.multiple_of(i * block, block), block)
        first = tokens_ref[c * (blocks // 2) + i].astype(F32) + small_out[2:3, :]
        first = first + dot_nn(whole_ref[rows, :], out_weight[...].reshape(width, width))
        average = jnp.mean(first, axis=1, keepdims=True)
        centred = first - average
        inv = lax.rsqrt(jnp.mean(centred * centred, axis=1, keepdims=True) + EPSILON)
        normed = centred * inv
        normed_ref[rows, :] = normed
        inv_out[rows, :] = jnp.broadcast_to(inv, (block, 128))
        low_ref[rows, :] = (normed * small_out[3:4, :] + small_out[4:5, :]).astype(BF)
        return carry

    lax.fori_loop(0, half // block, normalize, 0)
    per = expand // mine

    def rise_place(i):
        rows = pl.ds(pl.multiple_of((i % 2) * (half // 2), half // 2), half // 2)
        return rows, columns((per // 2) * (i // 2 % 2) + i // 4)

    def out_copies(i):
        row = first_flush + len(flushes)
        slot = i % 2
        rows, place = rise_place(i)
        return (
            net.stay(row + slot, active_ref.at[slot], active_out.at[rows, place]),
            net.stay(row + 2 + slot, slope_ref.at[slot], slope_out.at[rows, place]),
        )

    def rise(i, carry):
        events(first_rise + i, first_rise, total)
        rows, place = rise_place(i)
        upper = dot_nn(low_ref[rows, :], up_weight[:, :, :, :, place].reshape(width, mine))
        active, slope = gelu_parts(upper + rise_bias_out[0:1, place])

        @pl.when(i >= 2)
        def _():
            for copy in out_copies(i - 2):
                copy.wait()

        active_ref[i % 2] = active.astype(BF)
        slope_ref[i % 2] = slope.astype(BF)
        for copy in out_copies(i):
            copy.start()
        return carry

    lax.fori_loop(0, 2 * per, rise, 0)
    for slot, item, step in placed:
        if slot == total:
            item.step(step)
    for i in (2 * per - 2, 2 * per - 1):
        for copy in out_copies(i):
            copy.wait()
    for item in chunks + [entry, upstream, vectors] + flushes:
        item.finish()
    cross.wait_send()


def front(order, entry, upstream, joined, relaxed, out_shard, up_shard, down_shard, vectors):
    micro, own_blocks, block, width = entry.shape
    own_rows = own_blocks * block
    rows = 4 * own_rows
    half = rows // 2
    blocks = rows // block
    mine = width // CORES
    heads = relaxed.shape[0] // CORES
    expand = up_shard.shape[2]
    like = jax.ShapeDtypeStruct
    grown = lambda shard: (LINE, 2) + shard.shape
    joined_shape = (LINE, 2) + joined.shape[:2] + (3 * mine,)
    mask_shape = (heads, LINE, 2) + relaxed.shape[1:]
    vmem = lambda shape, kind=BF: pltpu.VMEM(shape, kind)
    return pl.pallas_call(
        functools.partial(front_kernel, block),
        name="front",
        in_specs=[SMEM] + [ANY] * 8,
        out_specs=[ANY] * 14 + [VMEM] + [ANY] * 2 + [VMEM] * 2,
        out_shape=[
            like((blocks, block, width), BF),
            like(joined_shape, BF),
            like((rows, mine), BF),
            like((rows, mine), BF),
            like((rows, mine), BF),
            like(mask_shape, BF),
            like((rows, mine), BF),
            like((rows, 128), F32),
            like((half, width), BF),
            like(grown(out_shard), BF),
            like(grown(up_shard), BF),
            like(grown(down_shard), BF),
            like((blocks, block, width), BF),
            like((half, width), F32),
            like((half, 128), F32),
            like((half, expand), BF),
            like((half, expand), BF),
            like((16, width), F32),
            like((1, expand), F32),
        ],
        scratch_shapes=[
            vmem((blocks, block, width)),
            vmem((blocks, block, width)),
            vmem(joined_shape),
            vmem((rows, mine)),
            vmem((rows, mine)),
            vmem((rows, mine)),
            vmem(mask_shape),
            vmem((rows, mine)),
            vmem((rows, 128), F32),
            vmem((half, width)),
            vmem(grown(out_shard)),
            vmem(grown(up_shard)),
            vmem((half, width), F32),
            vmem((half, width)),
            vmem((2, half // 2, mine)),
            vmem((2, half // 2, mine)),
            vmem((LINE, 2) + vectors.shape, vectors.dtype),
            vmem((4, 2, down_shard.shape[2], mine)),
            vmem(entry.shape[1:]),
        ]
        + copy_semaphores(48, 10),
        compiler_params=pltpu.CompilerParams(
            collective_id=4, has_side_effects=True, vmem_limit_bytes=VMEM_LIMIT
        ),
    )(order, entry, upstream, joined, relaxed, out_shard, up_shard, down_shard, vectors)


def scatter_buffers(count, shape, with_twin):
    half, columns = shape
    whole = pltpu.VMEM((count, LINE, 2, 2, half, columns), BF)
    line = pltpu.VMEM((count, LINE, half, columns), BF)
    return (
        [whole]
        + ([whole] if with_twin else [])
        + [
            line,
            pltpu.VMEM((count, 2, LINE, half, columns), BF),
            pltpu.VMEM((count, LINE - 1, half, columns), BF),
        ]
    )


REAR = dict(pace=4.0, lag=21.0, tail=4.5, attend=3.6, finish=5.0, spread=0.6)


def rear_kernel(
    block,
    scale,
    query_ref,
    key_ref,
    value_ref,
    mask_ref,
    out_ref,
    log_ref,
    joined_weight,
    small_ref,
    place_ref,
    delta_half,
    tokens_in,
    first_in,
    out_grad,
    up_grad,
    down_grad,
    layer_in,
    out_final,
    up_final,
    down_final,
    mask_final,
    joined_final,
    tokens_out,
    small_out,
    layer_out,
    delta_ref,
    key_sum,
    value_sum,
    query_turned,
    delta_turned,
    dmask_sum,
    dquery_ref,
    dkey_ref,
    dvalue_ref,
    tokens_ref,
    first_ref,
    part,
    first,
    second,
    third,
    joined_part,
    joined_first,
    joined_second,
    joined_third,
    mask_part,
    mask_first,
    mask_second,
    mask_third,
    give,
    keep,
    got,
    sums,
    from_peers,
    *sems,
):
    net = Net(*sems)
    x, c = net.x, net.c
    trunk = TRUNK * block
    wide = 3 * block
    low = low_lanes()
    lane = lax.broadcasted_iota(jnp.int32, (1, 128), 1)
    rows_all, mine = query_ref.shape
    blocks, _, width = tokens_ref.shape
    pairs = mine // (2 * LOW_HALF)
    heads = mask_ref.shape[0]
    half = rows_all // 2
    strip = mask_final.shape[3]
    chunks = []

    def own(index):
        return pl.ds(pl.multiple_of(index * mine, mine), mine)

    def dense(load, twin_load, final):
        k = len(chunks)
        twin = joined_part.at[k] if k < 3 else mask_part.at[k - 3, :, :, :, :, 0:mine]
        buffers = (first.at[k], second.at[k], third.at[k])
        chunks.append(Scatter(net, k, load, part.at[k], twin, twin_load, *buffers, final))

    dense(
        out_grad.at[:, :, :, :, own(c)],
        out_grad.at[:, :, :, :, own(1 - c)],
        lambda a, b: out_final.at[a, :, own(b)],
    )
    for j in range(4):
        dense(
            down_grad.at[:, :, j, :, :, own(c)],
            down_grad.at[:, :, j, :, :, own(1 - c)],
            lambda a, b, j=j: down_final.at[j, a, :, own(b)],
        )
    for j in range(4):
        dense(
            up_grad.at[:, :, :, :, own(4 * c + j)],
            up_grad.at[:, :, :, :, own(4 * (1 - c) + j)],
            lambda a, b, j=j: up_final.at[a, :, own(4 * b + j)],
        )
    dense_count = len(chunks)
    for p in range(pairs):
        for h in (2 * p, 2 * p + 1):
            buffers = (mask_first.at[h], mask_second.at[h], mask_third.at[h])
            chunks.append(
                Scatter(
                    net,
                    len(chunks),
                    None,
                    mask_part.at[h, :, :, :, 0:strip],
                    None,
                    None,
                    *buffers,
                    lambda a, b, h=h: mask_final.at[b, h, a],
                )
            )
        buffers = (joined_first.at[p], joined_second.at[p], joined_third.at[p])
        chunks.append(
            Scatter(
                net,
                len(chunks),
                None,
                joined_part.at[p],
                None,
                None,
                *buffers,
                lambda a, b, p=p: joined_final.at[p, a, b],
            )
        )
    spare = len(chunks)
    net.greet(("x", "c", "y", 1, 2, 3))

    mine_rows = pl.ds(pl.multiple_of(c * half, half), half)
    delta_cross = net.remote(spare, 0, delta_half.at[:, own(1 - c)], delta_ref.at[mine_rows], "c")
    delta_cross.start()
    delta_home = net.stay(spare, delta_half.at[:, own(c)], delta_ref.at[mine_rows])
    delta_home.start()
    tokens_load = net.stay(spare + 1, tokens_in, tokens_ref)
    first_load = net.stay(spare + 2, first_in, first_ref)
    tokens_load.start()
    own_blocks = blocks // 4
    layer_home = net.stay(spare + 3, layer_in.at[0:own_blocks], layer_out.at[x])
    layer_home.start()
    layer_cross = net.remote(spare, 3, layer_in.at[own_blocks:], layer_out.at[x], "x")
    layer_cross.start()

    own_rows = give.shape[1]
    per = own_rows // block

    def collect(target, core):
        for a in range(2):
            for b in range(per):
                place = place_ref[(2 * a + core) * per + b]
                target[a, b * block : (b + 1) * block] = tokens_ref[place]

    class Tokens:
        def core(self):
            return net.remote(spare, 1, give, got, "c")

        def chip(self):
            return net.remote(spare, 2, keep.at[1 - x], tokens_out.at[x], "x")

        def step(self, number):
            if number == 0:
                collect(give, 1 - c)
                self.core().start()
                collect(keep, c)
            elif number == 1:
                self.core().wait_recv()
                keep[...] = (keep[...].astype(F32) + got[...].astype(F32)).astype(BF)
                self.chip().start()
                tokens_out[x] = keep[x]
            elif number == 2:
                self.chip().wait_recv()

        def finish(self):
            self.core().wait_send()
            self.chip().wait_send()

    class Vectors:
        def copy(self, slot):
            peer = ("c", "x", "y", 1, 2, 3)[slot]
            source = sums.at[min(slot, 3)]
            return net.remote(spare + 1, slot, source, from_peers.at[slot], peer)

        def step(self, number):
            if number == 0:
                self.copy(0).start()
            elif number < 3:
                self.copy(number - 1).wait_recv()
                sums[number] = sums[number - 1] + from_peers[number - 1]
                self.copy(number).start()
            elif number == 3:
                self.copy(2).wait_recv()
                sums[3] = sums[2] + from_peers[2]
                for slot in (3, 4, 5):
                    self.copy(slot).start()
            elif number == 4:
                total = sums[3]
                for slot in (3, 4, 5):
                    self.copy(slot).wait_recv()
                    total = total + from_peers[slot]
                small_out[...] = total

        def finish(self):
            for slot in range(6):
                self.copy(slot).wait_send()

    home = Tokens()
    vectors = Vectors()
    starts = []
    ready = []
    time = 0.0
    for p in range(pairs):
        for _ in range(8):
            starts.append(time)
            time += REAR["attend"]
        time += REAR["finish"]
        ready.append(time)
    first_spread = len(starts)
    for _ in range(blocks // 2):
        starts.append(time)
        time += REAR["spread"]
    total = len(starts)
    end = time
    plan = []
    for i, chunk in enumerate(chunks):
        if i < dense_count:
            moments = [0.0, min(1.0 + i * REAR["pace"], ready[0] - REAR["finish"] - 0.01)]
        else:
            p = (i - dense_count) // 3
            start = max(i * REAR["pace"], ready[p] + 0.01 + 0.1 * ((i - dense_count) % 3))
            moments = [start, start]
        lag = REAR["lag"] if i < dense_count + 3 * (pairs - 1) else REAR["tail"]
        for _ in range(4):
            moments.append(moments[-1] + lag)
        moments.append(1000.0 + i)
        for step, moment in enumerate(moments):
            plan.append((moment + 0.001 * step, chunk, step))
    for step, moment in enumerate((0.0, 4.0, 24.0)):
        plan.append((end + moment, home, step))
    for step in range(5):
        plan.append((end + 3.0 + 6.0 * step, vectors, step))
    plan.sort(key=lambda item: item[0])
    placed = []
    for moment, item, step in plan:
        slot = next((s for s in range(total) if starts[s] > moment), total) - 1
        placed.append((total if moment >= end else slot, item, step))

    def events(slot, begin, until, kinds=None):
        for number in range(begin, until):
            if kinds is not None and (number - begin) % 8 not in kinds:
                continue
            steps = [entry for entry in placed if entry[0] == number]
            if steps:

                @pl.when(slot == number)
                def _(steps=steps):
                    for _, item, step in steps:
                        item.step(step)

    sums[0] = small_ref[...]
    tokens_load.wait()
    first_load.start()
    delta_home.wait()
    delta_cross.wait_recv()

    def one_pair(p, carry):
        pair_lanes = pl.ds(pl.multiple_of(p * 2 * LOW_HALF, 2 * LOW_HALF), 2 * LOW_HALF)
        key_sum[...] = jnp.zeros_like(key_sum)
        value_sum[...] = jnp.zeros_like(value_sum)
        dmask_sum[...] = jnp.zeros_like(dmask_sum)
        query_turned[...] = query_ref[:, pair_lanes].astype(F32).T.astype(BF)
        delta_turned[...] = delta_ref[:, pair_lanes].astype(F32).T.astype(BF)

        def cell(which, query_head, delta_head, log, row_term, mask, place, rows):
            lanes = slice(LOW_HALF * which, LOW_HALF * which + LOW_HALF)
            key = key_ref[place, pair_lanes]
            probs = jnp.exp(dot_nt(query_head, key) - log)
            pair = dot_nt(delta_head, value_ref[place, pair_lanes]) * probs
            mask = mask.astype(F32)
            dscores = (pair * mask - probs * row_term).astype(BF)
            weights = (probs * mask).astype(BF)
            key_sum[lanes, place] += dot_nn(query_turned[lanes, rows], dscores)
            value_sum[lanes, place] += dot_nn(delta_turned[lanes, rows], weights)
            return dot_nn(dscores, key), pair

        def heads_of(rows):
            query = query_ref[rows, pair_lanes]
            delta = delta_ref[rows, pair_lanes]
            product = delta.astype(F32) * out_ref[rows, pair_lanes].astype(F32)
            logs = log_ref[rows, :]
            for which in range(2):
                log = jnp.sum(jnp.where(lane == 2 * p + which, logs, 0.0), axis=1, keepdims=True)
                lanes = slice(LOW_HALF * which, LOW_HALF * which + LOW_HALF)
                row_term = jnp.sum(product[:, lanes], axis=1, keepdims=True)
                yield which, one_head(query, which), one_head(delta, which), log, row_term

        def fold(which, mask_place, pair, tiles):
            for tile in sorted(set(tiles)):
                dmask_sum[which, mask_place, tile * block : (tile + 1) * block] += sum(
                    pair[:, a * block : (a + 1) * block] for a, t in enumerate(tiles) if t == tile
                )

        def finish_rows(rows, dqueries):
            both = jnp.where(low, dqueries[0], dqueries[1]) * scale
            dquery_ref[rows, pair_lanes] = both.astype(BF)

        def trunk_rows(index, carry):
            for part_slot in range(2):
                events(8 * p + 2 * index + part_slot, 0, first_spread, range(part_slot, 4, 2))
            rows = pl.ds(pl.multiple_of(index * 2 * block, 2 * block), 2 * block)
            dqueries = []
            for which, query_head, delta_head, log, row_term in heads_of(rows):
                mask_rows = mask_ref[2 * p + which, rows, :]
                near = (query_head, delta_head, log, row_term)
                dquery, pair = cell(which, *near, mask_rows, pl.ds(0, trunk), rows)
                dmask_sum[which, rows, :] += pair
                side = mask_columns(mask_rows, (1, 0, 1), block)
                for g in range(GROUPS):
                    more, pair = cell(which, *near, side, pl.ds(trunk + wide * g, wide), rows)
                    dquery = dquery + more
                    fold(which, rows, pair, (1, 0, 1))
                dqueries.append(dquery)
            finish_rows(rows, dqueries)
            return carry

        lax.fori_loop(0, TRUNK // 2, trunk_rows, 0)

        def group_rows(group, carry):
            events(8 * p + 4 + group, 0, first_spread, range(4, 8))
            base = pl.multiple_of(trunk + wide * group, block)
            rows = pl.ds(base, wide)
            dqueries = []
            for which, query_head, delta_head, log, row_term in heads_of(rows):
                strips = [mask_ref[2 * p + which, t * block : (t + 1) * block, :] for t in (1, 0, 1)]
                mask_rows = jnp.concatenate(strips, axis=0)
                dquery, pair = cell(
                    which, query_head, delta_head, log, row_term, mask_rows, pl.ds(0, trunk), rows
                )
                dmask_sum[which, block : 2 * block, :] += pair[0:block] + pair[2 * block :]
                dmask_sum[which, 0:block, :] += pair[block : 2 * block]
                near = []
                for row in range(3):
                    at = slice(row * block, (row + 1) * block)
                    start, size, tiles = group_columns(row, block)
                    tile = 0 if row == 1 else 1
                    more, pair = cell(
                        which,
                        query_head[at],
                        delta_head[at],
                        log[at],
                        row_term[at],
                        mask_columns(strips[row], tiles, block),
                        pl.ds(pl.multiple_of(base + start, block), size),
                        pl.ds(pl.multiple_of(base + row * block, block), block),
                    )
                    fold(which, pl.ds(tile * block, block), pair, tiles)
                    near.append(more)
                dqueries.append(dquery + jnp.concatenate(near, axis=0))
            finish_rows(rows, dqueries)
            return carry

        lax.fori_loop(0, GROUPS, group_rows, 0)
        dkey_ref[:, pair_lanes] = key_sum[...].T.astype(BF)
        dvalue_ref[:, pair_lanes] = value_sum[...].T.astype(BF)
        query_turned[...] = dquery_ref[:, pair_lanes].astype(F32).T.astype(BF)
        place = pl.ds(pl.multiple_of(c * mine + p * 128, 128), 128)
        for row, source in ((0, dquery_ref), (1, dvalue_ref)):
            column = jnp.sum(source[:, pair_lanes].astype(F32), axis=0, keepdims=True)
            sums[0, row : row + 1, place] = column
        tokens = tokens_ref[...].reshape(rows_all, width)
        for t, source in enumerate((query_turned, key_sum, value_sum)):
            grad = dot_nn(source[...].astype(BF), tokens).T.astype(BF)
            columns = slice(t * 128, t * 128 + 128)
            joined_part[p, :, :, :, :, columns] = grad.reshape(joined_part.shape[1:5] + (128,))
        shape = mask_part.shape[2:4] + (strip, mask_part.shape[5])
        for which in range(2):
            for tile in range(LINE):
                rows = dmask_sum[which, tile * block : (tile + 1) * block, :].astype(BF)
                mask_part[2 * p + which, tile, :, :, 0:strip, :] = rows.reshape(shape)
        return carry

    lax.fori_loop(0, pairs, one_pair, 0)
    first_load.wait()

    def spread(i, carry):
        events(first_spread + i, first_spread, total)
        rows = pl.ds(pl.multiple_of(2 * block * i, 2 * block), 2 * block)
        grads = (dquery_ref, dkey_ref, dvalue_ref)
        out = 0.0
        for t, grad in enumerate(grads):
            out = out + dot_nt(grad[rows, :], joined_weight[:, t * mine : (t + 1) * mine])
        inside = (i // (blocks // 4) == c).astype(F32)
        at = i % (blocks // 4)
        out = out + inside * first_ref[pl.ds(2 * at, 2)].reshape(2 * block, width)
        tokens_ref[pl.ds(2 * i, 2)] = out.astype(BF).reshape(2, block, width)
        return carry

    lax.fori_loop(0, blocks // 2, spread, 0)
    for slot, item, step in placed:
        if slot == total:
            item.step(step)
    layer_home.wait()
    layer_cross.wait_recv()
    layer_cross.wait_send()
    for item in chunks + [home, vectors]:
        item.finish()
    delta_cross.wait_send()


def rear(
    query, key, value, mask, out, logs, weight, small, place, delta, tokens, first, out_grad, up_grad,
    down_grad, layer, block, scale
):
    rows, mine = query.shape
    width = 2 * mine
    heads, span, _ = mask.shape
    pairs = heads // 2
    blocks = rows // block
    own_rows = rows // 4
    strip = span // 16
    piece = out_grad.shape[3]
    like = jax.ShapeDtypeStruct
    vmem = lambda shape, kind=BF: pltpu.VMEM(shape, kind)
    mask_buffers = scatter_buffers(heads, (strip, span), False)
    mask_buffers[0] = vmem((heads, LINE, 2, 2, piece, span))
    return pl.pallas_call(
        functools.partial(rear_kernel, block, scale),
        name="rear",
        in_specs=[VMEM] * 8 + [SMEM] + [ANY] * 7,
        out_specs=[VMEM] * 7 + [ANY],
        out_shape=[
            like((2,) + out_grad.shape[3:], BF),
            like((2,) + up_grad.shape[3:], BF),
            like((4, 2) + down_grad.shape[4:], BF),
            like((2, heads, 2, strip, span), BF),
            like((pairs, 2, 2, piece, mine), BF),
            like((2, own_rows, width), BF),
            like(small.shape, F32),
            like((2, blocks // 4, block, width), BF),
        ],
        scratch_shapes=[
            vmem((rows, mine)),
            vmem((2 * LOW_HALF, rows), F32),
            vmem((2 * LOW_HALF, rows), F32),
            vmem((2 * LOW_HALF, rows)),
            vmem((2 * LOW_HALF, rows)),
            vmem((2, span, span), F32),
            vmem((rows, mine)),
            vmem((rows, mine)),
            vmem((rows, mine)),
            vmem(tokens.shape),
            vmem(first.shape, F32),
        ]
        + scatter_buffers(9, (piece, mine), False)
        + scatter_buffers(pairs, (piece, mine), False)
        + mask_buffers
        + [vmem((2, own_rows, width))] * 3
        + [vmem((4,) + small.shape, F32), vmem((6,) + small.shape, F32)]
        + copy_semaphores(24, 11),
        compiler_params=pltpu.CompilerParams(
            collective_id=5, has_side_effects=True, vmem_limit_bytes=VMEM_LIMIT
        ),
    )(
        query, key, value, mask, out, logs, weight, small, place, delta, tokens, first, out_grad,
        up_grad, down_grad, layer
    )


def gather_rows(array, axis=0):
    return lax.all_gather(array, "fsdp", axis=axis, tiled=True)


def per_device(
    layer_entry_matrix,
    loss_sensitivity,
    ancestor_block_table,
    gate_trained_scores,
    gate_random_jitter,
    softening_scale,
    triple_projection_matrix,
    asker_constant_vector,
    content_constant_vector,
    mixer_exit_matrix,
    mixer_exit_constant,
    mixer_scaling_factor,
    mixer_recentering_term,
    dense_expand_matrix,
    dense_expand_constant,
    dense_contract_matrix,
    dense_contract_constant,
    dense_scaling_factor,
    dense_recentering_term,
):
    micro, _, own_rows, width = layer_entry_matrix.shape
    leaf_count = lax.axis_size("leaf")
    blocks = ancestor_block_table.shape[2]
    rows = own_rows * leaf_count
    block = rows // blocks
    heads, _, span = gate_trained_scores.shape
    leaf = lax.axis_index("leaf")
    tree = leaf // CORES
    core = leaf % CORES
    my_heads = heads // CORES
    my_width = width // CORES
    half = rows // CORES
    pairs = [[CORES * i + c for c in range(CORES)] for i in range(leaf_count // CORES)]
    score_scale = 1.0 / math.sqrt(width // heads)

    orders = [tree_order(ancestor_block_table[m, 0]) for m in range(micro)]
    order = jnp.where(tree == 0, orders[0][0], orders[1][0])

    def own_tree(tokens):
        whole = lax.all_gather(tokens[:, 0], "leaf", axis=1, tiled=True)
        mine = lax.dynamic_index_in_dim(whole, tree, 0, keepdims=False)
        return reorder(mine.reshape(blocks, block, width), order).reshape(rows, width)

    def own_tokens(halves):
        whole = lax.all_gather(halves, "leaf", axis=0, tiled=True)
        whole = whole.reshape(micro, blocks, block, width)
        mine = [reorder(whole[m], orders[m][1]) for m in range(micro)]
        mine = jnp.stack(mine).reshape(micro, 1, rows, width)
        return lax.dynamic_slice_in_dim(mine, leaf * own_rows, own_rows, 2)

    def own_half(array):
        return lax.dynamic_slice_in_dim(array, core * half, half, 0)

    softened = jax.nn.sigmoid(
        (gate_trained_scores + gate_random_jitter) / softening_scale[:, None, None]
    )
    relaxed = lax.dynamic_slice_in_dim(softened.astype(BF), core * my_heads, my_heads, 0)
    mask = gather_rows(relaxed, 1)
    joined_weight = gather_rows(triple_projection_matrix)
    out_weight = gather_rows(mixer_exit_matrix)
    up_weight = gather_rows(dense_expand_matrix)
    down_weight = gather_rows(dense_contract_matrix)
    vectors = [
        asker_constant_vector,
        content_constant_vector,
        mixer_exit_constant,
        mixer_scaling_factor,
        mixer_recentering_term,
        dense_contract_constant,
        dense_scaling_factor,
        dense_recentering_term,
        dense_expand_constant,
    ]
    packed = gather_rows(jnp.concatenate(vectors)[None])
    places = []
    first = 0
    for vector in vectors:
        places.append((first, first + vector.shape[0]))
        first += vector.shape[0]
    (
        query_bias,
        value_bias,
        out_bias,
        first_gain,
        first_shift,
        down_bias,
        second_gain,
        second_shift,
        up_bias,
    ) = [packed[:, a:b].reshape(-1).astype(F32) for a, b in places]

    tokens = own_tree(layer_entry_matrix)
    upstream = own_half(own_tree(loss_sensitivity)).astype(F32)

    def my_columns(matrix, which):
        return lax.dynamic_slice_in_dim(matrix, which * width + core * my_width, my_width, 1)

    def my_part(vector):
        return lax.dynamic_slice_in_dim(vector, core * my_width, my_width, 0)

    weight3 = jnp.concatenate([my_columns(joined_weight, i) for i in range(3)], axis=1)
    joined = dot_nn(tokens, weight3)
    query = (joined[:, :my_width] + my_part(query_bias)).astype(BF) * jnp.asarray(score_scale, BF)
    key = joined[:, my_width : 2 * my_width].astype(BF)
    value = (joined[:, 2 * my_width :] + my_part(value_bias)).astype(BF)

    attended_mine, logs = attend(query, key, value, mask, block)
    attended = own_half(
        lax.all_gather(attended_mine, "leaf", axis=1, tiled=True, axis_index_groups=pairs)
    )

    rows_mine = own_half(tokens).astype(F32)
    hidden, normed_first, inv_first = layer_norm(
        rows_mine + dot_nn(attended, out_weight) + out_bias, first_gain, first_shift
    )
    hidden_low = hidden.astype(BF)
    active, slope = gelu_parts(dot_nn(hidden_low, up_weight) + up_bias)
    active = active.astype(BF)
    output, normed_second, inv_second = layer_norm(
        hidden + dot_nn(active, down_weight) + down_bias, second_gain, second_shift
    )
    layer_out = own_tokens(output.astype(BF))

    delta_second, second_gain_grad, second_shift_grad = norm_backward(
        upstream, normed_second, inv_second, second_gain
    )
    delta_branch = delta_second.astype(BF)
    down_weight_grad = dot_tn(active, delta_branch)
    down_bias_grad = jnp.sum(delta_branch.astype(F32), axis=0)
    delta_up = (dot_nt(delta_branch, down_weight) * slope).astype(BF)
    up_weight_grad = dot_tn(hidden_low, delta_up)
    up_bias_grad = jnp.sum(delta_up.astype(F32), axis=0)
    delta_first, first_gain_grad, first_shift_grad = norm_backward(
        delta_second + dot_nt(delta_up, up_weight), normed_first, inv_first, first_gain
    )
    delta_proj = delta_first.astype(BF)
    out_weight_grad = dot_tn(attended, delta_proj)
    out_bias_grad = jnp.sum(delta_proj.astype(F32), axis=0)
    delta_attended = lax.all_gather(
        dot_nt(delta_proj, out_weight).astype(BF),
        "leaf",
        axis=0,
        tiled=True,
        axis_index_groups=pairs,
    )
    delta_attended = lax.dynamic_slice_in_dim(delta_attended, core * my_width, my_width, 1)

    dquery, dkey, dvalue, dmask = attend_back(
        query, key, value, mask, attended_mine, logs, delta_attended, block, score_scale
    )
    djoined = jnp.concatenate([dquery, dkey, dvalue], axis=1)
    joined_grad = dot_tn(tokens, djoined)
    query_bias_grad = jnp.sum(dquery.astype(F32), axis=0)
    value_bias_grad = jnp.sum(dvalue.astype(F32), axis=0)
    dtokens = lax.psum_scatter(
        dot_nt(djoined, weight3).astype(BF),
        "leaf",
        scatter_dimension=0,
        tiled=True,
        axis_index_groups=pairs,
    )
    tokens_grad = own_tokens((delta_first + dtokens.astype(F32)).astype(BF))

    def placed(part, whole_size, start, axis):
        shape = list(part.shape)
        shape[axis] = whole_size
        return lax.dynamic_update_slice_in_dim(jnp.zeros(shape, part.dtype), part, start, axis)

    def owned(grad, axis=0):
        return lax.psum_scatter(
            grad.astype(BF), "fsdp", scatter_dimension=axis, tiled=True
        )

    joined_part = owned(joined_grad)
    joined_full = jnp.zeros((joined_part.shape[0], 3 * width), BF)
    for i in range(3):
        joined_full = lax.dynamic_update_slice_in_dim(
            joined_full,
            joined_part[:, i * my_width : (i + 1) * my_width],
            i * width + core * my_width,
            1,
        )
    matrices = (
        joined_full,
        owned(out_weight_grad),
        owned(up_weight_grad),
        owned(down_weight_grad),
        placed(owned(dmask, 1), heads, core * my_heads, 0),
    )
    joined_total, out_total, up_total, down_total, mask_total = [
        lax.psum(matrix, "leaf").astype(F32) for matrix in matrices
    ]
    small = (
        placed(query_bias_grad, width, core * my_width, 0),
        placed(value_bias_grad, width, core * my_width, 0),
        out_bias_grad,
        first_gain_grad,
        first_shift_grad,
        up_bias_grad,
        down_bias_grad,
        second_gain_grad,
        second_shift_grad,
    )
    fsdp_count = lax.axis_size("fsdp")
    packed_grads = jnp.concatenate([s.reshape(fsdp_count, -1) for s in small], axis=1)
    packed_grads = lax.psum(
        lax.psum_scatter(packed_grads, "fsdp", scatter_dimension=0, tiled=True), "leaf"
    )[0]
    vector_grads = []
    first = 0
    for s in small:
        size = s.shape[0] // fsdp_count
        vector_grads.append(packed_grads[first : first + size])
        first += size
    mask_gradient = mask_total * softened * (1.0 - softened) / softening_scale[:, None, None]
    return (
        layer_out,
        tokens_grad,
        joined_total,
        vector_grads[0],
        vector_grads[1],
        out_total,
        vector_grads[2],
        vector_grads[3],
        vector_grads[4],
        up_total,
        vector_grads[5],
        down_total,
        vector_grads[6],
        vector_grads[7],
        vector_grads[8],
        mask_gradient,
    )


def fast_device(
    layer_entry_matrix,
    loss_sensitivity,
    ancestor_block_table,
    gate_trained_scores,
    gate_random_jitter,
    softening_scale,
    triple_projection_matrix,
    asker_constant_vector,
    content_constant_vector,
    mixer_exit_matrix,
    mixer_exit_constant,
    mixer_scaling_factor,
    mixer_recentering_term,
    dense_expand_matrix,
    dense_expand_constant,
    dense_contract_matrix,
    dense_contract_constant,
    dense_scaling_factor,
    dense_recentering_term,
):
    micro, _, own_rows, width = layer_entry_matrix.shape
    blocks = ancestor_block_table.shape[2]
    rows = own_rows * 4
    block = rows // blocks
    heads, strip, span = gate_trained_scores.shape
    leaf = lax.axis_index("leaf")
    tree, core = leaf // CORES, leaf % CORES
    mine = width // CORES
    half = rows // CORES
    shard = width // 8
    hidden_shard = dense_contract_matrix.shape[0]
    score_scale = 1.0 / math.sqrt(width // heads)

    table = lax.dynamic_index_in_dim(ancestor_block_table[:, 0], tree, 0, keepdims=False)
    order, place = tree_order(table)
    softened = jax.nn.sigmoid(
        (gate_trained_scores + gate_random_jitter) / softening_scale[:, None, None]
    )
    relaxed = softened.astype(BF).reshape(heads, 2, strip // 2, span)
    vectors = [
        asker_constant_vector,
        content_constant_vector,
        mixer_exit_constant,
        mixer_scaling_factor,
        mixer_recentering_term,
        dense_contract_constant,
        dense_scaling_factor,
        dense_recentering_term,
        dense_expand_constant,
    ]
    sizes = [vector.shape[0] for vector in vectors]
    used = sum(sizes)
    places = [sum(sizes[:i]) for i in range(len(sizes))]
    wide = jnp.pad(jnp.stack(vectors[:8]), ((0, 0), (0, 128 - shard)))
    tall = vectors[8].reshape(-1, 128)
    flat = jnp.pad(jnp.concatenate([wide, tall]), ((0, 8 - tall.shape[0]), (0, 0)))

    (
        tokens,
        joined_weight,
        query,
        key,
        value,
        mask,
        attended_mine,
        logs,
        attended,
        out_weight,
        up_weight,
        down_weight,
        tree_upstream,
        normed_first,
        inv_first,
        active,
        slope,
        gathered,
        _,
    ) = front(
        order,
        layer_entry_matrix.reshape(micro, own_rows // block, block, width),
        loss_sensitivity.reshape(micro, own_rows // block, block, width),
        triple_projection_matrix.reshape(2, shard // 2, 3 * width),
        relaxed,
        mixer_exit_matrix.reshape(2, shard // 2, width),
        dense_expand_matrix.reshape(2, shard // 2, -1),
        dense_contract_matrix.reshape(4, 2, hidden_shard // 8, width),
        flat,
    )
    first_gain, first_shift, down_bias, second_gain, second_shift = [
        gathered[i : i + 1] for i in range(3, 8)
    ]
    inv_first = inv_first[:, :1]
    joined_weight = joined_weight.reshape(width, 3 * mine)
    mask = mask.reshape(heads // CORES, span, span)
    out_weight = out_weight.reshape(width, width)
    up_weight = up_weight.reshape(width, -1)
    down_weight = down_weight.reshape(-1, width)
    half_order = lax.dynamic_slice_in_dim(order, core * (blocks // 2), blocks // 2, 0)
    upstream = pick(half_order, tree_upstream, tree_upstream).reshape(half, width).astype(F32)
    tokens = tokens.reshape(rows, width)
    hidden = normed_first * first_gain + first_shift
    hidden_low = hidden.astype(BF)
    output, normed_second, inv_second = layer_norm(
        hidden + dot_nn(active, down_weight) + down_bias, second_gain, second_shift
    )
    to_core = [(i, i ^ 1) for i in range(4)]
    low_output = output.astype(BF).reshape(blocks // 2, block, width)
    twin_output = lax.ppermute(low_output, "leaf", to_core)
    swap = core * (blocks // 2)
    own_blocks = blocks // 4
    here = lax.dynamic_slice_in_dim(place, leaf * own_blocks, own_blocks, 0)
    there = lax.dynamic_slice_in_dim(place, (leaf ^ 2) * own_blocks, own_blocks, 0)
    wanted = jnp.concatenate([here, there])
    wanted = (wanted + swap) % blocks
    picked = pick(wanted, low_output, twin_output)
    delta_second, second_gain_grad, second_shift_grad = norm_backward(
        upstream, normed_second, inv_second, second_gain
    )
    delta_branch = delta_second.astype(BF)
    down_weight_grad = dot_tn(active, delta_branch).astype(BF)
    down_bias_grad = jnp.sum(delta_branch.astype(F32), axis=0)
    delta_branch, picked = lax.optimization_barrier((delta_branch, picked))
    delta_up = (dot_nt(delta_branch, down_weight) * slope.astype(F32)).astype(BF)
    up_weight_grad = dot_tn(hidden_low, delta_up).astype(BF)
    up_bias_grad = jnp.sum(delta_up.astype(F32), axis=0)
    delta_first, first_gain_grad, first_shift_grad = norm_backward(
        delta_second + dot_nt(delta_up, up_weight), normed_first, inv_first, first_gain
    )
    delta_proj = delta_first.astype(BF)
    out_weight_grad = dot_tn(attended, delta_proj).astype(BF)
    out_bias_grad = jnp.sum(delta_proj.astype(F32), axis=0)
    delta_attended = dot_nt(delta_proj, out_weight).astype(BF)

    blank = jnp.zeros((1, width), F32)
    small = jnp.concatenate(
        [
            blank,
            blank,
            out_bias_grad[None],
            first_gain_grad[None],
            first_shift_grad[None],
            down_bias_grad[None],
            second_gain_grad[None],
            second_shift_grad[None],
            up_bias_grad.reshape(-1, width),
            jnp.zeros((4, width), F32),
        ]
    )
    out_total, up_total, down_total, mask_total, joined_total, tokens_grad, small, layer_out = rear(
        query,
        key,
        value,
        mask,
        attended_mine,
        logs,
        joined_weight,
        small,
        place,
        delta_attended,
        tokens.reshape(blocks, block, width),
        delta_first.reshape(blocks // 2, block, width),
        out_weight_grad.reshape(LINE, 2, 2, shard // 2, width),
        up_weight_grad.reshape(LINE, 2, 2, shard // 2, -1),
        down_weight_grad.reshape(LINE, 2, 4, 2, hidden_shard // 8, width),
        picked,
        block,
        score_scale,
    )
    spot = lax.axis_index("fsdp")
    narrow = lax.dynamic_slice_in_dim(small[:8], spot * shard, shard, 1)
    vector_grads = [narrow[i] for i in range(8)]
    vector_grads.append(
        lax.dynamic_slice_in_dim(small[8:12].reshape(-1), spot * hidden_shard, hidden_shard, 0)
    )
    joined_total = joined_total.reshape(-1, 2, 2, shard // 2, 3, 128).transpose(1, 3, 4, 2, 0, 5)
    mask_total = mask_total.reshape(heads, strip, span)
    mask_gradient = (
        mask_total.astype(F32) * softened * (1.0 - softened) / softening_scale[:, None, None]
    )
    return (
        layer_out.reshape(micro, 1, own_rows, width),
        tokens_grad[:, None],
        joined_total.reshape(shard, 3 * width).astype(F32),
        vector_grads[0],
        vector_grads[1],
        out_total.reshape(shard, width).astype(F32),
        vector_grads[2],
        vector_grads[3],
        vector_grads[4],
        up_total.reshape(shard, -1).astype(F32),
        vector_grads[8],
        down_total.reshape(hidden_shard, width).astype(F32),
        vector_grads[5],
        vector_grads[6],
        vector_grads[7],
        mask_gradient,
    )


def solution(mesh):
    placed = (
        P(None, "fsdp", "leaf", None),
        P(None, "fsdp", "leaf", None),
        P(None, "fsdp", None),
        P(None, "fsdp", None),
        P(None, "fsdp", None),
        P(),
        P("fsdp", None),
        P("fsdp"),
        P("fsdp"),
        P("fsdp", None),
        P("fsdp"),
        P("fsdp"),
        P("fsdp"),
        P("fsdp", None),
        P("fsdp"),
        P("fsdp", None),
        P("fsdp"),
        P("fsdp"),
        P("fsdp"),
    )
    return jax.shard_map(
        fast_device if mesh.shape["fsdp"] == 8 and mesh.shape["leaf"] == 4 else per_device,
        mesh=mesh,
        in_specs=placed,
        out_specs=(
            P(None, "fsdp", "leaf", None),
            P(None, "fsdp", "leaf", None),
            P("fsdp", None),
            P("fsdp"),
            P("fsdp"),
            P("fsdp", None),
            P("fsdp"),
            P("fsdp"),
            P("fsdp"),
            P("fsdp", None),
            P("fsdp"),
            P("fsdp", None),
            P("fsdp"),
            P("fsdp"),
            P("fsdp"),
            P(None, "fsdp", None),
        ),
        check_vma=False,
    )
```

```python
import functools
import math

import jax
import jax.numpy as jnp
from jax import lax
from jax.experimental import pallas as pl
from jax.experimental.pallas import tpu as pltpu
from jax.sharding import PartitionSpec as P

EPSILON = 1e-05
F32 = jnp.float32
BF = jnp.bfloat16
TRUNK = 4
GROUPS = 4
CORES = 2
LOW_HALF = 64


def layer_norm(values, gain_vec, shift_vec):
    average = jnp.mean(values, axis=-1, keepdims=True)
    centred = values - average
    inv_scale = lax.rsqrt(jnp.mean(centred * centred, axis=-1, keepdims=True) + EPSILON)
    normed = centred * inv_scale
    return (normed * gain_vec + shift_vec, normed, inv_scale)


def norm_backward(upstream, normed, inv_scale, gain_vec):
    scaled = upstream * gain_vec
    inner_term = (
        scaled
        - jnp.mean(scaled, axis=-1, keepdims=True)
        - normed * jnp.mean(scaled * normed, axis=-1, keepdims=True)
    )
    return (inv_scale * inner_term, jnp.sum(upstream * normed, axis=0), jnp.sum(upstream, axis=0))


def gelu_parts(values):
    cdf = 0.5 * (1.0 + lax.erf(values / math.sqrt(2.0)))
    density = jnp.exp(-0.5 * values * values) / math.sqrt(2.0 * math.pi)
    return (values * cdf, cdf + values * density)


def dot_nn(left, right):
    return jnp.dot(left, right, preferred_element_type=F32)


def dot_nt(left, right):
    return lax.dot_general(left, right, (((1,), (1,)), ((), ())), preferred_element_type=F32)


def dot_tn(left, right):
    return lax.dot_general(left, right, (((0,), (0,)), ((), ())), preferred_element_type=F32)


def tree_order(parent):
    count = parent.shape[0]
    ids = jnp.arange(count, dtype=jnp.int32)
    up = (parent[:, None] == ids[None, :]) & (ids[:, None] != ids[None, :])
    up = up.astype(F32)
    reach = up
    power = up
    for _ in range(TRUNK + 1):
        power = jnp.sum(power[:, :, None] * up[None, :, :], axis=1)
        reach = reach + power
    depth = jnp.sum(reach, axis=1)
    before = (ids[None, :] < ids[:, None]).astype(F32)
    branch = (depth == TRUNK).astype(F32)
    rank = jnp.sum(before * branch[None, :], axis=1)
    own_rank = jnp.where(depth == TRUNK, rank, jnp.sum(up * rank[None, :], axis=1))
    siblings = jnp.sum(up[:, None, :] * up[None, :, :], axis=2) * before
    second = jnp.sum(siblings, axis=1)
    within = jnp.where(depth == TRUNK, 1.0, 2.0 * second)
    place = jnp.where(depth < TRUNK, depth, TRUNK + 3.0 * own_rank + within).astype(jnp.int32)
    order = jnp.sum((place[:, None] == ids[None, :]) * ids[:, None], axis=0).astype(jnp.int32)
    return (order, place)


def low_lanes():
    return lax.broadcasted_iota(jnp.int32, (1, 2 * LOW_HALF), 1) < LOW_HALF


def one_head(pair, which):
    keep = low_lanes() if which == 0 else jnp.logical_not(low_lanes())
    return jnp.where(keep, pair, jnp.zeros_like(pair))


def group_columns(row, block):
    return ((0, 2 * block, (1, 0)), (0, 3 * block, (1, 0, 1)), (block, 2 * block, (0, 1)))[row]


def mask_columns(mask_rows, tiles, block):
    return jnp.concatenate([mask_rows[:, t * block : (t + 1) * block] for t in tiles], axis=1)


def attend_kernel(block, query_ref, key_ref, value_ref, mask_ref, out_ref, log_ref):
    trunk = TRUNK * block
    wide = 3 * block
    low = low_lanes()

    def soften(parts, masks, values):
        top = parts[0].max(axis=1, keepdims=True)
        for part in parts[1:]:
            top = jnp.maximum(top, part.max(axis=1, keepdims=True))
        total = 0.0
        out = 0.0
        for part, mask, value in zip(parts, masks, values):
            weight = jnp.exp(part - top)
            total = total + weight.sum(axis=1, keepdims=True)
            out = out + dot_nn((weight * mask.astype(F32)).astype(BF), value)
        return (out * (1.0 / total), top + jnp.log(total))

    def emit(rows, results):
        count = results[0][1].shape[0]
        out_ref[rows, :] = jnp.where(low, results[0][0], results[1][0]).astype(BF)
        logs = [jnp.broadcast_to(result[1], (count, 2 * LOW_HALF)) for result in results]
        log_ref[rows, :] = jnp.where(low, logs[0], logs[1])

    def trunk_rows(index, carry):
        rows = pl.ds(pl.multiple_of(index * block, block), block)
        query = query_ref[rows, :]
        results = []
        for which in range(2):
            mask_rows = mask_ref[which, rows, :]
            columns = [(0, trunk, mask_rows)]
            side = mask_columns(mask_rows, (1, 0, 1), block)
            columns += [(trunk + wide * g, wide, side) for g in range(GROUPS)]
            head = one_head(query, which)
            parts = [dot_nt(head, key_ref[c : c + w, :]) for c, w, _ in columns]
            values = [value_ref[c : c + w, :] for c, w, _ in columns]
            results.append(soften(parts, [column[2] for column in columns], values))
        emit(rows, results)
        return carry

    lax.fori_loop(0, TRUNK, trunk_rows, 0)

    def group_rows(group, carry):
        base = pl.multiple_of(trunk + wide * group, block)
        for row in range(3):
            rows = pl.ds(pl.multiple_of(base + block * row, block), block)
            query = query_ref[rows, :]
            tile = 0 if row == 1 else 1
            start, width, tiles = group_columns(row, block)
            columns = pl.ds(pl.multiple_of(base + start, block), width)
            results = []
            for which in range(2):
                mask_rows = mask_ref[which, tile * block : (tile + 1) * block, :]
                head = one_head(query, which)
                parts = [dot_nt(head, key_ref[0:trunk, :]), dot_nt(head, key_ref[columns, :])]
                masks = [mask_rows, mask_columns(mask_rows, tiles, block)]
                values = [value_ref[0:trunk, :], value_ref[columns, :]]
                results.append(soften(parts, masks, values))
            emit(rows, results)
        return carry

    lax.fori_loop(0, GROUPS, group_rows, 0)


def attend(query, key, value, mask, block):
    rows, width = query.shape
    pairs = width // (2 * LOW_HALF)
    span = mask.shape[1]
    spec = pl.BlockSpec((rows, 2 * LOW_HALF), lambda p: (0, p))
    return pl.pallas_call(
        functools.partial(attend_kernel, block),
        grid=(pairs,),
        name="attend",
        in_specs=[spec, spec, spec, pl.BlockSpec((2, span, span), lambda p: (p, 0, 0))],
        out_specs=[spec, spec],
        out_shape=[
            jax.ShapeDtypeStruct((rows, width), BF),
            jax.ShapeDtypeStruct((rows, width), F32),
        ],
        compiler_params=pltpu.CompilerParams(vmem_limit_bytes=48 << 20),
    )(query, key, value, mask)


def attend_back_kernel(
    block,
    scale,
    query_ref,
    key_ref,
    value_ref,
    mask_ref,
    out_ref,
    log_ref,
    delta_ref,
    dquery_ref,
    dkey_ref,
    dvalue_ref,
    dmask_ref,
    key_sum,
    value_sum,
    query_turned,
    delta_turned,
):
    trunk = TRUNK * block
    wide = 3 * block
    low = low_lanes()
    key_sum[...] = jnp.zeros_like(key_sum)
    value_sum[...] = jnp.zeros_like(value_sum)
    dmask_ref[...] = jnp.zeros_like(dmask_ref)
    query_turned[...] = query_ref[...].astype(F32).T.astype(BF)
    delta_turned[...] = delta_ref[...].astype(F32).T.astype(BF)

    def work(rows, mask_place, columns):
        query = query_ref[rows, :]
        delta = delta_ref[rows, :]
        product = delta.astype(F32) * out_ref[rows, :].astype(F32)
        logs = log_ref[rows, :]
        dqueries = []
        for which in range(2):
            first = LOW_HALF * which
            lanes = slice(first, first + LOW_HALF)
            query_head = one_head(query, which)
            delta_head = one_head(delta, which)
            log = logs[:, first : first + 1]
            row_term = jnp.sum(product[:, lanes], axis=1, keepdims=True)
            mask_rows = mask_ref[which, mask_place, :]
            dquery = 0.0
            for place, tiles in columns:
                key = key_ref[place, :]
                value = value_ref[place, :]
                probs = jnp.exp(dot_nt(query_head, key) - log)
                pair = dot_nt(delta_head, value) * probs
                mask = mask_rows if tiles is None else mask_columns(mask_rows, tiles, block)
                mask = mask.astype(F32)
                if tiles is None:
                    dmask_ref[which, mask_place, :] += pair
                else:
                    for tile in sorted(set(tiles)):
                        dmask_ref[which, mask_place, tile * block : (tile + 1) * block] += sum(
                            pair[:, a * block : (a + 1) * block]
                            for a, t in enumerate(tiles)
                            if t == tile
                        )
                dscores = (pair * mask - probs * row_term).astype(BF)
                weights = (probs * mask).astype(BF)
                dquery = dquery + dot_nn(dscores, key)
                key_sum[lanes, place] += dot_nn(query_turned[lanes, rows], dscores)
                value_sum[lanes, place] += dot_nn(delta_turned[lanes, rows], weights)
            dqueries.append(dquery)
        dquery_ref[rows, :] = (jnp.where(low, dqueries[0], dqueries[1]) * scale).astype(BF)

    def trunk_rows(index, carry):
        rows = pl.ds(pl.multiple_of(index * block, block), block)
        columns = [(pl.ds(0, trunk), None)]
        columns += [(pl.ds(trunk + wide * g, wide), (1, 0, 1)) for g in range(GROUPS)]
        work(rows, rows, columns)
        return carry

    lax.fori_loop(0, TRUNK, trunk_rows, 0)

    def group_rows(group, carry):
        base = pl.multiple_of(trunk + wide * group, block)
        for row in range(3):
            rows = pl.ds(pl.multiple_of(base + block * row, block), block)
            tile = 0 if row == 1 else 1
            start, width, tiles = group_columns(row, block)
            near = pl.ds(pl.multiple_of(base + start, block), width)
            work(rows, pl.ds(tile * block, block), [(pl.ds(0, trunk), None), (near, tiles)])
        return carry

    lax.fori_loop(0, GROUPS, group_rows, 0)
    dkey_ref[...] = key_sum[...].T.astype(BF)
    dvalue_ref[...] = value_sum[...].T.astype(BF)


def attend_back(query, key, value, mask, out, logs, delta, block, scale):
    rows, width = query.shape
    pair_width = 2 * LOW_HALF
    pairs = width // pair_width
    span = mask.shape[1]
    spec = pl.BlockSpec((rows, pair_width), lambda p: (0, p))
    mask_spec = pl.BlockSpec((2, span, span), lambda p: (p, 0, 0))
    return pl.pallas_call(
        functools.partial(attend_back_kernel, block, scale),
        grid=(pairs,),
        name="attend_back",
        in_specs=[spec, spec, spec, mask_spec, spec, spec, spec],
        out_specs=[spec, spec, spec, mask_spec],
        out_shape=[jax.ShapeDtypeStruct((rows, width), BF)] * 3
        + [jax.ShapeDtypeStruct(mask.shape, F32)],
        scratch_shapes=[
            pltpu.VMEM((pair_width, rows), F32),
            pltpu.VMEM((pair_width, rows), F32),
            pltpu.VMEM((pair_width, rows), BF),
            pltpu.VMEM((pair_width, rows), BF),
        ],
        compiler_params=pltpu.CompilerParams(vmem_limit_bytes=48 << 20),
    )(query, key, value, mask, out, logs, delta)


def reorder_kernel(order_ref, source_ref, target_ref):
    target_ref[...] = source_ref[...]


def reorder(tokens, order):
    count, block, width = tokens.shape
    return pl.pallas_call(
        reorder_kernel,
        name="reorder",
        grid_spec=pltpu.PrefetchScalarGridSpec(
            num_scalar_prefetch=1,
            grid=(count,),
            in_specs=[pl.BlockSpec((1, block, width), lambda i, order_ref: (order_ref[i], 0, 0))],
            out_specs=pl.BlockSpec((1, block, width), lambda i, order_ref: (i, 0, 0)),
        ),
        out_shape=jax.ShapeDtypeStruct(tokens.shape, tokens.dtype),
    )(order, tokens)


MESH = pl.DeviceIdType.MESH
ANY = pl.BlockSpec(memory_space=pl.ANY)
VMEM = pl.BlockSpec(memory_space=pltpu.VMEM)
SMEM = pl.BlockSpec(memory_space=pltpu.SMEM)
VMEM_LIMIT = 62 << 20
LINE = 4
ALL = slice(None)


class Net:
    def __init__(self, send, recv, local):
        leaf, shard = lax.axis_index("leaf"), lax.axis_index("fsdp")
        self.leaf, self.shard = leaf, shard
        self.x, self.c = leaf // 2, leaf % 2
        self.z, self.y = shard // 2, shard % 2
        self.send, self.recv, self.local = send, recv, local

    def near(self, which):
        x, c, y, z = self.x, self.c, self.y, self.z
        if which == "x":
            x = 1 - x
        elif which == "c":
            c = 1 - c
        elif which == "xc":
            x, c = 1 - x, 1 - c
        elif which == "y":
            y = 1 - y
        else:
            z = (z + which) % LINE
        return (x * 2 + c, z * 2 + y)

    def greet(self, peers):
        barrier = pltpu.get_barrier_semaphore()
        for peer in peers:
            pl.semaphore_signal(barrier, inc=1, device_id=self.near(peer), device_id_type=MESH)
        pl.semaphore_wait(barrier, len(peers))

    def remote(self, row, slot, source, target, peer):
        return pltpu.make_async_remote_copy(
            src_ref=source,
            dst_ref=target,
            send_sem=self.send.at[row, slot],
            recv_sem=self.recv.at[row, slot],
            device_id=self.near(peer),
            device_id_type=MESH,
        )

    def stay(self, row, source, target):
        return pltpu.make_async_copy(source, target, self.local.at[row])


class Gather:
    def __init__(self, net, row, own, whole, share, split=2):
        self.net, self.row, self.own, self.whole, self.share = net, row, own, whole, share
        self.split = split

    def copy(self, slot):
        net, whole = self.net, self.whole
        x, y, z = net.x, net.y, net.z
        if slot < 3:
            return net.remote(self.row, slot, self.own(x), whole(z, y, x), slot + 1)
        if slot < 6:
            piece = whole((z + LINE - (slot - 2)) % LINE, y, x)
            return net.remote(self.row, slot, piece, piece, "x")
        if slot == 6:
            piece, peer = whole(ALL, y, x), "y"
        elif slot == 7:
            piece, peer = whole(slice(0, self.split), 1 - y, x), "x"
        elif slot == 8:
            piece, peer = whole(slice(self.split, 4), y, 1 - x), "y"
        else:
            piece, peer = whole(ALL, ALL, ALL), "c"
        return net.remote(self.row, slot, piece, piece, peer)

    def home(self):
        return self.net.stay(self.row, self.own(ALL), self.whole(self.net.z, self.net.y, ALL))

    def step(self, number):
        if number == 0:
            self.home().start()
            for slot in range(3):
                self.copy(slot).start()
        elif number == 1:
            self.home().wait()
            for slot in range(3):
                self.copy(slot).wait_recv()
            for slot in range(3, 7):
                self.copy(slot).start()
        elif number == 2:
            for slot in range(3, 7):
                self.copy(slot).wait_recv()
            for slot in (7, 8):
                self.copy(slot).start()
        elif number == 3:
            for slot in (7, 8):
                self.copy(slot).wait_recv()
            if self.share:
                self.copy(9).start()
        elif number == 4:
            if self.share:
                self.copy(9).wait_recv()

    def finish(self):
        for slot in range(10 if self.share else 9):
            self.copy(slot).wait_send()


class Scatter:
    def __init__(self, net, row, load, part, twin, twin_load, first, second, third, final):
        self.net, self.row, self.load, self.part = net, row, load, part
        self.twin, self.twin_load = twin, twin_load
        self.first, self.second, self.third, self.final = first, second, third, final

    def copy(self, slot):
        net, part = self.net, self.part
        x, y, z, c = net.x, net.y, net.z, net.c
        if slot == 0:
            return net.remote(self.row, slot, self.twin_load, self.twin, "c")
        if slot == 1:
            return net.remote(self.row, slot, part.at[0:1, 1 - y, 1 - x], self.first.at[0:1], "x")
        if slot == 2:
            return net.remote(self.row, slot, part.at[1:4, 1 - y, 1 - x], self.first.at[1:4], "y")
        if slot == 3:
            return net.remote(self.row, slot, part.at[:, y, 1 - x], self.second.at[0], "x")
        if slot == 4:
            return net.remote(self.row, slot, part.at[:, 1 - y, x], self.second.at[1], "y")
        if slot < 8:
            step = slot - 4
            piece = part.at[(z + step) % LINE, y, x]
            return net.remote(self.row, slot, piece, self.third.at[step - 1], step)
        if slot < 10:
            return net.remote(self.row, slot, part.at[z, y, x], self.final(x, c), "xc"[slot - 8])
        piece = self.final(1 - x, c)
        return net.remote(self.row, slot, piece, piece, "c")

    def home(self):
        return self.net.stay(self.row, self.load, self.part)

    def keep(self):
        net = self.net
        piece = self.part.at[net.z, net.y, net.x]
        return net.stay(self.row, piece, self.final(net.x, net.c))

    def step(self, number):
        net, part = self.net, self.part
        x, y, z = net.x, net.y, net.z
        if number == 0:
            if self.load is not None:
                self.home().start()
            if self.twin is not None:
                self.copy(0).start()
        elif number == 1:
            if self.load is not None:
                self.home().wait()
            if self.twin is not None:
                self.copy(0).wait_recv()
                for a in range(LINE):
                    part[a] = part[a] + self.twin[a]
            self.copy(1).start()
            self.copy(2).start()
        elif number == 2:
            self.copy(1).wait_recv()
            part[0, 1 - y, x] = part[0, 1 - y, x] + self.first[0]
            self.copy(2).wait_recv()
            part[1:4, y, 1 - x] = part[1:4, y, 1 - x] + self.first[1:4]
            self.copy(3).start()
            self.copy(4).start()
        elif number == 3:
            self.copy(3).wait_recv()
            self.copy(4).wait_recv()
            mine = part[:, y, x].astype(F32) + self.second[0].astype(F32)
            part[:, y, x] = (mine + self.second[1].astype(F32)).astype(BF)
            for slot in (5, 6, 7):
                self.copy(slot).start()
        elif number == 4:
            total = part[z, y, x].astype(F32)
            for slot in (5, 6, 7):
                self.copy(slot).wait_recv()
                total = total + self.third[slot - 5].astype(F32)
            part[z, y, x] = total.astype(BF)
            for slot in (8, 9):
                self.copy(slot).start()
            self.keep().start()
        elif number == 5:
            self.keep().wait()
            self.copy(8).wait_recv()
            self.copy(10).start()
        elif number == 6:
            for slot in (9, 10):
                self.copy(slot).wait_recv()

    def finish(self):
        for slot in range(0 if self.twin is not None else 1, 11):
            self.copy(slot).wait_send()


def copy_semaphores(rows, slots):
    return [
        pltpu.SemaphoreType.DMA((rows, slots)),
        pltpu.SemaphoreType.DMA((rows, slots)),
        pltpu.SemaphoreType.DMA((rows,)),
    ]


def run_plan(plan, slot, total):
    for number in range(total):
        steps = [entry for entry in plan if int(entry[0]) == number]
        if steps:

            @pl.when(slot == number)
            def _(steps=steps):
                for _, chunk, step in steps:
                    chunk.step(step)


def run_rest(plan, total):
    for time, chunk, step in plan:
        if time >= total:
            chunk.step(step)


def pick_kernel(order_ref, low_ref, high_ref, out_ref, sems):
    count = low_ref.shape[0]
    for i in range(out_ref.shape[0]):
        at = order_ref[i]

        @pl.when(at < count)
        def _(i=i, at=at):
            pltpu.make_async_copy(low_ref.at[at], out_ref.at[i], sems.at[i]).start()

        @pl.when(at >= count)
        def _(i=i, at=at):
            pltpu.make_async_copy(high_ref.at[at - count], out_ref.at[i], sems.at[i]).start()

    for i in range(out_ref.shape[0]):
        pltpu.make_async_copy(low_ref.at[0], out_ref.at[i], sems.at[i]).wait()


def pick(order, low, high):
    count = order.shape[0]
    return pl.pallas_call(
        pick_kernel,
        name="pick",
        in_specs=[SMEM, ANY, ANY],
        out_specs=VMEM,
        out_shape=jax.ShapeDtypeStruct((count,) + low.shape[1:], low.dtype),
        scratch_shapes=[pltpu.SemaphoreType.DMA((count,))],
        compiler_params=pltpu.CompilerParams(vmem_limit_bytes=VMEM_LIMIT),
    )(order, low, high)


class Sharing:
    def __init__(self, net, row, own, tree, stage=None):
        self.net, self.row, self.own, self.tree, self.stage = net, row, own, tree, stage

    def copy(self, slot):
        net, own, tree = self.net, self.own, self.tree
        count = own.shape[1]
        half = count // 2
        part = pl.ds((slot % 2) * half, half)
        place = tree.at[pl.ds(net.leaf * count + (slot % 2) * half, half)]
        if slot < 2:
            return net.remote(self.row, slot, own.at[1 - net.x, part], place, "x")
        if slot < 4:
            return net.remote(self.row, slot, own.at[net.x, part], place, "c")
        place = tree.at[pl.ds((net.leaf + 2) % 4 * count + (slot % 2) * half, half)]
        return net.remote(self.row, slot, place, place, "c")

    def home(self):
        count = self.own.shape[1]
        source = self.own.at[self.net.x] if self.stage is None else self.stage
        return self.net.stay(self.row, source, self.tree.at[pl.ds(self.net.leaf * count, count)])

    def load(self):
        return self.net.stay(self.row + 1, self.own.at[self.net.x], self.stage)

    def step(self, number):
        if number == 0:
            for slot in range(4):
                self.copy(slot).start()
            if self.stage is not None:
                self.load().wait()
            self.home().start()
        elif number < 3:
            self.copy(number - 1).wait_recv()
            self.copy(number + 3).start()
        elif number == 3:
            for slot in (2, 3, 4, 5):
                self.copy(slot).wait_recv()
            self.home().wait()

    def finish(self):
        for slot in range(6):
            self.copy(slot).wait_send()


class Flush:
    def __init__(self, net, row, source, target):
        self.move = lambda: net.stay(row, source, target)

    def step(self, number):
        self.move().start()

    def finish(self):
        self.move().wait()


class WideGather(Gather):
    def copy(self, slot):
        net, whole = self.net, self.whole
        if slot < 3:
            piece = whole(net.z, net.y, ALL)
            return net.remote(self.row, slot, self.own(ALL), piece, slot + 1)
        if slot == 3:
            piece, peer = whole(ALL, net.y, ALL), "y"
        else:
            piece, peer = whole(ALL, ALL, ALL), "c"
        return net.remote(self.row, slot, piece, piece, peer)

    def step(self, number):
        if number == 0:
            self.home().start()
            for slot in range(3):
                self.copy(slot).start()
        elif number == 1:
            self.home().wait()
            for slot in range(3):
                self.copy(slot).wait_recv()
            self.copy(3).start()
        elif number == 2:
            self.copy(3).wait_recv()
            if self.share:
                self.copy(4).start()
        elif number == 4:
            if self.share:
                self.copy(4).wait_recv()

    def finish(self):
        for slot in range(5 if self.share else 4):
            self.copy(slot).wait_send()


class FarGather(Gather):
    def __init__(self, net, row, own, whole, share, split, stage, spare):
        super().__init__(net, row, own, whole, share, split)
        self.stage, self.spare = stage, spare

    def load(self):
        return self.net.stay(self.spare, self.own(ALL), self.stage)

    def home(self):
        return self.net.stay(self.row, self.stage, self.whole(self.net.z, self.net.y, ALL))

    def step(self, number):
        if number == 0:
            self.load().wait()
        super().step(number)


FRONT = dict(
    pace=4.4,
    lead=5.0,
    lag1=9.0,
    lag2=11.0,
    lag3=11.0,
    lag4=8.0,
    origin=34.0,
    join=1.0,
    attend=1.55,
    norm=0.7,
    rise=1.0,
    splits=(2,),
    wide=(),
    upstream=(60.0, 72.0, 80.0, 90.0),
)


def front_kernel(
    block,
    order_ref,
    entry_ref,
    upstream_ref,
    joined_shard,
    scores_ref,
    jitter_ref,
    scale_ref,
    out_shard,
    up_shard,
    down_shard,
    vectors_ref,
    tokens_out,
    joined_out,
    query_out,
    key_out,
    value_out,
    mask_out,
    attended_out,
    log_out,
    whole_out,
    out_out,
    up_out,
    down_out,
    tree_out,
    normed_out,
    inv_out,
    active_out,
    slope_out,
    small_out,
    rise_bias_out,
    entry_tree,
    tokens_ref,
    joined_weight,
    query_ref,
    key_ref,
    value_ref,
    mask_ref,
    attended_ref,
    log_ref,
    whole_ref,
    out_weight,
    up_weight,
    normed_ref,
    low_ref,
    active_ref,
    slope_ref,
    packed_ref,
    down_stage,
    upstream_stage,
    scores_own,
    jitter_own,
    relaxed_ref,
    *sems,
):
    net = Net(*sems)
    c, y, z = net.c, net.y, net.z
    trunk = TRUNK * block
    wide = 3 * block
    low = low_lanes()
    rows_all, mine = query_ref.shape
    width = tokens_ref.shape[2]
    blocks = tokens_ref.shape[0]
    pairs = mine // (2 * LOW_HALF)
    heads = relaxed_ref.shape[0]
    half = rows_all // 2
    expand = up_weight.shape[4]
    splits = FRONT["splits"]
    chunks = []

    def add(own, whole, share):
        split = splits[len(chunks) % len(splits)]
        kind = WideGather if len(chunks) in FRONT["wide"] else Gather
        chunks.append(kind(net, len(chunks), own, whole, share, split))

    def columns(index):
        return pl.ds(pl.multiple_of(index * mine, mine), mine)

    for i in range(3):
        add(
            lambda part, i=i: joined_shard.at[part, :, columns(2 * i + c)],
            lambda a, b, part, i=i: joined_weight.at[a, b, part, :, columns(i)],
            False,
        )
    for h in range(heads):
        add(
            lambda part, h=h: relaxed_ref.at[h, part],
            lambda a, b, part, h=h: mask_ref.at[h, a, b, part],
            False,
        )
    add(
        lambda part: out_shard.at[part, :, columns(c)],
        lambda a, b, part: out_weight.at[a, b, part, :, columns(c)],
        True,
    )
    for j in range(4):
        add(
            lambda part, j=j: up_shard.at[part, :, columns(4 * c + j)],
            lambda a, b, part, j=j: up_weight.at[a, b, part, :, columns(4 * c + j)],
            True,
        )
    spare = len(chunks) + 4
    for j in range(4):
        chunks.append(
            FarGather(
                net,
                len(chunks),
                lambda part, j=j: down_shard.at[j, part, :, columns(c)],
                lambda a, b, part, j=j: down_out.at[a, b, j, part, :, columns(c)],
                True,
                splits[len(chunks) % len(splits)],
                down_stage.at[j],
                spare + j,
            )
        )
    spare += 4
    entry = Sharing(net, spare, entry_ref, entry_tree)
    upstream = Sharing(net, spare + 1, upstream_ref, tree_out, upstream_stage)
    vector_row = spare + 3
    flushes = []
    first_flush = spare + 4

    def flush(source, target):
        flushes.append(Flush(net, first_flush + len(flushes), source, target))
        return flushes[-1]

    def vector_copy(slot):
        if slot < 3:
            return net.remote(vector_row, slot, vectors_ref, packed_ref.at[z, y], slot + 1)
        return net.remote(vector_row, slot, packed_ref.at[:, y], packed_ref.at[:, y], "y")

    class Vectors:
        def home(self):
            return net.stay(vector_row, vectors_ref, packed_ref.at[z, y])

        def step(self, number):
            if number == 0:
                self.home().start()
                for slot in range(3):
                    vector_copy(slot).start()
            elif number == 1:
                self.home().wait()
                for slot in range(3):
                    vector_copy(slot).wait_recv()
                vector_copy(3).start()
            elif number == 2:
                vector_copy(3).wait_recv()

        def finish(self):
            for slot in range(4):
                vector_copy(slot).wait_send()

    vectors = Vectors()
    net.greet(("x", "c", "y", 1, 2, 3))
    for chunk in chunks[-4:]:
        chunk.load().start()
    upstream.load().start()
    own_heads = pl.ds(c * heads, heads)
    mask_loads = [
        net.stay(first_flush + 16, scores_ref.at[own_heads], scores_own),
        net.stay(first_flush + 17, jitter_ref.at[own_heads], jitter_own),
    ]
    for load in mask_loads:
        load.start()

    starts = []
    time = FRONT["origin"]
    for count, length in (
        (blocks // 2, FRONT["join"]),
        (8 * pairs, FRONT["attend"]),
        (half // block, FRONT["norm"]),
        (2 * (expand // mine), FRONT["rise"]),
    ):
        for _ in range(count):
            starts.append(time)
            time += length
    total = len(starts)
    first_attend = blocks // 2
    first_norm = first_attend + 8 * pairs
    first_rise = first_norm + half // block

    plan = []
    for i, chunk in enumerate(chunks):
        start = i * FRONT["pace"]
        limit = 1e9
        if i < 3:
            limit = starts[0]
        elif i < 3 + heads:
            limit = starts[first_attend + 8 * ((i - 3) // 2)]
        elif i == 3 + heads:
            limit = starts[first_norm]
        elif i < 8 + heads:
            limit = starts[first_rise + 4 * (i - 4 - heads)]
        moments = [max(0.0, start - FRONT["lead"]), start + FRONT["lag1"]]
        for lag in ("lag2", "lag3", "lag4"):
            moments.append(moments[-1] + FRONT[lag])
        for step, moment in enumerate(moments):
            plan.append((min(moment, limit - 0.001 * (6 - step)), chunk, step))
    for step, moment in enumerate((0.0, 14.0, 24.0, 30.0)):
        plan.append((min(moment, starts[0] - 0.001), entry, step))
    for step, moment in enumerate((0.1, 9.0, 20.0)):
        plan.append((min(moment, starts[0] - 0.001), vectors, step))
    for step, moment in enumerate(FRONT["upstream"]):
        plan.append((moment, upstream, step))
    after = starts[first_attend] + 0.5
    plan.append((after, flush(joined_weight, joined_out), 0))
    plan.append((after + 2, flush(tokens_ref, tokens_out), 0))
    plan.append((after + 6, flush(query_ref, query_out), 0))
    plan.append((after + 8, flush(key_ref, key_out), 0))
    plan.append((after + 10, flush(value_ref, value_out), 0))
    plan.append((starts[first_attend + 16] + 0.1, flush(mask_ref, mask_out), 0))
    plan.append((starts[first_norm], flush(attended_ref, attended_out), 0))
    plan.append((starts[first_norm], flush(log_ref, log_out), 0))
    plan.append((starts[first_norm], flush(whole_ref, whole_out), 0))
    plan.append((starts[first_norm] + 0.1, flush(out_weight, out_out), 0))
    plan.append((starts[-4] + 0.01, flush(up_weight, up_out), 0))
    plan.append((starts[first_rise] + 1, flush(normed_ref, normed_out), 0))
    plan.sort(key=lambda item: item[0])
    placed = []
    for moment, item, step in plan:
        slot = next((s for s in range(total) if starts[s] > moment), total)
        slot = -1 if moment < starts[0] else max(slot - 1, 0)
        if moment >= starts[-1] + FRONT["rise"]:
            slot = total
        placed.append((slot, item, step))

    def events(slot, first, last, kinds=None):
        for number in range(first, last):
            if kinds is not None and (number - first) % 8 not in kinds:
                continue
            steps = [entry for entry in placed if entry[0] == number]
            if steps:

                @pl.when(slot == number)
                def _(steps=steps):
                    for _, item, step in steps:
                        item.step(step)

    early = [entry for entry in plan if entry[0] < 0.5]
    for _, item, step in early:
        item.step(step)
    for load in mask_loads:
        load.wait()

    def relax(h, carry):
        soft = jax.nn.sigmoid((scores_own[h] + jitter_own[h]) / scale_ref[c * heads + h])
        relaxed_ref[h] = soft.astype(BF).reshape(relaxed_ref.shape[1:])
        return carry

    lax.fori_loop(0, heads, relax, 0)
    for slot, item, step in placed[len(early) :]:
        if slot < 0:
            item.step(step)

    shard = width // 8
    lane = lax.broadcasted_iota(jnp.int32, (128, width), 1)
    line = lax.broadcasted_iota(jnp.int32, (128, width), 0)
    assembled = jnp.zeros((16, width), F32)
    for f in range(8):
        place = jnp.where((lane == line + shard * f) & (line < shard), 1.0, 0.0).astype(BF)
        assembled = assembled + dot_nn(packed_ref[f // 2, f % 2], place)
        for m in range(3):
            at = (f * 3 + m) * 128
            rise_bias_out[0:1, at : at + 128] = packed_ref[f // 2, f % 2, 8 + m : 9 + m, :].astype(F32)
    small_out[...] = assembled

    def project(i, carry):
        events(i, 0, first_attend)
        tokens_ref[2 * i] = entry_tree[order_ref[2 * i]]
        tokens_ref[2 * i + 1] = entry_tree[order_ref[2 * i + 1]]
        rows = pl.ds(pl.multiple_of(2 * block * i, 2 * block), 2 * block)
        pair = tokens_ref[pl.ds(2 * i, 2)].reshape(2 * block, width)
        joined = dot_nn(pair, joined_weight[...].reshape(width, 3 * mine))
        query = (joined[:, :mine] + small_out[0:1, columns(c)]).astype(BF).astype(F32)
        query_ref[rows, :] = (query * (1.0 / math.sqrt(LOW_HALF))).astype(BF)
        key_ref[rows, :] = joined[:, mine : 2 * mine].astype(BF)
        value_ref[rows, :] = (joined[:, 2 * mine :] + small_out[1:2, columns(c)]).astype(BF)
        return carry

    lax.fori_loop(0, blocks // 2, project, 0)

    def soften(parts, masks, values):
        top = parts[0].max(axis=1, keepdims=True)
        for part in parts[1:]:
            top = jnp.maximum(top, part.max(axis=1, keepdims=True))
        scale = 0.0
        out = 0.0
        for part, mask, value in zip(parts, masks, values):
            weight = jnp.exp(part - top)
            scale = scale + weight.sum(axis=1, keepdims=True)
            out = out + dot_nn((weight * mask.astype(F32)).astype(BF), value)
        return (out * (1.0 / scale), top + jnp.log(scale))

    def emit(rows, p, lanes, results):
        attended_ref[rows, lanes] = jnp.where(low, results[0][0], results[1][0]).astype(BF)
        logs = log_ref[rows, :]
        for which in range(2):
            logs = jnp.where(lane_row == 2 * p + which, results[which][1], logs)
        log_ref[rows, :] = logs

    lane_row = lax.broadcasted_iota(jnp.int32, (1, 128), 1)
    log_ref[...] = jnp.zeros_like(log_ref)

    def one_pair(p, carry):
        lanes = pl.ds(pl.multiple_of(p * 2 * LOW_HALF, 2 * LOW_HALF), 2 * LOW_HALF)

        def mask_strip(which, tile):
            return mask_ref[2 * p + which, tile].reshape(block, mask_ref.shape[-1])

        def trunk_rows(index, carry):
            for part_slot in range(2):
                slot = first_attend + 8 * p + 2 * index + part_slot
                events(slot, first_attend, first_norm, range(part_slot, 4, 2))
            rows = pl.ds(pl.multiple_of(index * 2 * block, 2 * block), 2 * block)
            query = query_ref[rows, lanes]
            results = []
            for which in range(2):
                strips = [mask_strip(which, 2 * index + s) for s in range(2)]
                mask_rows = jnp.concatenate(strips, axis=0)
                places = [(0, trunk, mask_rows)]
                side = mask_columns(mask_rows, (1, 0, 1), block)
                places += [(trunk + wide * g, wide, side) for g in range(GROUPS)]
                head = one_head(query, which)
                parts = [dot_nt(head, key_ref[a : a + w, lanes]) for a, w, _ in places]
                values = [value_ref[a : a + w, lanes] for a, w, _ in places]
                results.append(soften(parts, [place[2] for place in places], values))
            emit(rows, p, lanes, results)
            return carry

        lax.fori_loop(0, TRUNK // 2, trunk_rows, 0)

        def group_rows(group, carry):
            events(first_attend + 8 * p + 4 + group, first_attend, first_norm, range(4, 8))
            base = pl.multiple_of(trunk + wide * group, block)
            rows = pl.ds(base, wide)
            query = query_ref[rows, lanes]
            results = []
            for which in range(2):
                strips = [mask_strip(which, t) for t in (1, 0, 1)]
                head = one_head(query, which)
                far = dot_nt(head, key_ref[0:trunk, lanes])
                top = far.max(axis=1, keepdims=True)
                near = []
                tops = []
                for row in range(3):
                    start, size, tiles = group_columns(row, block)
                    place = pl.ds(pl.multiple_of(base + start, block), size)
                    at = slice(row * block, (row + 1) * block)
                    part = dot_nt(head[at], key_ref[place, lanes])
                    near.append((part, place, mask_columns(strips[row], tiles, block)))
                    tops.append(jnp.maximum(top[at], part.max(axis=1, keepdims=True)))
                top = jnp.concatenate(tops, axis=0)
                weight = jnp.exp(far - top)
                mask_rows = jnp.concatenate(strips, axis=0).astype(F32)
                scale = weight.sum(axis=1, keepdims=True)
                out = dot_nn((weight * mask_rows).astype(BF), value_ref[0:trunk, lanes])
                scales = []
                outs = []
                for row, (part, place, mask) in enumerate(near):
                    weight = jnp.exp(part - tops[row])
                    scales.append(weight.sum(axis=1, keepdims=True))
                    weight = (weight * mask.astype(F32)).astype(BF)
                    outs.append(dot_nn(weight, value_ref[place, lanes]))
                scale = scale + jnp.concatenate(scales, axis=0)
                out = (out + jnp.concatenate(outs, axis=0)) * (1.0 / scale)
                results.append((out, top + jnp.log(scale)))
            emit(rows, p, lanes, results)
            return carry

        lax.fori_loop(0, GROUPS, group_rows, 0)
        return carry

    lax.fori_loop(0, pairs, one_pair, 0)
    mine_rows = pl.ds(pl.multiple_of(c * half, half), half)
    their_rows = pl.ds(pl.multiple_of((1 - c) * half, half), half)
    cross = net.remote(vector_row, 4, attended_ref.at[their_rows], whole_ref.at[:, columns(c)], "c")
    cross.start()
    whole_ref[:, columns(c)] = attended_ref[mine_rows, :]
    cross.wait_recv()

    def normalize(i, carry):
        events(first_norm + i, first_norm, first_rise)
        rows = pl.ds(pl.multiple_of(i * block, block), block)
        first = tokens_ref[c * (blocks // 2) + i].astype(F32) + small_out[2:3, :]
        first = first + dot_nn(whole_ref[rows, :], out_weight[...].reshape(width, width))
        average = jnp.mean(first, axis=1, keepdims=True)
        centred = first - average
        inv = lax.rsqrt(jnp.mean(centred * centred, axis=1, keepdims=True) + EPSILON)
        normed = centred * inv
        normed_ref[rows, :] = normed
        inv_out[rows, :] = jnp.broadcast_to(inv, (block, 128))
        low_ref[rows, :] = (normed * small_out[3:4, :] + small_out[4:5, :]).astype(BF)
        return carry

    lax.fori_loop(0, half // block, normalize, 0)
    per = expand // mine

    def rise_place(i):
        rows = pl.ds(pl.multiple_of((i % 2) * (half // 2), half // 2), half // 2)
        return rows, columns((per // 2) * (i // 2 % 2) + i // 4)

    def out_copies(i):
        row = first_flush + len(flushes)
        slot = i % 2
        rows, place = rise_place(i)
        return (
            net.stay(row + slot, active_ref.at[slot], active_out.at[rows, place]),
            net.stay(row + 2 + slot, slope_ref.at[slot], slope_out.at[rows, place]),
        )

    def rise(i, carry):
        events(first_rise + i, first_rise, total)
        rows, place = rise_place(i)
        upper = dot_nn(low_ref[rows, :], up_weight[:, :, :, :, place].reshape(width, mine))
        active, slope = gelu_parts(upper + rise_bias_out[0:1, place])

        @pl.when(i >= 2)
        def _():
            for copy in out_copies(i - 2):
                copy.wait()

        active_ref[i % 2] = active.astype(BF)
        slope_ref[i % 2] = slope.astype(BF)
        for copy in out_copies(i):
            copy.start()
        return carry

    lax.fori_loop(0, 2 * per, rise, 0)
    for slot, item, step in placed:
        if slot == total:
            item.step(step)
    for i in (2 * per - 2, 2 * per - 1):
        for copy in out_copies(i):
            copy.wait()
    for item in chunks + [entry, upstream, vectors] + flushes:
        item.finish()
    cross.wait_send()


def front(
    order, entry, upstream, joined, scores, jitter, scale, out_shard, up_shard, down_shard, vectors
):
    micro, own_blocks, block, width = entry.shape
    own_rows = own_blocks * block
    rows = 4 * own_rows
    half = rows // 2
    blocks = rows // block
    mine = width // CORES
    heads = scores.shape[0] // CORES
    strip, span = scores.shape[1:]
    expand = up_shard.shape[2]
    like = jax.ShapeDtypeStruct
    grown = lambda shard: (LINE, 2) + shard.shape
    joined_shape = (LINE, 2) + joined.shape[:2] + (3 * mine,)
    mask_shape = (heads, LINE, 2, 2, strip // 2, span)
    vmem = lambda shape, kind=BF: pltpu.VMEM(shape, kind)
    return pl.pallas_call(
        functools.partial(front_kernel, block),
        name="front",
        in_specs=[SMEM] + [ANY] * 5 + [SMEM] + [ANY] * 4,
        out_specs=[ANY] * 14 + [VMEM] + [ANY] * 2 + [VMEM] * 2,
        out_shape=[
            like((blocks, block, width), BF),
            like(joined_shape, BF),
            like((rows, mine), BF),
            like((rows, mine), BF),
            like((rows, mine), BF),
            like(mask_shape, BF),
            like((rows, mine), BF),
            like((rows, 128), F32),
            like((half, width), BF),
            like(grown(out_shard), BF),
            like(grown(up_shard), BF),
            like(grown(down_shard), BF),
            like((blocks, block, width), BF),
            like((half, width), F32),
            like((half, 128), F32),
            like((half, expand), BF),
            like((half, expand), BF),
            like((16, width), F32),
            like((1, expand), F32),
        ],
        scratch_shapes=[
            vmem((blocks, block, width)),
            vmem((blocks, block, width)),
            vmem(joined_shape),
            vmem((rows, mine)),
            vmem((rows, mine)),
            vmem((rows, mine)),
            vmem(mask_shape),
            vmem((rows, mine)),
            vmem((rows, 128), F32),
            vmem((half, width)),
            vmem(grown(out_shard)),
            vmem(grown(up_shard)),
            vmem((half, width), F32),
            vmem((half, width)),
            vmem((2, half // 2, mine)),
            vmem((2, half // 2, mine)),
            vmem((LINE, 2) + vectors.shape, vectors.dtype),
            vmem((4, 2, down_shard.shape[2], mine)),
            vmem(entry.shape[1:]),
            vmem((heads, strip, span), F32),
            vmem((heads, strip, span), F32),
            vmem((heads, 2, strip // 2, span)),
        ]
        + copy_semaphores(48, 10),
        compiler_params=pltpu.CompilerParams(
            collective_id=4, has_side_effects=True, vmem_limit_bytes=VMEM_LIMIT
        ),
    )(order, entry, upstream, joined, scores, jitter, scale, out_shard, up_shard, down_shard, vectors)


def scatter_buffers(count, shape, with_twin):
    half, columns = shape
    whole = pltpu.VMEM((count, LINE, 2, 2, half, columns), BF)
    line = pltpu.VMEM((count, LINE, half, columns), BF)
    return (
        [whole]
        + ([whole] if with_twin else [])
        + [
            line,
            pltpu.VMEM((count, 2, LINE, half, columns), BF),
            pltpu.VMEM((count, LINE - 1, half, columns), BF),
        ]
    )


REAR = dict(pace=4.0, lag=21.0, tail=4.5, attend=3.6, finish=5.0, spread=0.6)


def rear_kernel(
    block,
    scale,
    query_ref,
    key_ref,
    value_ref,
    mask_ref,
    out_ref,
    log_ref,
    joined_weight,
    small_ref,
    place_ref,
    delta_half,
    tokens_in,
    first_in,
    out_grad,
    up_grad,
    down_grad,
    layer_in,
    out_final,
    up_final,
    down_final,
    mask_final,
    joined_final,
    tokens_out,
    small_out,
    layer_out,
    delta_ref,
    key_sum,
    value_sum,
    query_turned,
    delta_turned,
    dmask_sum,
    dquery_ref,
    dkey_ref,
    dvalue_ref,
    tokens_ref,
    first_ref,
    part,
    first,
    second,
    third,
    joined_part,
    joined_first,
    joined_second,
    joined_third,
    mask_part,
    mask_first,
    mask_second,
    mask_third,
    give,
    keep,
    got,
    sums,
    from_peers,
    *sems,
):
    net = Net(*sems)
    x, c = net.x, net.c
    trunk = TRUNK * block
    wide = 3 * block
    low = low_lanes()
    lane = lax.broadcasted_iota(jnp.int32, (1, 128), 1)
    rows_all, mine = query_ref.shape
    blocks, _, width = tokens_ref.shape
    pairs = mine // (2 * LOW_HALF)
    heads = mask_ref.shape[0]
    half = rows_all // 2
    strip = mask_final.shape[3]
    chunks = []

    def own(index):
        return pl.ds(pl.multiple_of(index * mine, mine), mine)

    def dense(load, twin_load, final):
        k = len(chunks)
        twin = joined_part.at[k] if k < 3 else mask_part.at[k - 3, :, :, :, :, 0:mine]
        buffers = (first.at[k], second.at[k], third.at[k])
        chunks.append(Scatter(net, k, load, part.at[k], twin, twin_load, *buffers, final))

    dense(
        out_grad.at[:, :, :, :, own(c)],
        out_grad.at[:, :, :, :, own(1 - c)],
        lambda a, b: out_final.at[a, :, own(b)],
    )
    for j in range(4):
        dense(
            down_grad.at[:, :, j, :, :, own(c)],
            down_grad.at[:, :, j, :, :, own(1 - c)],
            lambda a, b, j=j: down_final.at[j, a, :, own(b)],
        )
    for j in range(4):
        dense(
            up_grad.at[:, :, :, :, own(4 * c + j)],
            up_grad.at[:, :, :, :, own(4 * (1 - c) + j)],
            lambda a, b, j=j: up_final.at[a, :, own(4 * b + j)],
        )
    dense_count = len(chunks)
    for p in range(pairs):
        for h in (2 * p, 2 * p + 1):
            buffers = (mask_first.at[h], mask_second.at[h], mask_third.at[h])
            chunks.append(
                Scatter(
                    net,
                    len(chunks),
                    None,
                    mask_part.at[h, :, :, :, 0:strip],
                    None,
                    None,
                    *buffers,
                    lambda a, b, h=h: mask_final.at[b, h, a],
                )
            )
        buffers = (joined_first.at[p], joined_second.at[p], joined_third.at[p])
        chunks.append(
            Scatter(
                net,
                len(chunks),
                None,
                joined_part.at[p],
                None,
                None,
                *buffers,
                lambda a, b, p=p: joined_final.at[p, a, b],
            )
        )
    spare = len(chunks)
    net.greet(("x", "c", "y", 1, 2, 3))

    mine_rows = pl.ds(pl.multiple_of(c * half, half), half)
    delta_cross = net.remote(spare, 0, delta_half.at[:, own(1 - c)], delta_ref.at[mine_rows], "c")
    delta_cross.start()
    delta_home = net.stay(spare, delta_half.at[:, own(c)], delta_ref.at[mine_rows])
    delta_home.start()
    tokens_load = net.stay(spare + 1, tokens_in, tokens_ref)
    first_load = net.stay(spare + 2, first_in, first_ref)
    tokens_load.start()
    own_blocks = blocks // 4
    layer_home = net.stay(spare + 3, layer_in.at[0:own_blocks], layer_out.at[x])
    layer_home.start()
    layer_cross = net.remote(spare, 3, layer_in.at[own_blocks:], layer_out.at[x], "x")
    layer_cross.start()

    own_rows = give.shape[1]
    per = own_rows // block

    def collect(target, core):
        for a in range(2):
            for b in range(per):
                place = place_ref[(2 * a + core) * per + b]
                target[a, b * block : (b + 1) * block] = tokens_ref[place]

    class Tokens:
        def core(self):
            return net.remote(spare, 1, give, got, "c")

        def chip(self):
            return net.remote(spare, 2, keep.at[1 - x], tokens_out.at[x], "x")

        def step(self, number):
            if number == 0:
                collect(give, 1 - c)
                self.core().start()
                collect(keep, c)
            elif number == 1:
                self.core().wait_recv()
                keep[...] = (keep[...].astype(F32) + got[...].astype(F32)).astype(BF)
                self.chip().start()
                tokens_out[x] = keep[x]
            elif number == 2:
                self.chip().wait_recv()

        def finish(self):
            self.core().wait_send()
            self.chip().wait_send()

    class Vectors:
        def copy(self, slot):
            peer = ("c", "x", "y", 1, 2, 3)[slot]
            source = sums.at[min(slot, 3)]
            return net.remote(spare + 1, slot, source, from_peers.at[slot], peer)

        def step(self, number):
            if number == 0:
                self.copy(0).start()
            elif number < 3:
                self.copy(number - 1).wait_recv()
                sums[number] = sums[number - 1] + from_peers[number - 1]
                self.copy(number).start()
            elif number == 3:
                self.copy(2).wait_recv()
                sums[3] = sums[2] + from_peers[2]
                for slot in (3, 4, 5):
                    self.copy(slot).start()
            elif number == 4:
                total = sums[3]
                for slot in (3, 4, 5):
                    self.copy(slot).wait_recv()
                    total = total + from_peers[slot]
                small_out[...] = total

        def finish(self):
            for slot in range(6):
                self.copy(slot).wait_send()

    home = Tokens()
    vectors = Vectors()
    starts = []
    ready = []
    time = 0.0
    for p in range(pairs):
        for _ in range(8):
            starts.append(time)
            time += REAR["attend"]
        time += REAR["finish"]
        ready.append(time)
    first_spread = len(starts)
    for _ in range(blocks // 2):
        starts.append(time)
        time += REAR["spread"]
    total = len(starts)
    end = time
    plan = []
    for i, chunk in enumerate(chunks):
        if i < dense_count:
            moments = [0.0, min(1.0 + i * REAR["pace"], ready[0] - REAR["finish"] - 0.01)]
        else:
            p = (i - dense_count) // 3
            start = max(i * REAR["pace"], ready[p] + 0.01 + 0.1 * ((i - dense_count) % 3))
            moments = [start, start]
        lag = REAR["lag"] if i < dense_count + 3 * (pairs - 1) else REAR["tail"]
        for _ in range(4):
            moments.append(moments[-1] + lag)
        moments.append(1000.0 + i)
        for step, moment in enumerate(moments):
            plan.append((moment + 0.001 * step, chunk, step))
    for step, moment in enumerate((0.0, 4.0, 24.0)):
        plan.append((end + moment, home, step))
    for step in range(5):
        plan.append((end + 3.0 + 6.0 * step, vectors, step))
    plan.sort(key=lambda item: item[0])
    placed = []
    for moment, item, step in plan:
        slot = next((s for s in range(total) if starts[s] > moment), total) - 1
        placed.append((total if moment >= end else slot, item, step))

    def events(slot, begin, until, kinds=None):
        for number in range(begin, until):
            if kinds is not None and (number - begin) % 8 not in kinds:
                continue
            steps = [entry for entry in placed if entry[0] == number]
            if steps:

                @pl.when(slot == number)
                def _(steps=steps):
                    for _, item, step in steps:
                        item.step(step)

    sums[0] = small_ref[...]
    tokens_load.wait()
    first_load.start()
    delta_home.wait()
    delta_cross.wait_recv()

    def one_pair(p, carry):
        pair_lanes = pl.ds(pl.multiple_of(p * 2 * LOW_HALF, 2 * LOW_HALF), 2 * LOW_HALF)
        key_sum[...] = jnp.zeros_like(key_sum)
        value_sum[...] = jnp.zeros_like(value_sum)
        dmask_sum[...] = jnp.zeros_like(dmask_sum)
        query_turned[...] = query_ref[:, pair_lanes].astype(F32).T.astype(BF)
        delta_turned[...] = delta_ref[:, pair_lanes].astype(F32).T.astype(BF)

        def cell(which, query_head, delta_head, log, row_term, mask, place, rows):
            lanes = slice(LOW_HALF * which, LOW_HALF * which + LOW_HALF)
            key = key_ref[place, pair_lanes]
            probs = jnp.exp(dot_nt(query_head, key) - log)
            pair = dot_nt(delta_head, value_ref[place, pair_lanes]) * probs
            mask = mask.astype(F32)
            dscores = (pair * mask - probs * row_term).astype(BF)
            weights = (probs * mask).astype(BF)
            key_sum[lanes, place] += dot_nn(query_turned[lanes, rows], dscores)
            value_sum[lanes, place] += dot_nn(delta_turned[lanes, rows], weights)
            return dot_nn(dscores, key), pair

        def heads_of(rows):
            query = query_ref[rows, pair_lanes]
            delta = delta_ref[rows, pair_lanes]
            product = delta.astype(F32) * out_ref[rows, pair_lanes].astype(F32)
            logs = log_ref[rows, :]
            for which in range(2):
                log = jnp.sum(jnp.where(lane == 2 * p + which, logs, 0.0), axis=1, keepdims=True)
                lanes = slice(LOW_HALF * which, LOW_HALF * which + LOW_HALF)
                row_term = jnp.sum(product[:, lanes], axis=1, keepdims=True)
                yield which, one_head(query, which), one_head(delta, which), log, row_term

        def fold(which, mask_place, pair, tiles):
            for tile in sorted(set(tiles)):
                dmask_sum[which, mask_place, tile * block : (tile + 1) * block] += sum(
                    pair[:, a * block : (a + 1) * block] for a, t in enumerate(tiles) if t == tile
                )

        def finish_rows(rows, dqueries):
            both = jnp.where(low, dqueries[0], dqueries[1]) * scale
            dquery_ref[rows, pair_lanes] = both.astype(BF)

        def trunk_rows(index, carry):
            for part_slot in range(2):
                events(8 * p + 2 * index + part_slot, 0, first_spread, range(part_slot, 4, 2))
            rows = pl.ds(pl.multiple_of(index * 2 * block, 2 * block), 2 * block)
            dqueries = []
            for which, query_head, delta_head, log, row_term in heads_of(rows):
                mask_rows = mask_ref[2 * p + which, rows, :]
                near = (query_head, delta_head, log, row_term)
                dquery, pair = cell(which, *near, mask_rows, pl.ds(0, trunk), rows)
                dmask_sum[which, rows, :] += pair
                side = mask_columns(mask_rows, (1, 0, 1), block)
                for g in range(GROUPS):
                    more, pair = cell(which, *near, side, pl.ds(trunk + wide * g, wide), rows)
                    dquery = dquery + more
                    fold(which, rows, pair, (1, 0, 1))
                dqueries.append(dquery)
            finish_rows(rows, dqueries)
            return carry

        lax.fori_loop(0, TRUNK // 2, trunk_rows, 0)

        def group_rows(group, carry):
            events(8 * p + 4 + group, 0, first_spread, range(4, 8))
            base = pl.multiple_of(trunk + wide * group, block)
            rows = pl.ds(base, wide)
            dqueries = []
            for which, query_head, delta_head, log, row_term in heads_of(rows):
                strips = [mask_ref[2 * p + which, t * block : (t + 1) * block, :] for t in (1, 0, 1)]
                mask_rows = jnp.concatenate(strips, axis=0)
                dquery, pair = cell(
                    which, query_head, delta_head, log, row_term, mask_rows, pl.ds(0, trunk), rows
                )
                dmask_sum[which, block : 2 * block, :] += pair[0:block] + pair[2 * block :]
                dmask_sum[which, 0:block, :] += pair[block : 2 * block]
                near = []
                for row in range(3):
                    at = slice(row * block, (row + 1) * block)
                    start, size, tiles = group_columns(row, block)
                    tile = 0 if row == 1 else 1
                    more, pair = cell(
                        which,
                        query_head[at],
                        delta_head[at],
                        log[at],
                        row_term[at],
                        mask_columns(strips[row], tiles, block),
                        pl.ds(pl.multiple_of(base + start, block), size),
                        pl.ds(pl.multiple_of(base + row * block, block), block),
                    )
                    fold(which, pl.ds(tile * block, block), pair, tiles)
                    near.append(more)
                dqueries.append(dquery + jnp.concatenate(near, axis=0))
            finish_rows(rows, dqueries)
            return carry

        lax.fori_loop(0, GROUPS, group_rows, 0)
        dkey_ref[:, pair_lanes] = key_sum[...].T.astype(BF)
        dvalue_ref[:, pair_lanes] = value_sum[...].T.astype(BF)
        query_turned[...] = dquery_ref[:, pair_lanes].astype(F32).T.astype(BF)
        place = pl.ds(pl.multiple_of(c * mine + p * 128, 128), 128)
        for row, source in ((0, dquery_ref), (1, dvalue_ref)):
            column = jnp.sum(source[:, pair_lanes].astype(F32), axis=0, keepdims=True)
            sums[0, row : row + 1, place] = column
        tokens = tokens_ref[...].reshape(rows_all, width)
        for t, source in enumerate((query_turned, key_sum, value_sum)):
            grad = dot_nn(source[...].astype(BF), tokens).T.astype(BF)
            columns = slice(t * 128, t * 128 + 128)
            joined_part[p, :, :, :, :, columns] = grad.reshape(joined_part.shape[1:5] + (128,))
        shape = mask_part.shape[2:4] + (strip, mask_part.shape[5])
        for which in range(2):
            for tile in range(LINE):
                rows = dmask_sum[which, tile * block : (tile + 1) * block, :].astype(BF)
                mask_part[2 * p + which, tile, :, :, 0:strip, :] = rows.reshape(shape)
        return carry

    lax.fori_loop(0, pairs, one_pair, 0)
    first_load.wait()

    def spread(i, carry):
        events(first_spread + i, first_spread, total)
        rows = pl.ds(pl.multiple_of(2 * block * i, 2 * block), 2 * block)
        grads = (dquery_ref, dkey_ref, dvalue_ref)
        out = 0.0
        for t, grad in enumerate(grads):
            out = out + dot_nt(grad[rows, :], joined_weight[:, t * mine : (t + 1) * mine])
        inside = (i // (blocks // 4) == c).astype(F32)
        at = i % (blocks // 4)
        out = out + inside * first_ref[pl.ds(2 * at, 2)].reshape(2 * block, width)
        tokens_ref[pl.ds(2 * i, 2)] = out.astype(BF).reshape(2, block, width)
        return carry

    lax.fori_loop(0, blocks // 2, spread, 0)
    for slot, item, step in placed:
        if slot == total:
            item.step(step)
    layer_home.wait()
    layer_cross.wait_recv()
    layer_cross.wait_send()
    for item in chunks + [home, vectors]:
        item.finish()
    delta_cross.wait_send()


def rear(
    query, key, value, mask, out, logs, weight, small, place, delta, tokens, first, out_grad, up_grad,
    down_grad, layer, block, scale
):
    rows, mine = query.shape
    width = 2 * mine
    heads, span, _ = mask.shape
    pairs = heads // 2
    blocks = rows // block
    own_rows = rows // 4
    strip = span // 16
    piece = out_grad.shape[3]
    like = jax.ShapeDtypeStruct
    vmem = lambda shape, kind=BF: pltpu.VMEM(shape, kind)
    mask_buffers = scatter_buffers(heads, (strip, span), False)
    mask_buffers[0] = vmem((heads, LINE, 2, 2, piece, span))
    return pl.pallas_call(
        functools.partial(rear_kernel, block, scale),
        name="rear",
        in_specs=[VMEM] * 8 + [SMEM] + [ANY] * 7,
        out_specs=[VMEM] * 7 + [ANY],
        out_shape=[
            like((2,) + out_grad.shape[3:], BF),
            like((2,) + up_grad.shape[3:], BF),
            like((4, 2) + down_grad.shape[4:], BF),
            like((2, heads, 2, strip, span), BF),
            like((pairs, 2, 2, piece, mine), BF),
            like((2, own_rows, width), BF),
            like(small.shape, F32),
            like((2, blocks // 4, block, width), BF),
        ],
        scratch_shapes=[
            vmem((rows, mine)),
            vmem((2 * LOW_HALF, rows), F32),
            vmem((2 * LOW_HALF, rows), F32),
            vmem((2 * LOW_HALF, rows)),
            vmem((2 * LOW_HALF, rows)),
            vmem((2, span, span), F32),
            vmem((rows, mine)),
            vmem((rows, mine)),
            vmem((rows, mine)),
            vmem(tokens.shape),
            vmem(first.shape, F32),
        ]
        + scatter_buffers(9, (piece, mine), False)
        + scatter_buffers(pairs, (piece, mine), False)
        + mask_buffers
        + [vmem((2, own_rows, width))] * 3
        + [vmem((4,) + small.shape, F32), vmem((6,) + small.shape, F32)]
        + copy_semaphores(24, 11),
        compiler_params=pltpu.CompilerParams(
            collective_id=5, has_side_effects=True, vmem_limit_bytes=VMEM_LIMIT
        ),
    )(
        query, key, value, mask, out, logs, weight, small, place, delta, tokens, first, out_grad,
        up_grad, down_grad, layer
    )


def settle_kernel(
    out_ref, up_ref, down_ref, joined_ref, mask_ref, scores_ref, jitter_ref, scale_ref,
    out_grad, up_grad, down_grad, joined_grad, mask_grad
):
    out_grad[...] = out_ref[...].astype(F32).reshape(out_grad.shape)
    up_grad[...] = up_ref[...].astype(F32).reshape(up_grad.shape)
    down_grad[...] = down_ref[...].astype(F32).reshape(down_grad.shape)
    pairs, halves, cores, rows, _ = joined_ref.shape
    for p in range(pairs):
        for a in range(halves):
            for b in range(cores):
                for t in range(3):
                    at = ((t * cores + b) * pairs + p) * 128
                    piece = joined_ref[p, a, b, :, t * 128 : (t + 1) * 128]
                    joined_grad[a * rows : (a + 1) * rows, at : at + 128] = piece.astype(F32)

    def head(h, carry):
        scale = scale_ref[h]
        soft = jax.nn.sigmoid((scores_ref[h] + jitter_ref[h]) / scale)
        total = mask_ref[h].astype(F32).reshape(soft.shape)
        mask_grad[h] = total * soft * (1.0 - soft) / scale
        return carry

    lax.fori_loop(0, mask_grad.shape[0], head, 0)


def settle(out, up, down, joined, mask, scores, jitter, scale):
    half, width = out.shape[1:]
    like = jax.ShapeDtypeStruct
    return pl.pallas_call(
        settle_kernel,
        name="settle",
        in_specs=[VMEM] * 7 + [SMEM],
        out_specs=[VMEM] * 5,
        out_shape=[
            like((2 * half, width), F32),
            like((2 * half, up.shape[2]), F32),
            like((8 * half, width), F32),
            like((2 * half, 3 * width), F32),
            like(scores.shape, F32),
        ],
        compiler_params=pltpu.CompilerParams(vmem_limit_bytes=VMEM_LIMIT),
    )(out, up, down, joined, mask, scores, jitter, scale)


def gather_rows(array, axis=0):
    return lax.all_gather(array, "fsdp", axis=axis, tiled=True)


def per_device(
    layer_entry_matrix,
    loss_sensitivity,
    ancestor_block_table,
    gate_trained_scores,
    gate_random_jitter,
    softening_scale,
    triple_projection_matrix,
    asker_constant_vector,
    content_constant_vector,
    mixer_exit_matrix,
    mixer_exit_constant,
    mixer_scaling_factor,
    mixer_recentering_term,
    dense_expand_matrix,
    dense_expand_constant,
    dense_contract_matrix,
    dense_contract_constant,
    dense_scaling_factor,
    dense_recentering_term,
):
    micro, _, own_rows, width = layer_entry_matrix.shape
    leaf_count = lax.axis_size("leaf")
    blocks = ancestor_block_table.shape[2]
    rows = own_rows * leaf_count
    block = rows // blocks
    heads, _, span = gate_trained_scores.shape
    leaf = lax.axis_index("leaf")
    tree = leaf // CORES
    core = leaf % CORES
    my_heads = heads // CORES
    my_width = width // CORES
    half = rows // CORES
    pairs = [[CORES * i + c for c in range(CORES)] for i in range(leaf_count // CORES)]
    score_scale = 1.0 / math.sqrt(width // heads)

    orders = [tree_order(ancestor_block_table[m, 0]) for m in range(micro)]
    order = jnp.where(tree == 0, orders[0][0], orders[1][0])

    def own_tree(tokens):
        whole = lax.all_gather(tokens[:, 0], "leaf", axis=1, tiled=True)
        mine = lax.dynamic_index_in_dim(whole, tree, 0, keepdims=False)
        return reorder(mine.reshape(blocks, block, width), order).reshape(rows, width)

    def own_tokens(halves):
        whole = lax.all_gather(halves, "leaf", axis=0, tiled=True)
        whole = whole.reshape(micro, blocks, block, width)
        mine = [reorder(whole[m], orders[m][1]) for m in range(micro)]
        mine = jnp.stack(mine).reshape(micro, 1, rows, width)
        return lax.dynamic_slice_in_dim(mine, leaf * own_rows, own_rows, 2)

    def own_half(array):
        return lax.dynamic_slice_in_dim(array, core * half, half, 0)

    softened = jax.nn.sigmoid(
        (gate_trained_scores + gate_random_jitter) / softening_scale[:, None, None]
    )
    relaxed = lax.dynamic_slice_in_dim(softened.astype(BF), core * my_heads, my_heads, 0)
    mask = gather_rows(relaxed, 1)
    joined_weight = gather_rows(triple_projection_matrix)
    out_weight = gather_rows(mixer_exit_matrix)
    up_weight = gather_rows(dense_expand_matrix)
    down_weight = gather_rows(dense_contract_matrix)
    vectors = [
        asker_constant_vector,
        content_constant_vector,
        mixer_exit_constant,
        mixer_scaling_factor,
        mixer_recentering_term,
        dense_contract_constant,
        dense_scaling_factor,
        dense_recentering_term,
        dense_expand_constant,
    ]
    packed = gather_rows(jnp.concatenate(vectors)[None])
    places = []
    first = 0
    for vector in vectors:
        places.append((first, first + vector.shape[0]))
        first += vector.shape[0]
    (
        query_bias,
        value_bias,
        out_bias,
        first_gain,
        first_shift,
        down_bias,
        second_gain,
        second_shift,
        up_bias,
    ) = [packed[:, a:b].reshape(-1).astype(F32) for a, b in places]

    tokens = own_tree(layer_entry_matrix)
    upstream = own_half(own_tree(loss_sensitivity)).astype(F32)

    def my_columns(matrix, which):
        return lax.dynamic_slice_in_dim(matrix, which * width + core * my_width, my_width, 1)

    def my_part(vector):
        return lax.dynamic_slice_in_dim(vector, core * my_width, my_width, 0)

    weight3 = jnp.concatenate([my_columns(joined_weight, i) for i in range(3)], axis=1)
    joined = dot_nn(tokens, weight3)
    query = (joined[:, :my_width] + my_part(query_bias)).astype(BF) * jnp.asarray(score_scale, BF)
    key = joined[:, my_width : 2 * my_width].astype(BF)
    value = (joined[:, 2 * my_width :] + my_part(value_bias)).astype(BF)

    attended_mine, logs = attend(query, key, value, mask, block)
    attended = own_half(
        lax.all_gather(attended_mine, "leaf", axis=1, tiled=True, axis_index_groups=pairs)
    )

    rows_mine = own_half(tokens).astype(F32)
    hidden, normed_first, inv_first = layer_norm(
        rows_mine + dot_nn(attended, out_weight) + out_bias, first_gain, first_shift
    )
    hidden_low = hidden.astype(BF)
    active, slope = gelu_parts(dot_nn(hidden_low, up_weight) + up_bias)
    active = active.astype(BF)
    output, normed_second, inv_second = layer_norm(
        hidden + dot_nn(active, down_weight) + down_bias, second_gain, second_shift
    )
    layer_out = own_tokens(output.astype(BF))

    delta_second, second_gain_grad, second_shift_grad = norm_backward(
        upstream, normed_second, inv_second, second_gain
    )
    delta_branch = delta_second.astype(BF)
    down_weight_grad = dot_tn(active, delta_branch)
    down_bias_grad = jnp.sum(delta_branch.astype(F32), axis=0)
    delta_up = (dot_nt(delta_branch, down_weight) * slope).astype(BF)
    up_weight_grad = dot_tn(hidden_low, delta_up)
    up_bias_grad = jnp.sum(delta_up.astype(F32), axis=0)
    delta_first, first_gain_grad, first_shift_grad = norm_backward(
        delta_second + dot_nt(delta_up, up_weight), normed_first, inv_first, first_gain
    )
    delta_proj = delta_first.astype(BF)
    out_weight_grad = dot_tn(attended, delta_proj)
    out_bias_grad = jnp.sum(delta_proj.astype(F32), axis=0)
    delta_attended = lax.all_gather(
        dot_nt(delta_proj, out_weight).astype(BF),
        "leaf",
        axis=0,
        tiled=True,
        axis_index_groups=pairs,
    )
    delta_attended = lax.dynamic_slice_in_dim(delta_attended, core * my_width, my_width, 1)

    dquery, dkey, dvalue, dmask = attend_back(
        query, key, value, mask, attended_mine, logs, delta_attended, block, score_scale
    )
    djoined = jnp.concatenate([dquery, dkey, dvalue], axis=1)
    joined_grad = dot_tn(tokens, djoined)
    query_bias_grad = jnp.sum(dquery.astype(F32), axis=0)
    value_bias_grad = jnp.sum(dvalue.astype(F32), axis=0)
    dtokens = lax.psum_scatter(
        dot_nt(djoined, weight3).astype(BF),
        "leaf",
        scatter_dimension=0,
        tiled=True,
        axis_index_groups=pairs,
    )
    tokens_grad = own_tokens((delta_first + dtokens.astype(F32)).astype(BF))

    def placed(part, whole_size, start, axis):
        shape = list(part.shape)
        shape[axis] = whole_size
        return lax.dynamic_update_slice_in_dim(jnp.zeros(shape, part.dtype), part, start, axis)

    def owned(grad, axis=0):
        return lax.psum_scatter(
            grad.astype(BF), "fsdp", scatter_dimension=axis, tiled=True
        )

    joined_part = owned(joined_grad)
    joined_full = jnp.zeros((joined_part.shape[0], 3 * width), BF)
    for i in range(3):
        joined_full = lax.dynamic_update_slice_in_dim(
            joined_full,
            joined_part[:, i * my_width : (i + 1) * my_width],
            i * width + core * my_width,
            1,
        )
    matrices = (
        joined_full,
        owned(out_weight_grad),
        owned(up_weight_grad),
        owned(down_weight_grad),
        placed(owned(dmask, 1), heads, core * my_heads, 0),
    )
    joined_total, out_total, up_total, down_total, mask_total = [
        lax.psum(matrix, "leaf").astype(F32) for matrix in matrices
    ]
    small = (
        placed(query_bias_grad, width, core * my_width, 0),
        placed(value_bias_grad, width, core * my_width, 0),
        out_bias_grad,
        first_gain_grad,
        first_shift_grad,
        up_bias_grad,
        down_bias_grad,
        second_gain_grad,
        second_shift_grad,
    )
    fsdp_count = lax.axis_size("fsdp")
    packed_grads = jnp.concatenate([s.reshape(fsdp_count, -1) for s in small], axis=1)
    packed_grads = lax.psum(
        lax.psum_scatter(packed_grads, "fsdp", scatter_dimension=0, tiled=True), "leaf"
    )[0]
    vector_grads = []
    first = 0
    for s in small:
        size = s.shape[0] // fsdp_count
        vector_grads.append(packed_grads[first : first + size])
        first += size
    mask_gradient = mask_total * softened * (1.0 - softened) / softening_scale[:, None, None]
    return (
        layer_out,
        tokens_grad,
        joined_total,
        vector_grads[0],
        vector_grads[1],
        out_total,
        vector_grads[2],
        vector_grads[3],
        vector_grads[4],
        up_total,
        vector_grads[5],
        down_total,
        vector_grads[6],
        vector_grads[7],
        vector_grads[8],
        mask_gradient,
    )


def fast_device(
    layer_entry_matrix,
    loss_sensitivity,
    ancestor_block_table,
    gate_trained_scores,
    gate_random_jitter,
    softening_scale,
    triple_projection_matrix,
    asker_constant_vector,
    content_constant_vector,
    mixer_exit_matrix,
    mixer_exit_constant,
    mixer_scaling_factor,
    mixer_recentering_term,
    dense_expand_matrix,
    dense_expand_constant,
    dense_contract_matrix,
    dense_contract_constant,
    dense_scaling_factor,
    dense_recentering_term,
):
    micro, _, own_rows, width = layer_entry_matrix.shape
    blocks = ancestor_block_table.shape[2]
    rows = own_rows * 4
    block = rows // blocks
    heads, strip, span = gate_trained_scores.shape
    leaf = lax.axis_index("leaf")
    tree, core = leaf // CORES, leaf % CORES
    mine = width // CORES
    half = rows // CORES
    shard = width // 8
    hidden_shard = dense_contract_matrix.shape[0]
    score_scale = 1.0 / math.sqrt(width // heads)

    table = lax.dynamic_index_in_dim(ancestor_block_table[:, 0], tree, 0, keepdims=False)
    order, place = tree_order(table)
    vectors = [
        asker_constant_vector,
        content_constant_vector,
        mixer_exit_constant,
        mixer_scaling_factor,
        mixer_recentering_term,
        dense_contract_constant,
        dense_scaling_factor,
        dense_recentering_term,
        dense_expand_constant,
    ]
    sizes = [vector.shape[0] for vector in vectors]
    used = sum(sizes)
    places = [sum(sizes[:i]) for i in range(len(sizes))]
    wide = jnp.pad(jnp.stack(vectors[:8]), ((0, 0), (0, 128 - shard)))
    tall = vectors[8].reshape(-1, 128)
    flat = jnp.pad(jnp.concatenate([wide, tall]), ((0, 8 - tall.shape[0]), (0, 0)))

    (
        tokens,
        joined_weight,
        query,
        key,
        value,
        mask,
        attended_mine,
        logs,
        attended,
        out_weight,
        up_weight,
        down_weight,
        tree_upstream,
        normed_first,
        inv_first,
        active,
        slope,
        gathered,
        _,
    ) = front(
        order,
        layer_entry_matrix.reshape(micro, own_rows // block, block, width),
        loss_sensitivity.reshape(micro, own_rows // block, block, width),
        triple_projection_matrix.reshape(2, shard // 2, 3 * width),
        gate_trained_scores,
        gate_random_jitter,
        softening_scale,
        mixer_exit_matrix.reshape(2, shard // 2, width),
        dense_expand_matrix.reshape(2, shard // 2, -1),
        dense_contract_matrix.reshape(4, 2, hidden_shard // 8, width),
        flat,
    )
    first_gain, first_shift, down_bias, second_gain, second_shift = [
        gathered[i : i + 1] for i in range(3, 8)
    ]
    inv_first = inv_first[:, :1]
    joined_weight = joined_weight.reshape(width, 3 * mine)
    mask = mask.reshape(heads // CORES, span, span)
    out_weight = out_weight.reshape(width, width)
    up_weight = up_weight.reshape(width, -1)
    down_weight = down_weight.reshape(-1, width)
    half_order = lax.dynamic_slice_in_dim(order, core * (blocks // 2), blocks // 2, 0)
    upstream = pick(half_order, tree_upstream, tree_upstream).reshape(half, width).astype(F32)
    tokens = tokens.reshape(rows, width)
    hidden = normed_first * first_gain + first_shift
    hidden_low = hidden.astype(BF)
    output, normed_second, inv_second = layer_norm(
        hidden + dot_nn(active, down_weight) + down_bias, second_gain, second_shift
    )
    to_core = [(i, i ^ 1) for i in range(4)]
    low_output = output.astype(BF).reshape(blocks // 2, block, width)
    twin_output = lax.ppermute(low_output, "leaf", to_core)
    swap = core * (blocks // 2)
    own_blocks = blocks // 4
    here = lax.dynamic_slice_in_dim(place, leaf * own_blocks, own_blocks, 0)
    there = lax.dynamic_slice_in_dim(place, (leaf ^ 2) * own_blocks, own_blocks, 0)
    wanted = jnp.concatenate([here, there])
    wanted = (wanted + swap) % blocks
    picked = pick(wanted, low_output, twin_output)
    delta_second, second_gain_grad, second_shift_grad = norm_backward(
        upstream, normed_second, inv_second, second_gain
    )
    delta_branch = delta_second.astype(BF)
    down_weight_grad = dot_tn(active, delta_branch).astype(BF)
    down_bias_grad = jnp.sum(delta_branch.astype(F32), axis=0)
    delta_branch, picked = lax.optimization_barrier((delta_branch, picked))
    delta_up = (dot_nt(delta_branch, down_weight) * slope.astype(F32)).astype(BF)
    up_weight_grad = dot_tn(hidden_low, delta_up).astype(BF)
    up_bias_grad = jnp.sum(delta_up.astype(F32), axis=0)
    delta_first, first_gain_grad, first_shift_grad = norm_backward(
        delta_second + dot_nt(delta_up, up_weight), normed_first, inv_first, first_gain
    )
    delta_proj = delta_first.astype(BF)
    out_weight_grad = dot_tn(attended, delta_proj).astype(BF)
    out_bias_grad = jnp.sum(delta_proj.astype(F32), axis=0)
    delta_attended = dot_nt(delta_proj, out_weight).astype(BF)

    blank = jnp.zeros((1, width), F32)
    small = jnp.concatenate(
        [
            blank,
            blank,
            out_bias_grad[None],
            first_gain_grad[None],
            first_shift_grad[None],
            down_bias_grad[None],
            second_gain_grad[None],
            second_shift_grad[None],
            up_bias_grad.reshape(-1, width),
            jnp.zeros((4, width), F32),
        ]
    )
    out_total, up_total, down_total, mask_total, joined_total, tokens_grad, small, layer_out = rear(
        query,
        key,
        value,
        mask,
        attended_mine,
        logs,
        joined_weight,
        small,
        place,
        delta_attended,
        tokens.reshape(blocks, block, width),
        delta_first.reshape(blocks // 2, block, width),
        out_weight_grad.reshape(LINE, 2, 2, shard // 2, width),
        up_weight_grad.reshape(LINE, 2, 2, shard // 2, -1),
        down_weight_grad.reshape(LINE, 2, 4, 2, hidden_shard // 8, width),
        picked,
        block,
        score_scale,
    )
    spot = lax.axis_index("fsdp")
    narrow = lax.dynamic_slice_in_dim(small[:8], spot * shard, shard, 1)
    vector_grads = [narrow[i] for i in range(8)]
    vector_grads.append(
        lax.dynamic_slice_in_dim(small[8:12].reshape(-1), spot * hidden_shard, hidden_shard, 0)
    )
    out_total, up_total, down_total, joined_total, mask_gradient = settle(
        out_total,
        up_total,
        down_total,
        joined_total,
        mask_total.reshape(heads, 2, strip // 2, span),
        gate_trained_scores,
        gate_random_jitter,
        softening_scale,
    )
    return (
        layer_out.reshape(micro, 1, own_rows, width),
        tokens_grad[:, None],
        joined_total,
        vector_grads[0],
        vector_grads[1],
        out_total,
        vector_grads[2],
        vector_grads[3],
        vector_grads[4],
        up_total,
        vector_grads[8],
        down_total,
        vector_grads[5],
        vector_grads[6],
        vector_grads[7],
        mask_gradient,
    )


def solution(mesh):
    placed = (
        P(None, "fsdp", "leaf", None),
        P(None, "fsdp", "leaf", None),
        P(None, "fsdp", None),
        P(None, "fsdp", None),
        P(None, "fsdp", None),
        P(),
        P("fsdp", None),
        P("fsdp"),
        P("fsdp"),
        P("fsdp", None),
        P("fsdp"),
        P("fsdp"),
        P("fsdp"),
        P("fsdp", None),
        P("fsdp"),
        P("fsdp", None),
        P("fsdp"),
        P("fsdp"),
        P("fsdp"),
    )
    return jax.shard_map(
        fast_device if mesh.shape["fsdp"] == 8 and mesh.shape["leaf"] == 4 else per_device,
        mesh=mesh,
        in_specs=placed,
        out_specs=(
            P(None, "fsdp", "leaf", None),
            P(None, "fsdp", "leaf", None),
            P("fsdp", None),
            P("fsdp"),
            P("fsdp"),
            P("fsdp", None),
            P("fsdp"),
            P("fsdp"),
            P("fsdp"),
            P("fsdp", None),
            P("fsdp"),
            P("fsdp", None),
            P("fsdp"),
            P("fsdp"),
            P("fsdp"),
            P(None, "fsdp", None),
        ),
        check_vma=False,
    )
```

```python
import functools
import math

import jax
import jax.numpy as jnp
from jax import lax
from jax.experimental import pallas as pl
from jax.experimental.pallas import tpu as pltpu
from jax.sharding import PartitionSpec as P

EPSILON = 1e-05
F32 = jnp.float32
BF = jnp.bfloat16
TRUNK = 4
GROUPS = 4
CORES = 2
LOW_HALF = 64


def layer_norm(values, gain_vec, shift_vec):
    average = jnp.mean(values, axis=-1, keepdims=True)
    centred = values - average
    inv_scale = lax.rsqrt(jnp.mean(centred * centred, axis=-1, keepdims=True) + EPSILON)
    normed = centred * inv_scale
    return (normed * gain_vec + shift_vec, normed, inv_scale)


def norm_backward(upstream, normed, inv_scale, gain_vec):
    scaled = upstream * gain_vec
    inner_term = (
        scaled
        - jnp.mean(scaled, axis=-1, keepdims=True)
        - normed * jnp.mean(scaled * normed, axis=-1, keepdims=True)
    )
    return (inv_scale * inner_term, jnp.sum(upstream * normed, axis=0), jnp.sum(upstream, axis=0))


def gelu_parts(values):
    cdf = 0.5 * (1.0 + lax.erf(values / math.sqrt(2.0)))
    density = jnp.exp(-0.5 * values * values) / math.sqrt(2.0 * math.pi)
    return (values * cdf, cdf + values * density)


def dot_nn(left, right):
    return jnp.dot(left, right, preferred_element_type=F32)


def dot_nt(left, right):
    return lax.dot_general(left, right, (((1,), (1,)), ((), ())), preferred_element_type=F32)


def dot_tn(left, right):
    return lax.dot_general(left, right, (((0,), (0,)), ((), ())), preferred_element_type=F32)


def tree_order(parent):
    count = parent.shape[0]
    ids = jnp.arange(count, dtype=jnp.int32)
    up = (parent[:, None] == ids[None, :]) & (ids[:, None] != ids[None, :])
    up = up.astype(F32)
    reach = up
    power = up
    for _ in range(TRUNK + 1):
        power = jnp.sum(power[:, :, None] * up[None, :, :], axis=1)
        reach = reach + power
    depth = jnp.sum(reach, axis=1)
    before = (ids[None, :] < ids[:, None]).astype(F32)
    branch = (depth == TRUNK).astype(F32)
    rank = jnp.sum(before * branch[None, :], axis=1)
    own_rank = jnp.where(depth == TRUNK, rank, jnp.sum(up * rank[None, :], axis=1))
    siblings = jnp.sum(up[:, None, :] * up[None, :, :], axis=2) * before
    second = jnp.sum(siblings, axis=1)
    within = jnp.where(depth == TRUNK, 1.0, 2.0 * second)
    place = jnp.where(depth < TRUNK, depth, TRUNK + 3.0 * own_rank + within).astype(jnp.int32)
    order = jnp.sum((place[:, None] == ids[None, :]) * ids[:, None], axis=0).astype(jnp.int32)
    return (order, place)


def low_lanes():
    return lax.broadcasted_iota(jnp.int32, (1, 2 * LOW_HALF), 1) < LOW_HALF


def one_head(pair, which):
    keep = low_lanes() if which == 0 else jnp.logical_not(low_lanes())
    return jnp.where(keep, pair, jnp.zeros_like(pair))


def group_columns(row, block):
    return ((0, 2 * block, (1, 0)), (0, 3 * block, (1, 0, 1)), (block, 2 * block, (0, 1)))[row]


def mask_columns(mask_rows, tiles, block):
    return jnp.concatenate([mask_rows[:, t * block : (t + 1) * block] for t in tiles], axis=1)


def attend_kernel(block, query_ref, key_ref, value_ref, mask_ref, out_ref, log_ref):
    trunk = TRUNK * block
    wide = 3 * block
    low = low_lanes()

    def soften(parts, masks, values):
        top = parts[0].max(axis=1, keepdims=True)
        for part in parts[1:]:
            top = jnp.maximum(top, part.max(axis=1, keepdims=True))
        total = 0.0
        out = 0.0
        for part, mask, value in zip(parts, masks, values):
            weight = jnp.exp(part - top)
            total = total + weight.sum(axis=1, keepdims=True)
            out = out + dot_nn((weight * mask.astype(F32)).astype(BF), value)
        return (out * (1.0 / total), top + jnp.log(total))

    def emit(rows, results):
        count = results[0][1].shape[0]
        out_ref[rows, :] = jnp.where(low, results[0][0], results[1][0]).astype(BF)
        logs = [jnp.broadcast_to(result[1], (count, 2 * LOW_HALF)) for result in results]
        log_ref[rows, :] = jnp.where(low, logs[0], logs[1])

    def trunk_rows(index, carry):
        rows = pl.ds(pl.multiple_of(index * block, block), block)
        query = query_ref[rows, :]
        results = []
        for which in range(2):
            mask_rows = mask_ref[which, rows, :]
            columns = [(0, trunk, mask_rows)]
            side = mask_columns(mask_rows, (1, 0, 1), block)
            columns += [(trunk + wide * g, wide, side) for g in range(GROUPS)]
            head = one_head(query, which)
            parts = [dot_nt(head, key_ref[c : c + w, :]) for c, w, _ in columns]
            values = [value_ref[c : c + w, :] for c, w, _ in columns]
            results.append(soften(parts, [column[2] for column in columns], values))
        emit(rows, results)
        return carry

    lax.fori_loop(0, TRUNK, trunk_rows, 0)

    def group_rows(group, carry):
        base = pl.multiple_of(trunk + wide * group, block)
        for row in range(3):
            rows = pl.ds(pl.multiple_of(base + block * row, block), block)
            query = query_ref[rows, :]
            tile = 0 if row == 1 else 1
            start, width, tiles = group_columns(row, block)
            columns = pl.ds(pl.multiple_of(base + start, block), width)
            results = []
            for which in range(2):
                mask_rows = mask_ref[which, tile * block : (tile + 1) * block, :]
                head = one_head(query, which)
                parts = [dot_nt(head, key_ref[0:trunk, :]), dot_nt(head, key_ref[columns, :])]
                masks = [mask_rows, mask_columns(mask_rows, tiles, block)]
                values = [value_ref[0:trunk, :], value_ref[columns, :]]
                results.append(soften(parts, masks, values))
            emit(rows, results)
        return carry

    lax.fori_loop(0, GROUPS, group_rows, 0)


def attend(query, key, value, mask, block):
    rows, width = query.shape
    pairs = width // (2 * LOW_HALF)
    span = mask.shape[1]
    spec = pl.BlockSpec((rows, 2 * LOW_HALF), lambda p: (0, p))
    return pl.pallas_call(
        functools.partial(attend_kernel, block),
        grid=(pairs,),
        name="attend",
        in_specs=[spec, spec, spec, pl.BlockSpec((2, span, span), lambda p: (p, 0, 0))],
        out_specs=[spec, spec],
        out_shape=[
            jax.ShapeDtypeStruct((rows, width), BF),
            jax.ShapeDtypeStruct((rows, width), F32),
        ],
        compiler_params=pltpu.CompilerParams(vmem_limit_bytes=48 << 20),
    )(query, key, value, mask)


def attend_back_kernel(
    block,
    scale,
    query_ref,
    key_ref,
    value_ref,
    mask_ref,
    out_ref,
    log_ref,
    delta_ref,
    dquery_ref,
    dkey_ref,
    dvalue_ref,
    dmask_ref,
    key_sum,
    value_sum,
    query_turned,
    delta_turned,
):
    trunk = TRUNK * block
    wide = 3 * block
    low = low_lanes()
    key_sum[...] = jnp.zeros_like(key_sum)
    value_sum[...] = jnp.zeros_like(value_sum)
    dmask_ref[...] = jnp.zeros_like(dmask_ref)
    query_turned[...] = query_ref[...].astype(F32).T.astype(BF)
    delta_turned[...] = delta_ref[...].astype(F32).T.astype(BF)

    def work(rows, mask_place, columns):
        query = query_ref[rows, :]
        delta = delta_ref[rows, :]
        product = delta.astype(F32) * out_ref[rows, :].astype(F32)
        logs = log_ref[rows, :]
        dqueries = []
        for which in range(2):
            first = LOW_HALF * which
            lanes = slice(first, first + LOW_HALF)
            query_head = one_head(query, which)
            delta_head = one_head(delta, which)
            log = logs[:, first : first + 1]
            row_term = jnp.sum(product[:, lanes], axis=1, keepdims=True)
            mask_rows = mask_ref[which, mask_place, :]
            dquery = 0.0
            for place, tiles in columns:
                key = key_ref[place, :]
                value = value_ref[place, :]
                probs = jnp.exp(dot_nt(query_head, key) - log)
                pair = dot_nt(delta_head, value) * probs
                mask = mask_rows if tiles is None else mask_columns(mask_rows, tiles, block)
                mask = mask.astype(F32)
                if tiles is None:
                    dmask_ref[which, mask_place, :] += pair
                else:
                    for tile in sorted(set(tiles)):
                        dmask_ref[which, mask_place, tile * block : (tile + 1) * block] += sum(
                            pair[:, a * block : (a + 1) * block]
                            for a, t in enumerate(tiles)
                            if t == tile
                        )
                dscores = (pair * mask - probs * row_term).astype(BF)
                weights = (probs * mask).astype(BF)
                dquery = dquery + dot_nn(dscores, key)
                key_sum[lanes, place] += dot_nn(query_turned[lanes, rows], dscores)
                value_sum[lanes, place] += dot_nn(delta_turned[lanes, rows], weights)
            dqueries.append(dquery)
        dquery_ref[rows, :] = (jnp.where(low, dqueries[0], dqueries[1]) * scale).astype(BF)

    def trunk_rows(index, carry):
        rows = pl.ds(pl.multiple_of(index * block, block), block)
        columns = [(pl.ds(0, trunk), None)]
        columns += [(pl.ds(trunk + wide * g, wide), (1, 0, 1)) for g in range(GROUPS)]
        work(rows, rows, columns)
        return carry

    lax.fori_loop(0, TRUNK, trunk_rows, 0)

    def group_rows(group, carry):
        base = pl.multiple_of(trunk + wide * group, block)
        for row in range(3):
            rows = pl.ds(pl.multiple_of(base + block * row, block), block)
            tile = 0 if row == 1 else 1
            start, width, tiles = group_columns(row, block)
            near = pl.ds(pl.multiple_of(base + start, block), width)
            work(rows, pl.ds(tile * block, block), [(pl.ds(0, trunk), None), (near, tiles)])
        return carry

    lax.fori_loop(0, GROUPS, group_rows, 0)
    dkey_ref[...] = key_sum[...].T.astype(BF)
    dvalue_ref[...] = value_sum[...].T.astype(BF)


def attend_back(query, key, value, mask, out, logs, delta, block, scale):
    rows, width = query.shape
    pair_width = 2 * LOW_HALF
    pairs = width // pair_width
    span = mask.shape[1]
    spec = pl.BlockSpec((rows, pair_width), lambda p: (0, p))
    mask_spec = pl.BlockSpec((2, span, span), lambda p: (p, 0, 0))
    return pl.pallas_call(
        functools.partial(attend_back_kernel, block, scale),
        grid=(pairs,),
        name="attend_back",
        in_specs=[spec, spec, spec, mask_spec, spec, spec, spec],
        out_specs=[spec, spec, spec, mask_spec],
        out_shape=[jax.ShapeDtypeStruct((rows, width), BF)] * 3
        + [jax.ShapeDtypeStruct(mask.shape, F32)],
        scratch_shapes=[
            pltpu.VMEM((pair_width, rows), F32),
            pltpu.VMEM((pair_width, rows), F32),
            pltpu.VMEM((pair_width, rows), BF),
            pltpu.VMEM((pair_width, rows), BF),
        ],
        compiler_params=pltpu.CompilerParams(vmem_limit_bytes=48 << 20),
    )(query, key, value, mask, out, logs, delta)


def reorder_kernel(order_ref, source_ref, target_ref):
    target_ref[...] = source_ref[...]


def reorder(tokens, order):
    count, block, width = tokens.shape
    return pl.pallas_call(
        reorder_kernel,
        name="reorder",
        grid_spec=pltpu.PrefetchScalarGridSpec(
            num_scalar_prefetch=1,
            grid=(count,),
            in_specs=[pl.BlockSpec((1, block, width), lambda i, order_ref: (order_ref[i], 0, 0))],
            out_specs=pl.BlockSpec((1, block, width), lambda i, order_ref: (i, 0, 0)),
        ),
        out_shape=jax.ShapeDtypeStruct(tokens.shape, tokens.dtype),
    )(order, tokens)


MESH = pl.DeviceIdType.MESH
ANY = pl.BlockSpec(memory_space=pl.ANY)
VMEM = pl.BlockSpec(memory_space=pltpu.VMEM)
SMEM = pl.BlockSpec(memory_space=pltpu.SMEM)
VMEM_LIMIT = 62 << 20
LINE = 4
ALL = slice(None)


class Net:
    def __init__(self, send, recv, local):
        leaf, shard = lax.axis_index("leaf"), lax.axis_index("fsdp")
        self.leaf, self.shard = leaf, shard
        self.x, self.c = leaf // 2, leaf % 2
        self.z, self.y = shard // 2, shard % 2
        self.send, self.recv, self.local = send, recv, local

    def near(self, which):
        x, c, y, z = self.x, self.c, self.y, self.z
        if which == "x":
            x = 1 - x
        elif which == "c":
            c = 1 - c
        elif which == "xc":
            x, c = 1 - x, 1 - c
        elif which == "y":
            y = 1 - y
        else:
            z = (z + which) % LINE
        return (x * 2 + c, z * 2 + y)

    def greet(self, peers):
        barrier = pltpu.get_barrier_semaphore()
        for peer in peers:
            pl.semaphore_signal(barrier, inc=1, device_id=self.near(peer), device_id_type=MESH)
        pl.semaphore_wait(barrier, len(peers))

    def remote(self, row, slot, source, target, peer):
        return pltpu.make_async_remote_copy(
            src_ref=source,
            dst_ref=target,
            send_sem=self.send.at[row, slot],
            recv_sem=self.recv.at[row, slot],
            device_id=self.near(peer),
            device_id_type=MESH,
        )

    def stay(self, row, source, target):
        return pltpu.make_async_copy(source, target, self.local.at[row])


class Gather:
    def __init__(self, net, row, own, whole, share, split=2):
        self.net, self.row, self.own, self.whole, self.share = net, row, own, whole, share
        self.split = split

    def copy(self, slot):
        net, whole = self.net, self.whole
        x, y, z = net.x, net.y, net.z
        if slot < 3:
            return net.remote(self.row, slot, self.own(x), whole(z, y, x), slot + 1)
        if slot < 6:
            piece = whole((z + LINE - (slot - 2)) % LINE, y, x)
            return net.remote(self.row, slot, piece, piece, "x")
        if slot == 6:
            piece, peer = whole(ALL, y, x), "y"
        elif slot == 7:
            piece, peer = whole(slice(0, self.split), 1 - y, x), "x"
        elif slot == 8:
            piece, peer = whole(slice(self.split, 4), y, 1 - x), "y"
        else:
            piece, peer = whole(ALL, ALL, ALL), "c"
        return net.remote(self.row, slot, piece, piece, peer)

    def home(self):
        return self.net.stay(self.row, self.own(ALL), self.whole(self.net.z, self.net.y, ALL))

    def step(self, number):
        if number == 0:
            self.home().start()
            for slot in range(3):
                self.copy(slot).start()
        elif number == 1:
            self.home().wait()
            for slot in range(3):
                self.copy(slot).wait_recv()
            for slot in range(3, 7):
                self.copy(slot).start()
        elif number == 2:
            for slot in range(3, 7):
                self.copy(slot).wait_recv()
            for slot in (7, 8):
                self.copy(slot).start()
        elif number == 3:
            for slot in (7, 8):
                self.copy(slot).wait_recv()
            if self.share:
                self.copy(9).start()
        elif number == 4:
            if self.share:
                self.copy(9).wait_recv()

    def finish(self):
        for slot in range(10 if self.share else 9):
            self.copy(slot).wait_send()


class Scatter:
    def __init__(self, net, row, load, part, twin, twin_load, first, second, third, final):
        self.net, self.row, self.load, self.part = net, row, load, part
        self.twin, self.twin_load = twin, twin_load
        self.first, self.second, self.third, self.final = first, second, third, final

    def copy(self, slot):
        net, part = self.net, self.part
        x, y, z, c = net.x, net.y, net.z, net.c
        if slot == 0:
            return net.remote(self.row, slot, self.twin_load, self.twin, "c")
        if slot == 1:
            return net.remote(self.row, slot, part.at[0:1, 1 - y, 1 - x], self.first.at[0:1], "x")
        if slot == 2:
            return net.remote(self.row, slot, part.at[1:4, 1 - y, 1 - x], self.first.at[1:4], "y")
        if slot == 3:
            return net.remote(self.row, slot, part.at[:, y, 1 - x], self.second.at[0], "x")
        if slot == 4:
            return net.remote(self.row, slot, part.at[:, 1 - y, x], self.second.at[1], "y")
        if slot < 8:
            step = slot - 4
            piece = part.at[(z + step) % LINE, y, x]
            return net.remote(self.row, slot, piece, self.third.at[step - 1], step)
        if slot < 10:
            return net.remote(self.row, slot, part.at[z, y, x], self.final(x, c), "xc"[slot - 8])
        piece = self.final(1 - x, c)
        return net.remote(self.row, slot, piece, piece, "c")

    def home(self):
        return self.net.stay(self.row, self.load, self.part)

    def keep(self):
        net = self.net
        piece = self.part.at[net.z, net.y, net.x]
        return net.stay(self.row, piece, self.final(net.x, net.c))

    def step(self, number):
        net, part = self.net, self.part
        x, y, z = net.x, net.y, net.z
        if number == 0:
            if self.load is not None:
                self.home().start()
            if self.twin is not None:
                self.copy(0).start()
        elif number == 1:
            if self.load is not None:
                self.home().wait()
            if self.twin is not None:
                self.copy(0).wait_recv()
                for a in range(LINE):
                    part[a] = part[a] + self.twin[a]
            self.copy(1).start()
            self.copy(2).start()
        elif number == 2:
            self.copy(1).wait_recv()
            part[0, 1 - y, x] = part[0, 1 - y, x] + self.first[0]
            self.copy(2).wait_recv()
            part[1:4, y, 1 - x] = part[1:4, y, 1 - x] + self.first[1:4]
            self.copy(3).start()
            self.copy(4).start()
        elif number == 3:
            self.copy(3).wait_recv()
            self.copy(4).wait_recv()
            mine = part[:, y, x].astype(F32) + self.second[0].astype(F32)
            part[:, y, x] = (mine + self.second[1].astype(F32)).astype(BF)
            for slot in (5, 6, 7):
                self.copy(slot).start()
        elif number == 4:
            total = part[z, y, x].astype(F32)
            for slot in (5, 6, 7):
                self.copy(slot).wait_recv()
                total = total + self.third[slot - 5].astype(F32)
            part[z, y, x] = total.astype(BF)
            for slot in (8, 9):
                self.copy(slot).start()
            self.keep().start()
        elif number == 5:
            self.keep().wait()
            self.copy(8).wait_recv()
            self.copy(10).start()
        elif number == 6:
            for slot in (9, 10):
                self.copy(slot).wait_recv()

    def finish(self):
        for slot in range(0 if self.twin is not None else 1, 11):
            self.copy(slot).wait_send()


def copy_semaphores(rows, slots):
    return [
        pltpu.SemaphoreType.DMA((rows, slots)),
        pltpu.SemaphoreType.DMA((rows, slots)),
        pltpu.SemaphoreType.DMA((rows,)),
    ]


def run_plan(plan, slot, total):
    for number in range(total):
        steps = [entry for entry in plan if int(entry[0]) == number]
        if steps:

            @pl.when(slot == number)
            def _(steps=steps):
                for _, chunk, step in steps:
                    chunk.step(step)


def run_rest(plan, total):
    for time, chunk, step in plan:
        if time >= total:
            chunk.step(step)


def pick_kernel(order_ref, low_ref, high_ref, out_ref, sems):
    count = low_ref.shape[0]
    for i in range(out_ref.shape[0]):
        at = order_ref[i]

        @pl.when(at < count)
        def _(i=i, at=at):
            pltpu.make_async_copy(low_ref.at[at], out_ref.at[i], sems.at[i]).start()

        @pl.when(at >= count)
        def _(i=i, at=at):
            pltpu.make_async_copy(high_ref.at[at - count], out_ref.at[i], sems.at[i]).start()

    for i in range(out_ref.shape[0]):
        pltpu.make_async_copy(low_ref.at[0], out_ref.at[i], sems.at[i]).wait()


def pick(order, low, high):
    count = order.shape[0]
    return pl.pallas_call(
        pick_kernel,
        name="pick",
        in_specs=[SMEM, ANY, ANY],
        out_specs=VMEM,
        out_shape=jax.ShapeDtypeStruct((count,) + low.shape[1:], low.dtype),
        scratch_shapes=[pltpu.SemaphoreType.DMA((count,))],
        compiler_params=pltpu.CompilerParams(vmem_limit_bytes=VMEM_LIMIT),
    )(order, low, high)


class Sharing:
    def __init__(self, net, row, own, tree, stage=None):
        self.net, self.row, self.own, self.tree, self.stage = net, row, own, tree, stage

    def copy(self, slot):
        net, own, tree = self.net, self.own, self.tree
        count = own.shape[1]
        half = count // 2
        part = pl.ds((slot % 2) * half, half)
        place = tree.at[pl.ds(net.leaf * count + (slot % 2) * half, half)]
        if slot < 2:
            return net.remote(self.row, slot, own.at[1 - net.x, part], place, "x")
        if slot < 4:
            return net.remote(self.row, slot, own.at[net.x, part], place, "c")
        place = tree.at[pl.ds((net.leaf + 2) % 4 * count + (slot % 2) * half, half)]
        return net.remote(self.row, slot, place, place, "c")

    def home(self):
        count = self.own.shape[1]
        source = self.own.at[self.net.x] if self.stage is None else self.stage
        return self.net.stay(self.row, source, self.tree.at[pl.ds(self.net.leaf * count, count)])

    def load(self):
        return self.net.stay(self.row + 1, self.own.at[self.net.x], self.stage)

    def step(self, number):
        if number == 0:
            for slot in range(4):
                self.copy(slot).start()
            if self.stage is not None:
                self.load().wait()
            self.home().start()
        elif number < 3:
            self.copy(number - 1).wait_recv()
            self.copy(number + 3).start()
        elif number == 3:
            for slot in (2, 3, 4, 5):
                self.copy(slot).wait_recv()
            self.home().wait()

    def finish(self):
        for slot in range(6):
            self.copy(slot).wait_send()


class Flush:
    def __init__(self, net, row, source, target):
        self.move = lambda: net.stay(row, source, target)

    def step(self, number):
        self.move().start()

    def finish(self):
        self.move().wait()


class WideGather(Gather):
    def copy(self, slot):
        net, whole = self.net, self.whole
        if slot < 3:
            piece = whole(net.z, net.y, ALL)
            return net.remote(self.row, slot, self.own(ALL), piece, slot + 1)
        if slot == 3:
            piece, peer = whole(ALL, net.y, ALL), "y"
        else:
            piece, peer = whole(ALL, ALL, ALL), "c"
        return net.remote(self.row, slot, piece, piece, peer)

    def step(self, number):
        if number == 0:
            self.home().start()
            for slot in range(3):
                self.copy(slot).start()
        elif number == 1:
            self.home().wait()
            for slot in range(3):
                self.copy(slot).wait_recv()
            self.copy(3).start()
        elif number == 2:
            self.copy(3).wait_recv()
            if self.share:
                self.copy(4).start()
        elif number == 4:
            if self.share:
                self.copy(4).wait_recv()

    def finish(self):
        for slot in range(5 if self.share else 4):
            self.copy(slot).wait_send()


class FarGather(Gather):
    def __init__(self, net, row, own, whole, share, split, stage, spare):
        super().__init__(net, row, own, whole, share, split)
        self.stage, self.spare = stage, spare

    def load(self):
        return self.net.stay(self.spare, self.own(ALL), self.stage)

    def home(self):
        return self.net.stay(self.row, self.stage, self.whole(self.net.z, self.net.y, ALL))

    def step(self, number):
        if number == 0:
            self.load().wait()
        super().step(number)


FRONT = dict(
    pace=4.4,
    lead=5.0,
    lag1=9.0,
    lag2=11.0,
    lag3=11.0,
    lag4=8.0,
    origin=34.0,
    join=1.0,
    attend=1.55,
    norm=1.2,
    rise=1.0,
    splits=(2,),
    wide=(),
    upstream=(90.0, 102.0, 110.0, 122.0),
)


def front_kernel(
    block,
    order_ref,
    entry_ref,
    upstream_ref,
    joined_shard,
    scores_ref,
    jitter_ref,
    scale_ref,
    out_shard,
    up_shard,
    down_shard,
    vectors_ref,
    tokens_out,
    joined_out,
    query_out,
    key_out,
    value_out,
    mask_out,
    attended_out,
    log_out,
    whole_out,
    out_out,
    up_out,
    down_out,
    tree_out,
    normed_out,
    inv_out,
    active_out,
    slope_out,
    small_out,
    rise_bias_out,
    entry_tree,
    tokens_ref,
    joined_weight,
    query_ref,
    key_ref,
    value_ref,
    mask_ref,
    attended_ref,
    log_ref,
    whole_ref,
    out_weight,
    up_weight,
    normed_ref,
    low_ref,
    active_ref,
    slope_ref,
    packed_ref,
    down_stage,
    upstream_stage,
    scores_own,
    jitter_own,
    relaxed_ref,
    *sems,
):
    net = Net(*sems)
    c, y, z = net.c, net.y, net.z
    trunk = TRUNK * block
    wide = 3 * block
    low = low_lanes()
    rows_all, mine = query_ref.shape
    width = tokens_ref.shape[2]
    blocks = tokens_ref.shape[0]
    pairs = mine // (2 * LOW_HALF)
    heads = relaxed_ref.shape[0]
    half = rows_all // 2
    expand = up_weight.shape[4]
    splits = FRONT["splits"]
    chunks = []

    def add(own, whole, share):
        split = splits[len(chunks) % len(splits)]
        kind = WideGather if len(chunks) in FRONT["wide"] else Gather
        chunks.append(kind(net, len(chunks), own, whole, share, split))

    def columns(index):
        return pl.ds(pl.multiple_of(index * mine, mine), mine)

    for i in range(3):
        add(
            lambda part, i=i: joined_shard.at[part, :, columns(2 * i + c)],
            lambda a, b, part, i=i: joined_weight.at[a, b, part, :, columns(i)],
            False,
        )
    for h in range(heads):
        add(
            lambda part, h=h: relaxed_ref.at[h, part],
            lambda a, b, part, h=h: mask_ref.at[h, a, b, part],
            False,
        )
    add(
        lambda part: out_shard.at[part, :, columns(c)],
        lambda a, b, part: out_weight.at[a, b, part, :, columns(c)],
        True,
    )
    for j in range(4):
        add(
            lambda part, j=j: up_shard.at[part, :, columns(4 * c + j)],
            lambda a, b, part, j=j: up_weight.at[a, b, part, :, columns(4 * c + j)],
            True,
        )
    spare = len(chunks) + 4
    for j in range(4):
        chunks.append(
            FarGather(
                net,
                len(chunks),
                lambda part, j=j: down_shard.at[j, part, :, columns(c)],
                lambda a, b, part, j=j: down_out.at[a, b, j, part, :, columns(c)],
                True,
                splits[len(chunks) % len(splits)],
                down_stage.at[j],
                spare + j,
            )
        )
    spare += 4
    entry = Sharing(net, spare, entry_ref, entry_tree)
    upstream = Sharing(net, spare + 1, upstream_ref, tree_out, upstream_stage)
    vector_row = spare + 3
    flushes = []
    first_flush = spare + 4

    def flush(source, target):
        flushes.append(Flush(net, first_flush + len(flushes), source, target))
        return flushes[-1]

    def vector_copy(slot):
        if slot < 3:
            return net.remote(vector_row, slot, vectors_ref, packed_ref.at[z, y], slot + 1)
        return net.remote(vector_row, slot, packed_ref.at[:, y], packed_ref.at[:, y], "y")

    class Vectors:
        def home(self):
            return net.stay(vector_row, vectors_ref, packed_ref.at[z, y])

        def step(self, number):
            if number == 0:
                self.home().start()
                for slot in range(3):
                    vector_copy(slot).start()
            elif number == 1:
                self.home().wait()
                for slot in range(3):
                    vector_copy(slot).wait_recv()
                vector_copy(3).start()
            elif number == 2:
                vector_copy(3).wait_recv()

        def finish(self):
            for slot in range(4):
                vector_copy(slot).wait_send()

    vectors = Vectors()
    net.greet(("x", "c", "y", 1, 2, 3))
    for chunk in chunks[-4:]:
        chunk.load().start()
    upstream.load().start()
    own_heads = pl.ds(c * heads, heads)
    mask_loads = [
        net.stay(first_flush + 16, scores_ref.at[own_heads], scores_own),
        net.stay(first_flush + 17, jitter_ref.at[own_heads], jitter_own),
    ]
    for load in mask_loads:
        load.start()

    starts = []
    time = FRONT["origin"]
    for count, length in (
        (blocks // 2, FRONT["join"]),
        (8 * pairs, FRONT["attend"]),
        (half // (2 * block), FRONT["norm"]),
        (2 * (expand // mine), FRONT["rise"]),
    ):
        for _ in range(count):
            starts.append(time)
            time += length
    total = len(starts)
    first_attend = blocks // 2
    first_norm = first_attend + 8 * pairs
    first_rise = first_norm + half // (2 * block)

    plan = []
    for i, chunk in enumerate(chunks):
        start = i * FRONT["pace"]
        limit = 1e9
        if i < 3:
            limit = starts[0]
        elif i < 3 + heads:
            limit = starts[first_attend + 8 * ((i - 3) // 2)]
        elif i == 3 + heads:
            limit = starts[first_norm]
        elif i < 8 + heads:
            limit = starts[first_rise + 4 * (i - 4 - heads)]
        moments = [max(0.0, start - FRONT["lead"]), start + FRONT["lag1"]]
        for lag in ("lag2", "lag3", "lag4"):
            moments.append(moments[-1] + FRONT[lag])
        for step, moment in enumerate(moments):
            plan.append((min(moment, limit - 0.001 * (6 - step)), chunk, step))
    for step, moment in enumerate((0.0, 14.0, 24.0, 30.0)):
        plan.append((min(moment, starts[0] - 0.001), entry, step))
    for step, moment in enumerate((0.1, 9.0, 20.0)):
        plan.append((min(moment, starts[0] - 0.001), vectors, step))
    for step, moment in enumerate(FRONT["upstream"]):
        plan.append((moment, upstream, step))
    after = starts[first_attend] + 0.5
    plan.append((after, flush(joined_weight, joined_out), 0))
    plan.append((after + 2, flush(tokens_ref, tokens_out), 0))
    plan.append((after + 6, flush(query_ref, query_out), 0))
    plan.append((after + 8, flush(key_ref, key_out), 0))
    plan.append((after + 10, flush(value_ref, value_out), 0))
    plan.append((starts[first_attend + 16] + 0.1, flush(mask_ref, mask_out), 0))
    plan.append((starts[first_norm], flush(attended_ref, attended_out), 0))
    plan.append((starts[first_norm], flush(log_ref, log_out), 0))
    plan.append((starts[first_norm], flush(whole_ref, whole_out), 0))
    plan.append((starts[first_norm] + 0.1, flush(out_weight, out_out), 0))
    plan.append((starts[-4] + 0.01, flush(up_weight, up_out), 0))
    plan.append((starts[first_rise] + 1, flush(normed_ref, normed_out), 0))
    plan.sort(key=lambda item: item[0])
    placed = []
    for moment, item, step in plan:
        slot = next((s for s in range(total) if starts[s] > moment), total)
        slot = -1 if moment < starts[0] else max(slot - 1, 0)
        if moment >= starts[-1] + FRONT["rise"]:
            slot = total
        placed.append((slot, item, step))

    def events(slot, first, last, kinds=None):
        for number in range(first, last):
            if kinds is not None and (number - first) % 8 not in kinds:
                continue
            steps = [entry for entry in placed if entry[0] == number]
            if steps:

                @pl.when(slot == number)
                def _(steps=steps):
                    for _, item, step in steps:
                        item.step(step)

    early = [entry for entry in plan if entry[0] < 0.5]
    for _, item, step in early:
        item.step(step)
    for load in mask_loads:
        load.wait()

    def relax(h, carry):
        soft = jax.nn.sigmoid((scores_own[h] + jitter_own[h]) / scale_ref[c * heads + h])
        relaxed_ref[h] = soft.astype(BF).reshape(relaxed_ref.shape[1:])
        return carry

    lax.fori_loop(0, heads, relax, 0)
    for slot, item, step in placed[len(early) :]:
        if slot < 0:
            item.step(step)

    shard = width // 8
    lane = lax.broadcasted_iota(jnp.int32, (128, width), 1)
    line = lax.broadcasted_iota(jnp.int32, (128, width), 0)
    assembled = jnp.zeros((16, width), F32)
    for f in range(8):
        place = jnp.where((lane == line + shard * f) & (line < shard), 1.0, 0.0).astype(BF)
        assembled = assembled + dot_nn(packed_ref[f // 2, f % 2], place)
        for m in range(3):
            at = (f * 3 + m) * 128
            rise_bias_out[0:1, at : at + 128] = packed_ref[f // 2, f % 2, 8 + m : 9 + m, :].astype(F32)
    small_out[...] = assembled

    def project(i, carry):
        events(i, 0, first_attend)
        tokens_ref[2 * i] = entry_tree[order_ref[2 * i]]
        tokens_ref[2 * i + 1] = entry_tree[order_ref[2 * i + 1]]
        rows = pl.ds(pl.multiple_of(2 * block * i, 2 * block), 2 * block)
        pair = tokens_ref[pl.ds(2 * i, 2)].reshape(2 * block, width)
        joined = dot_nn(pair, joined_weight[...].reshape(width, 3 * mine))
        query = (joined[:, :mine] + small_out[0:1, columns(c)]).astype(BF).astype(F32)
        query_ref[rows, :] = (query * (1.0 / math.sqrt(LOW_HALF))).astype(BF)
        key_ref[rows, :] = joined[:, mine : 2 * mine].astype(BF)
        value_ref[rows, :] = (joined[:, 2 * mine :] + small_out[1:2, columns(c)]).astype(BF)
        return carry

    lax.fori_loop(0, blocks // 2, project, 0)

    def soften(parts, masks, values):
        top = parts[0].max(axis=1, keepdims=True)
        for part in parts[1:]:
            top = jnp.maximum(top, part.max(axis=1, keepdims=True))
        scale = 0.0
        out = 0.0
        for part, mask, value in zip(parts, masks, values):
            weight = jnp.exp(part - top)
            scale = scale + weight.sum(axis=1, keepdims=True)
            out = out + dot_nn((weight * mask.astype(F32)).astype(BF), value)
        return (out * (1.0 / scale), top + jnp.log(scale))

    def emit(rows, p, lanes, results):
        attended_ref[rows, lanes] = jnp.where(low, results[0][0], results[1][0]).astype(BF)
        logs = log_ref[rows, :]
        for which in range(2):
            logs = jnp.where(lane_row == 2 * p + which, results[which][1], logs)
        log_ref[rows, :] = logs

    lane_row = lax.broadcasted_iota(jnp.int32, (1, 128), 1)
    log_ref[...] = jnp.zeros_like(log_ref)

    def one_pair(p, carry):
        lanes = pl.ds(pl.multiple_of(p * 2 * LOW_HALF, 2 * LOW_HALF), 2 * LOW_HALF)

        def mask_strip(which, tile):
            return mask_ref[2 * p + which, tile].reshape(block, mask_ref.shape[-1])

        def trunk_rows(index, carry):
            for part_slot in range(2):
                slot = first_attend + 8 * p + 2 * index + part_slot
                events(slot, first_attend, first_norm, range(part_slot, 4, 2))
            rows = pl.ds(pl.multiple_of(index * 2 * block, 2 * block), 2 * block)
            query = query_ref[rows, lanes]
            results = []
            for which in range(2):
                strips = [mask_strip(which, 2 * index + s) for s in range(2)]
                mask_rows = jnp.concatenate(strips, axis=0)
                places = [(0, trunk, mask_rows)]
                side = mask_columns(mask_rows, (1, 0, 1), block)
                places += [(trunk + wide * g, wide, side) for g in range(GROUPS)]
                head = one_head(query, which)
                parts = [dot_nt(head, key_ref[a : a + w, lanes]) for a, w, _ in places]
                values = [value_ref[a : a + w, lanes] for a, w, _ in places]
                results.append(soften(parts, [place[2] for place in places], values))
            emit(rows, p, lanes, results)
            return carry

        lax.fori_loop(0, TRUNK // 2, trunk_rows, 0)

        def group_rows(group, carry):
            events(first_attend + 8 * p + 4 + group, first_attend, first_norm, range(4, 8))
            base = pl.multiple_of(trunk + wide * group, block)
            rows = pl.ds(base, wide)
            query = query_ref[rows, lanes]
            results = []
            for which in range(2):
                strips = [mask_strip(which, t) for t in (1, 0, 1)]
                head = one_head(query, which)
                far = dot_nt(head, key_ref[0:trunk, lanes])
                top = far.max(axis=1, keepdims=True)
                near = []
                tops = []
                for row in range(3):
                    start, size, tiles = group_columns(row, block)
                    place = pl.ds(pl.multiple_of(base + start, block), size)
                    at = slice(row * block, (row + 1) * block)
                    part = dot_nt(head[at], key_ref[place, lanes])
                    near.append((part, place, mask_columns(strips[row], tiles, block)))
                    tops.append(jnp.maximum(top[at], part.max(axis=1, keepdims=True)))
                top = jnp.concatenate(tops, axis=0)
                weight = jnp.exp(far - top)
                mask_rows = jnp.concatenate(strips, axis=0).astype(F32)
                scale = weight.sum(axis=1, keepdims=True)
                out = dot_nn((weight * mask_rows).astype(BF), value_ref[0:trunk, lanes])
                scales = []
                outs = []
                for row, (part, place, mask) in enumerate(near):
                    weight = jnp.exp(part - tops[row])
                    scales.append(weight.sum(axis=1, keepdims=True))
                    weight = (weight * mask.astype(F32)).astype(BF)
                    outs.append(dot_nn(weight, value_ref[place, lanes]))
                scale = scale + jnp.concatenate(scales, axis=0)
                out = (out + jnp.concatenate(outs, axis=0)) * (1.0 / scale)
                results.append((out, top + jnp.log(scale)))
            emit(rows, p, lanes, results)
            return carry

        lax.fori_loop(0, GROUPS, group_rows, 0)
        return carry

    lax.fori_loop(0, pairs, one_pair, 0)
    mine_rows = pl.ds(pl.multiple_of(c * half, half), half)
    their_rows = pl.ds(pl.multiple_of((1 - c) * half, half), half)
    cross = net.remote(vector_row, 4, attended_ref.at[their_rows], whole_ref.at[:, columns(c)], "c")
    cross.start()
    whole_ref[:, columns(c)] = attended_ref[mine_rows, :]
    cross.wait_recv()

    def normalize(i, carry):
        events(first_norm + i, first_norm, first_rise)
        rows = pl.ds(pl.multiple_of(i * 2 * block, 2 * block), 2 * block)
        pair = tokens_ref[pl.ds(c * (blocks // 2) + 2 * i, 2)].reshape(2 * block, width)
        first = pair.astype(F32) + small_out[2:3, :]
        first = first + dot_nn(whole_ref[rows, :], out_weight[...].reshape(width, width))
        average = jnp.mean(first, axis=1, keepdims=True)
        centred = first - average
        inv = lax.rsqrt(jnp.mean(centred * centred, axis=1, keepdims=True) + EPSILON)
        normed = centred * inv
        normed_ref[rows, :] = normed
        inv_out[rows, :] = jnp.broadcast_to(inv, (2 * block, 128))
        low_ref[rows, :] = (normed * small_out[3:4, :] + small_out[4:5, :]).astype(BF)
        return carry

    lax.fori_loop(0, half // (2 * block), normalize, 0)
    per = expand // mine

    def rise_place(i):
        rows = pl.ds(pl.multiple_of((i % 2) * (half // 2), half // 2), half // 2)
        return rows, columns((per // 2) * (i // 2 % 2) + i // 4)

    def out_copies(i):
        row = first_flush + len(flushes)
        slot = i % 2
        rows, place = rise_place(i)
        return (
            net.stay(row + slot, active_ref.at[slot], active_out.at[rows, place]),
            net.stay(row + 2 + slot, slope_ref.at[slot], slope_out.at[rows, place]),
        )

    def rise(i, carry):
        events(first_rise + i, first_rise, total)
        rows, place = rise_place(i)
        upper = dot_nn(low_ref[rows, :], up_weight[:, :, :, :, place].reshape(width, mine))
        active, slope = gelu_parts(upper + rise_bias_out[0:1, place])

        @pl.when(i >= 2)
        def _():
            for copy in out_copies(i - 2):
                copy.wait()

        active_ref[i % 2] = active.astype(BF)
        slope_ref[i % 2] = slope.astype(BF)
        for copy in out_copies(i):
            copy.start()
        return carry

    lax.fori_loop(0, 2 * per, rise, 0)
    for slot, item, step in placed:
        if slot == total:
            item.step(step)
    for i in (2 * per - 2, 2 * per - 1):
        for copy in out_copies(i):
            copy.wait()
    for item in chunks + [entry, upstream, vectors] + flushes:
        item.finish()
    cross.wait_send()


def front(
    order, entry, upstream, joined, scores, jitter, scale, out_shard, up_shard, down_shard, vectors
):
    micro, own_blocks, block, width = entry.shape
    own_rows = own_blocks * block
    rows = 4 * own_rows
    half = rows // 2
    blocks = rows // block
    mine = width // CORES
    heads = scores.shape[0] // CORES
    strip, span = scores.shape[1:]
    expand = up_shard.shape[2]
    like = jax.ShapeDtypeStruct
    grown = lambda shard: (LINE, 2) + shard.shape
    joined_shape = (LINE, 2) + joined.shape[:2] + (3 * mine,)
    mask_shape = (heads, LINE, 2, 2, strip // 2, span)
    vmem = lambda shape, kind=BF: pltpu.VMEM(shape, kind)
    return pl.pallas_call(
        functools.partial(front_kernel, block),
        name="front",
        in_specs=[SMEM] + [ANY] * 5 + [SMEM] + [ANY] * 4,
        out_specs=[ANY] * 14 + [VMEM] + [ANY] * 2 + [VMEM] * 2,
        out_shape=[
            like((blocks, block, width), BF),
            like(joined_shape, BF),
            like((rows, mine), BF),
            like((rows, mine), BF),
            like((rows, mine), BF),
            like(mask_shape, BF),
            like((rows, mine), BF),
            like((rows, 128), F32),
            like((half, width), BF),
            like(grown(out_shard), BF),
            like(grown(up_shard), BF),
            like(grown(down_shard), BF),
            like((blocks, block, width), BF),
            like((half, width), F32),
            like((half, 128), F32),
            like((half, expand), BF),
            like((half, expand), BF),
            like((16, width), F32),
            like((1, expand), F32),
        ],
        scratch_shapes=[
            vmem((blocks, block, width)),
            vmem((blocks, block, width)),
            vmem(joined_shape),
            vmem((rows, mine)),
            vmem((rows, mine)),
            vmem((rows, mine)),
            vmem(mask_shape),
            vmem((rows, mine)),
            vmem((rows, 128), F32),
            vmem((half, width)),
            vmem(grown(out_shard)),
            vmem(grown(up_shard)),
            vmem((half, width), F32),
            vmem((half, width)),
            vmem((2, half // 2, mine)),
            vmem((2, half // 2, mine)),
            vmem((LINE, 2) + vectors.shape, vectors.dtype),
            vmem((4, 2, down_shard.shape[2], mine)),
            vmem(entry.shape[1:]),
            vmem((heads, strip, span), F32),
            vmem((heads, strip, span), F32),
            vmem((heads, 2, strip // 2, span)),
        ]
        + copy_semaphores(48, 10),
        compiler_params=pltpu.CompilerParams(
            collective_id=4, has_side_effects=True, vmem_limit_bytes=VMEM_LIMIT
        ),
    )(order, entry, upstream, joined, scores, jitter, scale, out_shard, up_shard, down_shard, vectors)


def scatter_buffers(count, shape, with_twin):
    half, columns = shape
    whole = pltpu.VMEM((count, LINE, 2, 2, half, columns), BF)
    line = pltpu.VMEM((count, LINE, half, columns), BF)
    return (
        [whole]
        + ([whole] if with_twin else [])
        + [
            line,
            pltpu.VMEM((count, 2, LINE, half, columns), BF),
            pltpu.VMEM((count, LINE - 1, half, columns), BF),
        ]
    )


REAR = dict(pace=4.0, lag=21.0, tail=4.5, attend=3.6, finish=5.0, spread=0.6)


def rear_kernel(
    block,
    scale,
    query_ref,
    key_ref,
    value_ref,
    mask_ref,
    out_ref,
    log_ref,
    joined_weight,
    small_ref,
    place_ref,
    delta_half,
    tokens_in,
    first_in,
    out_grad,
    up_grad,
    down_grad,
    layer_in,
    out_final,
    up_final,
    down_final,
    mask_final,
    joined_final,
    tokens_out,
    small_out,
    layer_out,
    delta_ref,
    key_sum,
    value_sum,
    query_turned,
    delta_turned,
    dmask_sum,
    dquery_ref,
    dkey_ref,
    dvalue_ref,
    tokens_ref,
    first_ref,
    part,
    first,
    second,
    third,
    joined_part,
    joined_first,
    joined_second,
    joined_third,
    mask_part,
    mask_first,
    mask_second,
    mask_third,
    give,
    keep,
    got,
    sums,
    from_peers,
    *sems,
):
    net = Net(*sems)
    x, c = net.x, net.c
    trunk = TRUNK * block
    wide = 3 * block
    low = low_lanes()
    lane = lax.broadcasted_iota(jnp.int32, (1, 128), 1)
    rows_all, mine = query_ref.shape
    blocks, _, width = tokens_ref.shape
    pairs = mine // (2 * LOW_HALF)
    heads = mask_ref.shape[0]
    half = rows_all // 2
    strip = mask_final.shape[3]
    chunks = []

    def own(index):
        return pl.ds(pl.multiple_of(index * mine, mine), mine)

    def dense(load, twin_load, final):
        k = len(chunks)
        twin = joined_part.at[k] if k < 3 else mask_part.at[k - 3, :, :, :, :, 0:mine]
        buffers = (first.at[k], second.at[k], third.at[k])
        chunks.append(Scatter(net, k, load, part.at[k], twin, twin_load, *buffers, final))

    dense(
        out_grad.at[:, :, :, :, own(c)],
        out_grad.at[:, :, :, :, own(1 - c)],
        lambda a, b: out_final.at[a, :, own(b)],
    )
    for j in range(4):
        dense(
            down_grad.at[:, :, j, :, :, own(c)],
            down_grad.at[:, :, j, :, :, own(1 - c)],
            lambda a, b, j=j: down_final.at[j, a, :, own(b)],
        )
    for j in range(4):
        dense(
            up_grad.at[:, :, :, :, own(4 * c + j)],
            up_grad.at[:, :, :, :, own(4 * (1 - c) + j)],
            lambda a, b, j=j: up_final.at[a, :, own(4 * b + j)],
        )
    dense_count = len(chunks)
    for p in range(pairs):
        for h in (2 * p, 2 * p + 1):
            buffers = (mask_first.at[h], mask_second.at[h], mask_third.at[h])
            chunks.append(
                Scatter(
                    net,
                    len(chunks),
                    None,
                    mask_part.at[h, :, :, :, 0:strip],
                    None,
                    None,
                    *buffers,
                    lambda a, b, h=h: mask_final.at[b, h, a],
                )
            )
        buffers = (joined_first.at[p], joined_second.at[p], joined_third.at[p])
        chunks.append(
            Scatter(
                net,
                len(chunks),
                None,
                joined_part.at[p],
                None,
                None,
                *buffers,
                lambda a, b, p=p: joined_final.at[p, a, b],
            )
        )
    spare = len(chunks)
    net.greet(("x", "c", "y", 1, 2, 3))

    mine_rows = pl.ds(pl.multiple_of(c * half, half), half)
    delta_cross = net.remote(spare, 0, delta_half.at[:, own(1 - c)], delta_ref.at[mine_rows], "c")
    delta_cross.start()
    delta_home = net.stay(spare, delta_half.at[:, own(c)], delta_ref.at[mine_rows])
    delta_home.start()
    tokens_load = net.stay(spare + 1, tokens_in, tokens_ref)
    first_load = net.stay(spare + 2, first_in, first_ref)
    tokens_load.start()
    own_blocks = blocks // 4
    layer_home = net.stay(spare + 3, layer_in.at[0:own_blocks], layer_out.at[x])
    layer_home.start()
    layer_cross = net.remote(spare, 3, layer_in.at[own_blocks:], layer_out.at[x], "x")
    layer_cross.start()

    own_rows = give.shape[1]
    per = own_rows // block

    def collect(target, core):
        for a in range(2):
            for b in range(per):
                place = place_ref[(2 * a + core) * per + b]
                target[a, b * block : (b + 1) * block] = tokens_ref[place]

    class Tokens:
        def core(self):
            return net.remote(spare, 1, give, got, "c")

        def chip(self):
            return net.remote(spare, 2, keep.at[1 - x], tokens_out.at[x], "x")

        def step(self, number):
            if number == 0:
                collect(give, 1 - c)
                self.core().start()
                collect(keep, c)
            elif number == 1:
                self.core().wait_recv()
                keep[...] = (keep[...].astype(F32) + got[...].astype(F32)).astype(BF)
                self.chip().start()
                tokens_out[x] = keep[x]
            elif number == 2:
                self.chip().wait_recv()

        def finish(self):
            self.core().wait_send()
            self.chip().wait_send()

    class Vectors:
        def copy(self, slot):
            peer = ("c", "x", "y", 1, 2, 3)[slot]
            source = sums.at[min(slot, 3)]
            return net.remote(spare + 1, slot, source, from_peers.at[slot], peer)

        def step(self, number):
            if number == 0:
                self.copy(0).start()
            elif number < 3:
                self.copy(number - 1).wait_recv()
                sums[number] = sums[number - 1] + from_peers[number - 1]
                self.copy(number).start()
            elif number == 3:
                self.copy(2).wait_recv()
                sums[3] = sums[2] + from_peers[2]
                for slot in (3, 4, 5):
                    self.copy(slot).start()
            elif number == 4:
                total = sums[3]
                for slot in (3, 4, 5):
                    self.copy(slot).wait_recv()
                    total = total + from_peers[slot]
                small_out[...] = total

        def finish(self):
            for slot in range(6):
                self.copy(slot).wait_send()

    home = Tokens()
    vectors = Vectors()
    starts = []
    ready = []
    time = 0.0
    for p in range(pairs):
        for _ in range(8):
            starts.append(time)
            time += REAR["attend"]
        time += REAR["finish"]
        ready.append(time)
    first_spread = len(starts)
    for _ in range(blocks // 2):
        starts.append(time)
        time += REAR["spread"]
    total = len(starts)
    end = time
    plan = []
    for i, chunk in enumerate(chunks):
        if i < dense_count:
            moments = [0.0, min(1.0 + i * REAR["pace"], ready[0] - REAR["finish"] - 0.01)]
        else:
            p = (i - dense_count) // 3
            start = max(i * REAR["pace"], ready[p] + 0.01 + 0.1 * ((i - dense_count) % 3))
            moments = [start, start]
        lag = REAR["lag"] if i < dense_count + 3 * (pairs - 1) else REAR["tail"]
        for _ in range(4):
            moments.append(moments[-1] + lag)
        moments.append(1000.0 + i)
        for step, moment in enumerate(moments):
            plan.append((moment + 0.001 * step, chunk, step))
    for step, moment in enumerate((0.0, 4.0, 24.0)):
        plan.append((end + moment, home, step))
    for step in range(5):
        plan.append((end + 3.0 + 6.0 * step, vectors, step))
    plan.sort(key=lambda item: item[0])
    placed = []
    for moment, item, step in plan:
        slot = next((s for s in range(total) if starts[s] > moment), total) - 1
        placed.append((total if moment >= end else slot, item, step))

    def events(slot, begin, until, kinds=None):
        for number in range(begin, until):
            if kinds is not None and (number - begin) % 8 not in kinds:
                continue
            steps = [entry for entry in placed if entry[0] == number]
            if steps:

                @pl.when(slot == number)
                def _(steps=steps):
                    for _, item, step in steps:
                        item.step(step)

    sums[0] = small_ref[...]
    tokens_load.wait()
    first_load.start()
    delta_home.wait()
    delta_cross.wait_recv()

    def one_pair(p, carry):
        pair_lanes = pl.ds(pl.multiple_of(p * 2 * LOW_HALF, 2 * LOW_HALF), 2 * LOW_HALF)
        key_sum[...] = jnp.zeros_like(key_sum)
        value_sum[...] = jnp.zeros_like(value_sum)
        dmask_sum[...] = jnp.zeros_like(dmask_sum)
        query_turned[...] = query_ref[:, pair_lanes].astype(F32).T.astype(BF)
        delta_turned[...] = delta_ref[:, pair_lanes].astype(F32).T.astype(BF)

        def cell(which, query_head, delta_head, log, row_term, mask, place, rows):
            lanes = slice(LOW_HALF * which, LOW_HALF * which + LOW_HALF)
            key = key_ref[place, pair_lanes]
            probs = jnp.exp(dot_nt(query_head, key) - log)
            pair = dot_nt(delta_head, value_ref[place, pair_lanes]) * probs
            mask = mask.astype(F32)
            dscores = (pair * mask - probs * row_term).astype(BF)
            weights = (probs * mask).astype(BF)
            key_sum[lanes, place] += dot_nn(query_turned[lanes, rows], dscores)
            value_sum[lanes, place] += dot_nn(delta_turned[lanes, rows], weights)
            return dot_nn(dscores, key), pair

        def heads_of(rows):
            query = query_ref[rows, pair_lanes]
            delta = delta_ref[rows, pair_lanes]
            product = delta.astype(F32) * out_ref[rows, pair_lanes].astype(F32)
            logs = log_ref[rows, :]
            for which in range(2):
                log = jnp.sum(jnp.where(lane == 2 * p + which, logs, 0.0), axis=1, keepdims=True)
                lanes = slice(LOW_HALF * which, LOW_HALF * which + LOW_HALF)
                row_term = jnp.sum(product[:, lanes], axis=1, keepdims=True)
                yield which, one_head(query, which), one_head(delta, which), log, row_term

        def fold(which, mask_place, pair, tiles):
            for tile in sorted(set(tiles)):
                dmask_sum[which, mask_place, tile * block : (tile + 1) * block] += sum(
                    pair[:, a * block : (a + 1) * block] for a, t in enumerate(tiles) if t == tile
                )

        def finish_rows(rows, dqueries):
            both = jnp.where(low, dqueries[0], dqueries[1]) * scale
            dquery_ref[rows, pair_lanes] = both.astype(BF)

        def trunk_rows(index, carry):
            for part_slot in range(2):
                events(8 * p + 2 * index + part_slot, 0, first_spread, range(part_slot, 4, 2))
            rows = pl.ds(pl.multiple_of(index * 2 * block, 2 * block), 2 * block)
            dqueries = []
            for which, query_head, delta_head, log, row_term in heads_of(rows):
                mask_rows = mask_ref[2 * p + which, rows, :]
                near = (query_head, delta_head, log, row_term)
                dquery, pair = cell(which, *near, mask_rows, pl.ds(0, trunk), rows)
                dmask_sum[which, rows, :] += pair
                side = mask_columns(mask_rows, (1, 0, 1), block)
                for g in range(GROUPS):
                    more, pair = cell(which, *near, side, pl.ds(trunk + wide * g, wide), rows)
                    dquery = dquery + more
                    fold(which, rows, pair, (1, 0, 1))
                dqueries.append(dquery)
            finish_rows(rows, dqueries)
            return carry

        lax.fori_loop(0, TRUNK // 2, trunk_rows, 0)

        def group_rows(group, carry):
            events(8 * p + 4 + group, 0, first_spread, range(4, 8))
            base = pl.multiple_of(trunk + wide * group, block)
            rows = pl.ds(base, wide)
            dqueries = []
            for which, query_head, delta_head, log, row_term in heads_of(rows):
                strips = [mask_ref[2 * p + which, t * block : (t + 1) * block, :] for t in (1, 0, 1)]
                mask_rows = jnp.concatenate(strips, axis=0)
                dquery, pair = cell(
                    which, query_head, delta_head, log, row_term, mask_rows, pl.ds(0, trunk), rows
                )
                dmask_sum[which, block : 2 * block, :] += pair[0:block] + pair[2 * block :]
                dmask_sum[which, 0:block, :] += pair[block : 2 * block]
                near = []
                for row in range(3):
                    at = slice(row * block, (row + 1) * block)
                    start, size, tiles = group_columns(row, block)
                    tile = 0 if row == 1 else 1
                    more, pair = cell(
                        which,
                        query_head[at],
                        delta_head[at],
                        log[at],
                        row_term[at],
                        mask_columns(strips[row], tiles, block),
                        pl.ds(pl.multiple_of(base + start, block), size),
                        pl.ds(pl.multiple_of(base + row * block, block), block),
                    )
                    fold(which, pl.ds(tile * block, block), pair, tiles)
                    near.append(more)
                dqueries.append(dquery + jnp.concatenate(near, axis=0))
            finish_rows(rows, dqueries)
            return carry

        lax.fori_loop(0, GROUPS, group_rows, 0)
        dkey_ref[:, pair_lanes] = key_sum[...].T.astype(BF)
        dvalue_ref[:, pair_lanes] = value_sum[...].T.astype(BF)
        query_turned[...] = dquery_ref[:, pair_lanes].astype(F32).T.astype(BF)
        place = pl.ds(pl.multiple_of(c * mine + p * 128, 128), 128)
        for row, source in ((0, dquery_ref), (1, dvalue_ref)):
            column = jnp.sum(source[:, pair_lanes].astype(F32), axis=0, keepdims=True)
            sums[0, row : row + 1, place] = column
        tokens = tokens_ref[...].reshape(rows_all, width)
        for t, source in enumerate((query_turned, key_sum, value_sum)):
            grad = dot_nn(source[...].astype(BF), tokens).T.astype(BF)
            columns = slice(t * 128, t * 128 + 128)
            joined_part[p, :, :, :, :, columns] = grad.reshape(joined_part.shape[1:5] + (128,))
        shape = mask_part.shape[2:4] + (strip, mask_part.shape[5])
        for which in range(2):
            for tile in range(LINE):
                rows = dmask_sum[which, tile * block : (tile + 1) * block, :].astype(BF)
                mask_part[2 * p + which, tile, :, :, 0:strip, :] = rows.reshape(shape)
        return carry

    lax.fori_loop(0, pairs, one_pair, 0)
    first_load.wait()

    def spread(i, carry):
        events(first_spread + i, first_spread, total)
        rows = pl.ds(pl.multiple_of(2 * block * i, 2 * block), 2 * block)
        grads = (dquery_ref, dkey_ref, dvalue_ref)
        out = 0.0
        for t, grad in enumerate(grads):
            out = out + dot_nt(grad[rows, :], joined_weight[:, t * mine : (t + 1) * mine])
        inside = (i // (blocks // 4) == c).astype(F32)
        at = i % (blocks // 4)
        out = out + inside * first_ref[pl.ds(2 * at, 2)].reshape(2 * block, width)
        tokens_ref[pl.ds(2 * i, 2)] = out.astype(BF).reshape(2, block, width)
        return carry

    lax.fori_loop(0, blocks // 2, spread, 0)
    for slot, item, step in placed:
        if slot == total:
            item.step(step)
    layer_home.wait()
    layer_cross.wait_recv()
    layer_cross.wait_send()
    for item in chunks + [home, vectors]:
        item.finish()
    delta_cross.wait_send()


def rear(
    query, key, value, mask, out, logs, weight, small, place, delta, tokens, first, out_grad, up_grad,
    down_grad, layer, block, scale
):
    rows, mine = query.shape
    width = 2 * mine
    heads, span, _ = mask.shape
    pairs = heads // 2
    blocks = rows // block
    own_rows = rows // 4
    strip = span // 16
    piece = out_grad.shape[3]
    like = jax.ShapeDtypeStruct
    vmem = lambda shape, kind=BF: pltpu.VMEM(shape, kind)
    mask_buffers = scatter_buffers(heads, (strip, span), False)
    mask_buffers[0] = vmem((heads, LINE, 2, 2, piece, span))
    return pl.pallas_call(
        functools.partial(rear_kernel, block, scale),
        name="rear",
        in_specs=[VMEM] * 8 + [SMEM] + [ANY] * 7,
        out_specs=[VMEM] * 7 + [ANY],
        out_shape=[
            like((2,) + out_grad.shape[3:], BF),
            like((2,) + up_grad.shape[3:], BF),
            like((4, 2) + down_grad.shape[4:], BF),
            like((2, heads, 2, strip, span), BF),
            like((pairs, 2, 2, piece, mine), BF),
            like((2, own_rows, width), BF),
            like(small.shape, F32),
            like((2, blocks // 4, block, width), BF),
        ],
        scratch_shapes=[
            vmem((rows, mine)),
            vmem((2 * LOW_HALF, rows), F32),
            vmem((2 * LOW_HALF, rows), F32),
            vmem((2 * LOW_HALF, rows)),
            vmem((2 * LOW_HALF, rows)),
            vmem((2, span, span), F32),
            vmem((rows, mine)),
            vmem((rows, mine)),
            vmem((rows, mine)),
            vmem(tokens.shape),
            vmem(first.shape, F32),
        ]
        + scatter_buffers(9, (piece, mine), False)
        + scatter_buffers(pairs, (piece, mine), False)
        + mask_buffers
        + [vmem((2, own_rows, width))] * 3
        + [vmem((4,) + small.shape, F32), vmem((6,) + small.shape, F32)]
        + copy_semaphores(24, 11),
        compiler_params=pltpu.CompilerParams(
            collective_id=5, has_side_effects=True, vmem_limit_bytes=VMEM_LIMIT
        ),
    )(
        query, key, value, mask, out, logs, weight, small, place, delta, tokens, first, out_grad,
        up_grad, down_grad, layer
    )


def settle_kernel(
    out_ref, up_ref, down_ref, joined_ref, mask_ref, scores_ref, jitter_ref, scale_ref,
    out_grad, up_grad, down_grad, joined_grad, mask_grad
):
    out_grad[...] = out_ref[...].astype(F32).reshape(out_grad.shape)
    up_grad[...] = up_ref[...].astype(F32).reshape(up_grad.shape)
    down_grad[...] = down_ref[...].astype(F32).reshape(down_grad.shape)
    pairs, halves, cores, rows, _ = joined_ref.shape
    for p in range(pairs):
        for a in range(halves):
            for b in range(cores):
                for t in range(3):
                    at = ((t * cores + b) * pairs + p) * 128
                    piece = joined_ref[p, a, b, :, t * 128 : (t + 1) * 128]
                    joined_grad[a * rows : (a + 1) * rows, at : at + 128] = piece.astype(F32)

    def head(h, carry):
        scale = scale_ref[h]
        soft = jax.nn.sigmoid((scores_ref[h] + jitter_ref[h]) / scale)
        total = mask_ref[h].astype(F32).reshape(soft.shape)
        mask_grad[h] = total * soft * (1.0 - soft) / scale
        return carry

    lax.fori_loop(0, mask_grad.shape[0], head, 0)


def settle(out, up, down, joined, mask, scores, jitter, scale):
    half, width = out.shape[1:]
    like = jax.ShapeDtypeStruct
    return pl.pallas_call(
        settle_kernel,
        name="settle",
        in_specs=[VMEM] * 7 + [SMEM],
        out_specs=[VMEM] * 5,
        out_shape=[
            like((2 * half, width), F32),
            like((2 * half, up.shape[2]), F32),
            like((8 * half, width), F32),
            like((2 * half, 3 * width), F32),
            like(scores.shape, F32),
        ],
        compiler_params=pltpu.CompilerParams(vmem_limit_bytes=VMEM_LIMIT),
    )(out, up, down, joined, mask, scores, jitter, scale)


def gather_rows(array, axis=0):
    return lax.all_gather(array, "fsdp", axis=axis, tiled=True)


def per_device(
    layer_entry_matrix,
    loss_sensitivity,
    ancestor_block_table,
    gate_trained_scores,
    gate_random_jitter,
    softening_scale,
    triple_projection_matrix,
    asker_constant_vector,
    content_constant_vector,
    mixer_exit_matrix,
    mixer_exit_constant,
    mixer_scaling_factor,
    mixer_recentering_term,
    dense_expand_matrix,
    dense_expand_constant,
    dense_contract_matrix,
    dense_contract_constant,
    dense_scaling_factor,
    dense_recentering_term,
):
    micro, _, own_rows, width = layer_entry_matrix.shape
    leaf_count = lax.axis_size("leaf")
    blocks = ancestor_block_table.shape[2]
    rows = own_rows * leaf_count
    block = rows // blocks
    heads, _, span = gate_trained_scores.shape
    leaf = lax.axis_index("leaf")
    tree = leaf // CORES
    core = leaf % CORES
    my_heads = heads // CORES
    my_width = width // CORES
    half = rows // CORES
    pairs = [[CORES * i + c for c in range(CORES)] for i in range(leaf_count // CORES)]
    score_scale = 1.0 / math.sqrt(width // heads)

    orders = [tree_order(ancestor_block_table[m, 0]) for m in range(micro)]
    order = jnp.where(tree == 0, orders[0][0], orders[1][0])

    def own_tree(tokens):
        whole = lax.all_gather(tokens[:, 0], "leaf", axis=1, tiled=True)
        mine = lax.dynamic_index_in_dim(whole, tree, 0, keepdims=False)
        return reorder(mine.reshape(blocks, block, width), order).reshape(rows, width)

    def own_tokens(halves):
        whole = lax.all_gather(halves, "leaf", axis=0, tiled=True)
        whole = whole.reshape(micro, blocks, block, width)
        mine = [reorder(whole[m], orders[m][1]) for m in range(micro)]
        mine = jnp.stack(mine).reshape(micro, 1, rows, width)
        return lax.dynamic_slice_in_dim(mine, leaf * own_rows, own_rows, 2)

    def own_half(array):
        return lax.dynamic_slice_in_dim(array, core * half, half, 0)

    softened = jax.nn.sigmoid(
        (gate_trained_scores + gate_random_jitter) / softening_scale[:, None, None]
    )
    relaxed = lax.dynamic_slice_in_dim(softened.astype(BF), core * my_heads, my_heads, 0)
    mask = gather_rows(relaxed, 1)
    joined_weight = gather_rows(triple_projection_matrix)
    out_weight = gather_rows(mixer_exit_matrix)
    up_weight = gather_rows(dense_expand_matrix)
    down_weight = gather_rows(dense_contract_matrix)
    vectors = [
        asker_constant_vector,
        content_constant_vector,
        mixer_exit_constant,
        mixer_scaling_factor,
        mixer_recentering_term,
        dense_contract_constant,
        dense_scaling_factor,
        dense_recentering_term,
        dense_expand_constant,
    ]
    packed = gather_rows(jnp.concatenate(vectors)[None])
    places = []
    first = 0
    for vector in vectors:
        places.append((first, first + vector.shape[0]))
        first += vector.shape[0]
    (
        query_bias,
        value_bias,
        out_bias,
        first_gain,
        first_shift,
        down_bias,
        second_gain,
        second_shift,
        up_bias,
    ) = [packed[:, a:b].reshape(-1).astype(F32) for a, b in places]

    tokens = own_tree(layer_entry_matrix)
    upstream = own_half(own_tree(loss_sensitivity)).astype(F32)

    def my_columns(matrix, which):
        return lax.dynamic_slice_in_dim(matrix, which * width + core * my_width, my_width, 1)

    def my_part(vector):
        return lax.dynamic_slice_in_dim(vector, core * my_width, my_width, 0)

    weight3 = jnp.concatenate([my_columns(joined_weight, i) for i in range(3)], axis=1)
    joined = dot_nn(tokens, weight3)
    query = (joined[:, :my_width] + my_part(query_bias)).astype(BF) * jnp.asarray(score_scale, BF)
    key = joined[:, my_width : 2 * my_width].astype(BF)
    value = (joined[:, 2 * my_width :] + my_part(value_bias)).astype(BF)

    attended_mine, logs = attend(query, key, value, mask, block)
    attended = own_half(
        lax.all_gather(attended_mine, "leaf", axis=1, tiled=True, axis_index_groups=pairs)
    )

    rows_mine = own_half(tokens).astype(F32)
    hidden, normed_first, inv_first = layer_norm(
        rows_mine + dot_nn(attended, out_weight) + out_bias, first_gain, first_shift
    )
    hidden_low = hidden.astype(BF)
    active, slope = gelu_parts(dot_nn(hidden_low, up_weight) + up_bias)
    active = active.astype(BF)
    output, normed_second, inv_second = layer_norm(
        hidden + dot_nn(active, down_weight) + down_bias, second_gain, second_shift
    )
    layer_out = own_tokens(output.astype(BF))

    delta_second, second_gain_grad, second_shift_grad = norm_backward(
        upstream, normed_second, inv_second, second_gain
    )
    delta_branch = delta_second.astype(BF)
    down_weight_grad = dot_tn(active, delta_branch)
    down_bias_grad = jnp.sum(delta_branch.astype(F32), axis=0)
    delta_up = (dot_nt(delta_branch, down_weight) * slope).astype(BF)
    up_weight_grad = dot_tn(hidden_low, delta_up)
    up_bias_grad = jnp.sum(delta_up.astype(F32), axis=0)
    delta_first, first_gain_grad, first_shift_grad = norm_backward(
        delta_second + dot_nt(delta_up, up_weight), normed_first, inv_first, first_gain
    )
    delta_proj = delta_first.astype(BF)
    out_weight_grad = dot_tn(attended, delta_proj)
    out_bias_grad = jnp.sum(delta_proj.astype(F32), axis=0)
    delta_attended = lax.all_gather(
        dot_nt(delta_proj, out_weight).astype(BF),
        "leaf",
        axis=0,
        tiled=True,
        axis_index_groups=pairs,
    )
    delta_attended = lax.dynamic_slice_in_dim(delta_attended, core * my_width, my_width, 1)

    dquery, dkey, dvalue, dmask = attend_back(
        query, key, value, mask, attended_mine, logs, delta_attended, block, score_scale
    )
    djoined = jnp.concatenate([dquery, dkey, dvalue], axis=1)
    joined_grad = dot_tn(tokens, djoined)
    query_bias_grad = jnp.sum(dquery.astype(F32), axis=0)
    value_bias_grad = jnp.sum(dvalue.astype(F32), axis=0)
    dtokens = lax.psum_scatter(
        dot_nt(djoined, weight3).astype(BF),
        "leaf",
        scatter_dimension=0,
        tiled=True,
        axis_index_groups=pairs,
    )
    tokens_grad = own_tokens((delta_first + dtokens.astype(F32)).astype(BF))

    def placed(part, whole_size, start, axis):
        shape = list(part.shape)
        shape[axis] = whole_size
        return lax.dynamic_update_slice_in_dim(jnp.zeros(shape, part.dtype), part, start, axis)

    def owned(grad, axis=0):
        return lax.psum_scatter(
            grad.astype(BF), "fsdp", scatter_dimension=axis, tiled=True
        )

    joined_part = owned(joined_grad)
    joined_full = jnp.zeros((joined_part.shape[0], 3 * width), BF)
    for i in range(3):
        joined_full = lax.dynamic_update_slice_in_dim(
            joined_full,
            joined_part[:, i * my_width : (i + 1) * my_width],
            i * width + core * my_width,
            1,
        )
    matrices = (
        joined_full,
        owned(out_weight_grad),
        owned(up_weight_grad),
        owned(down_weight_grad),
        placed(owned(dmask, 1), heads, core * my_heads, 0),
    )
    joined_total, out_total, up_total, down_total, mask_total = [
        lax.psum(matrix, "leaf").astype(F32) for matrix in matrices
    ]
    small = (
        placed(query_bias_grad, width, core * my_width, 0),
        placed(value_bias_grad, width, core * my_width, 0),
        out_bias_grad,
        first_gain_grad,
        first_shift_grad,
        up_bias_grad,
        down_bias_grad,
        second_gain_grad,
        second_shift_grad,
    )
    fsdp_count = lax.axis_size("fsdp")
    packed_grads = jnp.concatenate([s.reshape(fsdp_count, -1) for s in small], axis=1)
    packed_grads = lax.psum(
        lax.psum_scatter(packed_grads, "fsdp", scatter_dimension=0, tiled=True), "leaf"
    )[0]
    vector_grads = []
    first = 0
    for s in small:
        size = s.shape[0] // fsdp_count
        vector_grads.append(packed_grads[first : first + size])
        first += size
    mask_gradient = mask_total * softened * (1.0 - softened) / softening_scale[:, None, None]
    return (
        layer_out,
        tokens_grad,
        joined_total,
        vector_grads[0],
        vector_grads[1],
        out_total,
        vector_grads[2],
        vector_grads[3],
        vector_grads[4],
        up_total,
        vector_grads[5],
        down_total,
        vector_grads[6],
        vector_grads[7],
        vector_grads[8],
        mask_gradient,
    )


def fast_device(
    layer_entry_matrix,
    loss_sensitivity,
    ancestor_block_table,
    gate_trained_scores,
    gate_random_jitter,
    softening_scale,
    triple_projection_matrix,
    asker_constant_vector,
    content_constant_vector,
    mixer_exit_matrix,
    mixer_exit_constant,
    mixer_scaling_factor,
    mixer_recentering_term,
    dense_expand_matrix,
    dense_expand_constant,
    dense_contract_matrix,
    dense_contract_constant,
    dense_scaling_factor,
    dense_recentering_term,
):
    micro, _, own_rows, width = layer_entry_matrix.shape
    blocks = ancestor_block_table.shape[2]
    rows = own_rows * 4
    block = rows // blocks
    heads, strip, span = gate_trained_scores.shape
    leaf = lax.axis_index("leaf")
    tree, core = leaf // CORES, leaf % CORES
    mine = width // CORES
    half = rows // CORES
    shard = width // 8
    hidden_shard = dense_contract_matrix.shape[0]
    score_scale = 1.0 / math.sqrt(width // heads)

    table = lax.dynamic_index_in_dim(ancestor_block_table[:, 0], tree, 0, keepdims=False)
    order, place = tree_order(table)
    vectors = [
        asker_constant_vector,
        content_constant_vector,
        mixer_exit_constant,
        mixer_scaling_factor,
        mixer_recentering_term,
        dense_contract_constant,
        dense_scaling_factor,
        dense_recentering_term,
        dense_expand_constant,
    ]
    sizes = [vector.shape[0] for vector in vectors]
    used = sum(sizes)
    places = [sum(sizes[:i]) for i in range(len(sizes))]
    wide = jnp.pad(jnp.stack(vectors[:8]), ((0, 0), (0, 128 - shard)))
    tall = vectors[8].reshape(-1, 128)
    flat = jnp.pad(jnp.concatenate([wide, tall]), ((0, 8 - tall.shape[0]), (0, 0)))

    (
        tokens,
        joined_weight,
        query,
        key,
        value,
        mask,
        attended_mine,
        logs,
        attended,
        out_weight,
        up_weight,
        down_weight,
        tree_upstream,
        normed_first,
        inv_first,
        active,
        slope,
        gathered,
        _,
    ) = front(
        order,
        layer_entry_matrix.reshape(micro, own_rows // block, block, width),
        loss_sensitivity.reshape(micro, own_rows // block, block, width),
        triple_projection_matrix.reshape(2, shard // 2, 3 * width),
        gate_trained_scores,
        gate_random_jitter,
        softening_scale,
        mixer_exit_matrix.reshape(2, shard // 2, width),
        dense_expand_matrix.reshape(2, shard // 2, -1),
        dense_contract_matrix.reshape(4, 2, hidden_shard // 8, width),
        flat,
    )
    first_gain, first_shift, down_bias, second_gain, second_shift = [
        gathered[i : i + 1] for i in range(3, 8)
    ]
    inv_first = inv_first[:, :1]
    joined_weight = joined_weight.reshape(width, 3 * mine)
    mask = mask.reshape(heads // CORES, span, span)
    out_weight = out_weight.reshape(width, width)
    up_weight = up_weight.reshape(width, -1)
    down_weight = down_weight.reshape(-1, width)
    half_order = lax.dynamic_slice_in_dim(order, core * (blocks // 2), blocks // 2, 0)
    upstream = pick(half_order, tree_upstream, tree_upstream).reshape(half, width).astype(F32)
    tokens = tokens.reshape(rows, width)
    hidden = normed_first * first_gain + first_shift
    hidden_low = hidden.astype(BF)
    output, normed_second, inv_second = layer_norm(
        hidden + dot_nn(active, down_weight) + down_bias, second_gain, second_shift
    )
    to_core = [(i, i ^ 1) for i in range(4)]
    low_output = output.astype(BF).reshape(blocks // 2, block, width)
    twin_output = lax.ppermute(low_output, "leaf", to_core)
    swap = core * (blocks // 2)
    own_blocks = blocks // 4
    here = lax.dynamic_slice_in_dim(place, leaf * own_blocks, own_blocks, 0)
    there = lax.dynamic_slice_in_dim(place, (leaf ^ 2) * own_blocks, own_blocks, 0)
    wanted = jnp.concatenate([here, there])
    wanted = (wanted + swap) % blocks
    picked = pick(wanted, low_output, twin_output)
    delta_second, second_gain_grad, second_shift_grad = norm_backward(
        upstream, normed_second, inv_second, second_gain
    )
    delta_branch = delta_second.astype(BF)
    down_weight_grad = dot_tn(active, delta_branch).astype(BF)
    down_bias_grad = jnp.sum(delta_branch.astype(F32), axis=0)
    delta_branch, picked = lax.optimization_barrier((delta_branch, picked))
    delta_up = (dot_nt(delta_branch, down_weight) * slope.astype(F32)).astype(BF)
    up_weight_grad = dot_tn(hidden_low, delta_up).astype(BF)
    up_bias_grad = jnp.sum(delta_up.astype(F32), axis=0)
    delta_first, first_gain_grad, first_shift_grad = norm_backward(
        delta_second + dot_nt(delta_up, up_weight), normed_first, inv_first, first_gain
    )
    delta_proj = delta_first.astype(BF)
    out_weight_grad = dot_tn(attended, delta_proj).astype(BF)
    out_bias_grad = jnp.sum(delta_proj.astype(F32), axis=0)
    delta_attended = dot_nt(delta_proj, out_weight).astype(BF)

    blank = jnp.zeros((1, width), F32)
    small = jnp.concatenate(
        [
            blank,
            blank,
            out_bias_grad[None],
            first_gain_grad[None],
            first_shift_grad[None],
            down_bias_grad[None],
            second_gain_grad[None],
            second_shift_grad[None],
            up_bias_grad.reshape(-1, width),
            jnp.zeros((4, width), F32),
        ]
    )
    out_total, up_total, down_total, mask_total, joined_total, tokens_grad, small, layer_out = rear(
        query,
        key,
        value,
        mask,
        attended_mine,
        logs,
        joined_weight,
        small,
        place,
        delta_attended,
        tokens.reshape(blocks, block, width),
        delta_first.reshape(blocks // 2, block, width),
        out_weight_grad.reshape(LINE, 2, 2, shard // 2, width),
        up_weight_grad.reshape(LINE, 2, 2, shard // 2, -1),
        down_weight_grad.reshape(LINE, 2, 4, 2, hidden_shard // 8, width),
        picked,
        block,
        score_scale,
    )
    spot = lax.axis_index("fsdp")
    narrow = lax.dynamic_slice_in_dim(small[:8], spot * shard, shard, 1)
    vector_grads = [narrow[i] for i in range(8)]
    vector_grads.append(
        lax.dynamic_slice_in_dim(small[8:12].reshape(-1), spot * hidden_shard, hidden_shard, 0)
    )
    out_total, up_total, down_total, joined_total, mask_gradient = settle(
        out_total,
        up_total,
        down_total,
        joined_total,
        mask_total.reshape(heads, 2, strip // 2, span),
        gate_trained_scores,
        gate_random_jitter,
        softening_scale,
    )
    return (
        layer_out.reshape(micro, 1, own_rows, width),
        tokens_grad[:, None],
        joined_total,
        vector_grads[0],
        vector_grads[1],
        out_total,
        vector_grads[2],
        vector_grads[3],
        vector_grads[4],
        up_total,
        vector_grads[8],
        down_total,
        vector_grads[5],
        vector_grads[6],
        vector_grads[7],
        mask_gradient,
    )


def solution(mesh):
    placed = (
        P(None, "fsdp", "leaf", None),
        P(None, "fsdp", "leaf", None),
        P(None, "fsdp", None),
        P(None, "fsdp", None),
        P(None, "fsdp", None),
        P(),
        P("fsdp", None),
        P("fsdp"),
        P("fsdp"),
        P("fsdp", None),
        P("fsdp"),
        P("fsdp"),
        P("fsdp"),
        P("fsdp", None),
        P("fsdp"),
        P("fsdp", None),
        P("fsdp"),
        P("fsdp"),
        P("fsdp"),
    )
    return jax.shard_map(
        fast_device if mesh.shape["fsdp"] == 8 and mesh.shape["leaf"] == 4 else per_device,
        mesh=mesh,
        in_specs=placed,
        out_specs=(
            P(None, "fsdp", "leaf", None),
            P(None, "fsdp", "leaf", None),
            P("fsdp", None),
            P("fsdp"),
            P("fsdp"),
            P("fsdp", None),
            P("fsdp"),
            P("fsdp"),
            P("fsdp"),
            P("fsdp", None),
            P("fsdp"),
            P("fsdp", None),
            P("fsdp"),
            P("fsdp"),
            P("fsdp"),
            P(None, "fsdp", None),
        ),
        check_vma=False,
    )
```
